32 devices in a mesh: batch: 16 (over z, x, core), seq: 2 (over y).
Axes of the slice: x: 2, y: 2, z: 4, core: 2. Of those that a mesh axis runs over, the one named last changes fastest.
Arguments:
- clips_in: bfloat16 [32, 16, 14, 14, 512], P('batch', 'seq'), may hold values from -28 to 28
- cotangent: bfloat16 [32, 16, 14, 14, 512], P('batch', 'seq'), may hold values from -6 to 6
- offset_index: int32 [392, 392], replicated, may hold values from 0 to 2534, as said below
- first_gain: bfloat16 [2, 512], P(None, ('batch', 'seq')), may hold values from 0.5 to 1.5
- first_shift: bfloat16 [2, 512], P(None, ('batch', 'seq')), may hold values from -1 to 1
- inner_weight: bfloat16 [2, 512, 1536], P(None, ('batch', 'seq')), may hold values from -0.25 to 0.25
- inner_bias: bfloat16 [2, 1024], P(None, ('batch', 'seq')), may hold values from -0.5 to 0.5
- outer_weight: bfloat16 [2, 512, 512], P(None, ('batch', 'seq')), may hold values from -3 to 3
- outer_bias: bfloat16 [2, 512], P(None, ('batch', 'seq')), may hold values from -1 to 1
- second_gain: bfloat16 [2, 512], P(None, ('batch', 'seq')), may hold values from 0.5 to 1.5
- second_shift: bfloat16 [2, 512], P(None, ('batch', 'seq')), may hold values from -1 to 1
- up_weight: bfloat16 [2, 512, 2048], P(None, ('batch', 'seq')), may hold values from -0.25 to 0.25
- up_bias: bfloat16 [2, 2048], P(None, ('batch', 'seq')), may hold values from -1 to 1
- down_weight: bfloat16 [2, 2048, 512], P(None, ('batch', 'seq')), may hold values from -0.125 to 0.125
- down_bias: bfloat16 [2, 512], P(None, ('batch', 'seq')), may hold values from -1 to 1
- bias_table: float32 [2, 2535, 16], replicated, may hold values from -3 to 3
Outputs:
- clips_out: bfloat16 [32, 16, 14, 14, 512], P('batch', 'seq')
- clips_grad: bfloat16 [32, 16, 14, 14, 512], P('batch', 'seq')
- grad_first_gain: float32 [2, 512], P(None, ('batch', 'seq'))
- grad_first_shift: float32 [2, 512], P(None, ('batch', 'seq'))
- grad_inner_weight: float32 [2, 512, 1536], P(None, ('batch', 'seq'))
- grad_inner_bias: float32 [2, 1024], P(None, ('batch', 'seq'))
- grad_outer_weight: float32 [2, 512, 512], P(None, ('batch', 'seq'))
- grad_outer_bias: float32 [2, 512], P(None, ('batch', 'seq'))
- grad_second_gain: float32 [2, 512], P(None, ('batch', 'seq'))
- grad_second_shift: float32 [2, 512], P(None, ('batch', 'seq'))
- grad_up_weight: float32 [2, 512, 2048], P(None, ('batch', 'seq'))
- grad_up_bias: float32 [2, 2048], P(None, ('batch', 'seq'))
- grad_down_weight: float32 [2, 2048, 512], P(None, ('batch', 'seq'))
- grad_down_bias: float32 [2, 512], P(None, ('batch', 'seq'))
- grad_bias_table: float32 [2, 2535, 16], replicated
The draws below stay inside these ranges and needn't reach their ends.
Inputs may be any that keep to these rules, and one draw needn't show every extreme that they name: `offset_index`: entry (i, j) is the bias table row of the offset between window positions i and j; two pairs share a row exactly when their offsets are equal.
All inputs are finite; a program needn't handle non-finite values.
Results may differ from the reference program's by a relative error of at most 0.015.
Values may be sent and summed in bfloat16 or wider, within the bound.
A program may use at most 896 MiB of HBM per device.

```python
import math
import jax
import jax.numpy as jnp
from jax import lax

D = 512
HEADS = 16
HD = 32
FF = 2048
WT = 8
WH = 7
WW = 7
FRAMES = 16
HGT = 14
WID = 14
LAYERS = 2
CLIPS = 32
SHIFT_T = 4
SHIFT_S = 3
WIN = 392
WINDOWS = 8
BIAS_ROWS = 2535


def draw_offset_index(key, part):
    relabel = jax.random.permutation(key, BIAS_ROWS).astype(jnp.int32)
    places = jnp.arange(WIN, dtype=jnp.int32)
    frame_of = places // (WH * WW)
    row_of = places // WW % WH
    col_of = places % WW
    frame_diff = frame_of[:, None] - frame_of[None, :] + WT - 1
    row_diff = row_of[:, None] - row_of[None, :] + WH - 1
    col_diff = col_of[:, None] - col_of[None, :] + WW - 1
    canonical = (frame_diff * (2 * WH - 1) + row_diff) * (2 * WW - 1) + col_diff
    return jnp.take(relabel, canonical, axis=0).astype(jnp.int32)


def draw_clips_in(key, part):
    first_key, second_key, third_key = jax.random.split(key, 3)
    full_shape = (CLIPS, FRAMES, HGT, WID, D)
    row_shape = (CLIPS, FRAMES, HGT, WID, 1)
    noise = jnp.clip(jax.random.normal(first_key, full_shape, jnp.float32), -5.0, 5.0)
    row_scale = jnp.exp(jax.random.uniform(second_key, row_shape, jnp.float32, 0.0, math.log(10.0)))
    col_scale = jnp.exp(jax.random.uniform(third_key, (D,), jnp.float32, 0.0, math.log(10.0)))
    return (noise * row_scale * col_scale / 21.5).astype(jnp.bfloat16)


def level_of(rng, dims, shards, smallest, top_value):
    def one(position, blocks):
        steps = jax.random.uniform(jax.random.fold_in(jax.random.fold_in(rng, 6), position), (blocks,), jnp.float32, smallest / len(shards), top_value / len(shards))
        return jnp.repeat(jnp.exp(steps), dims[position] // blocks).reshape((-1,) + (1,) * (len(dims) - position - 1))

    level = one(*shards[0])
    for cut in shards[1:]:
        level = level * one(*cut)
    return level


def normal_values(own_key, shape, scale, bound, cuts=(), kind=jnp.bfloat16):
    values = jax.random.normal(own_key, shape, jnp.float32) * scale
    if len(cuts) > 0:
        values = level_of(own_key, shape, cuts, -0.22, 0.18) * values
    return jnp.clip(values, min=-bound, max=bound).astype(kind)


def setup_inputs(seed: int = 0) -> dict:
    splits = jax.random.split(jax.random.key(seed), 17)
    return {
        "clips_in": draw_clips_in(jax.random.fold_in(splits[16], 71), 0),
        "cotangent": normal_values(splits[1], (CLIPS, FRAMES, HGT, WID, D), 1.0, 6.0, ((0, 16), (1, 2))),
        "offset_index": draw_offset_index(jax.random.fold_in(splits[16], 71), 0),
        "first_gain": jnp.clip(1.0 + 0.1 * jax.random.normal(splits[3], (LAYERS, D), jnp.float32), 0.5, 1.5).astype(jnp.bfloat16),
        "first_shift": normal_values(splits[4], (LAYERS, D), 0.2, 1.0, ((1, 32),)),
        "inner_weight": normal_values(splits[5], (LAYERS, D, 3 * D), D ** -0.5, 0.25, ((1, 32),)),
        "inner_bias": normal_values(splits[6], (LAYERS, 2 * D), 0.1, 0.5, ((1, 32),)),
        "outer_weight": normal_values(splits[7], (LAYERS, D, D), (D // 128) ** -0.5, 3.0, ((1, 32),)),
        "outer_bias": normal_values(splits[8], (LAYERS, D), 0.2, 1.0, ((1, 32),)),
        "second_gain": jnp.clip(1.0 + 0.1 * jax.random.normal(splits[9], (LAYERS, D), jnp.float32), 0.5, 1.5).astype(jnp.bfloat16),
        "second_shift": normal_values(splits[10], (LAYERS, D), 0.2, 1.0, ((1, 32),)),
        "up_weight": normal_values(splits[11], (LAYERS, D, FF), D ** -0.5, 0.25, ((1, 32),)),
        "up_bias": normal_values(splits[12], (LAYERS, FF), 0.2, 1.0, ((1, 32),)),
        "down_weight": normal_values(splits[13], (LAYERS, FF, D), FF ** -0.5, 0.125, ((1, 32),)),
        "down_bias": normal_values(splits[14], (LAYERS, D), 0.2, 1.0, ((1, 32),)),
        "bias_table": normal_values(splits[15], (LAYERS, BIAS_ROWS, HEADS), 0.5, 3.0, (), jnp.float32),
    }


@jax.custom_vjp
def low(v):
    return lax.optimization_barrier(v.astype(jnp.bfloat16)).astype(jnp.float32)

@jax.custom_vjp
def low_back(v):
    return v

def low_keep(v):
    return (low(v), None)

def low_pass(kept, grad):
    return (grad,)

def back_keep(v):
    return (v, None)

def back_low(kept, grad):
    return (low(grad),)
low.defvjp(low_keep, low_pass)
low_back.defvjp(back_keep, back_low)
EPSILON = 1e-05
MASKED = -100.0
HIGHEST = lax.Precision.HIGHEST

def norm_rows(values, gain, shift):
    average = lax.optimization_barrier(jnp.mean(values, axis=-1, keepdims=True))
    centred = values - average
    spread = lax.optimization_barrier(jnp.mean(centred * centred, axis=-1, keepdims=True))
    return centred * lax.rsqrt(spread + EPSILON) * gain + shift

def product(left, right):
    return jnp.dot(left, right, precision=HIGHEST, preferred_element_type=jnp.float32)

def region_of(places, extent, window, offset):
    return (places >= extent - window).astype(jnp.int32) + (places >= extent - offset).astype(jnp.int32)

def region_grid():
    time_region = region_of(jnp.arange(FRAMES, dtype=jnp.int32), FRAMES, WT, SHIFT_T)
    row_region = region_of(jnp.arange(HGT, dtype=jnp.int32), HGT, WH, SHIFT_S)
    col_region = region_of(jnp.arange(WID, dtype=jnp.int32), WID, WW, SHIFT_S)
    return (time_region[:, None, None] * 3 + row_region[None, :, None]) * 3 + col_region[None, None, :]

def split_windows(field):
    width = field.shape[-1]
    shaped = field.reshape(FRAMES // WT, WT, HGT // WH, WH, WID // WW, WW, width)
    shaped = shaped.transpose(0, 2, 4, 1, 3, 5, 6)
    return shaped.reshape(WINDOWS, WIN, width)

def merge_windows(windows):
    width = windows.shape[-1]
    shaped = windows.reshape(FRAMES // WT, HGT // WH, WID // WW, WT, WH, WW, width)
    shaped = shaped.transpose(0, 3, 1, 4, 2, 5, 6)
    return shaped.reshape(FRAMES, HGT, WID, width)

def attention(query, keys, values, bias_heads, extra):
    head_shape = (WINDOWS, WIN, HEADS, HD)
    scores = jnp.einsum('wqhd,wkhd->whqk', query.reshape(head_shape), keys.reshape(head_shape), precision=HIGHEST, preferred_element_type=jnp.float32)
    total = low_back(scores) + bias_heads[None] + extra[:, None]
    soft = jax.nn.softmax(total, axis=-1)
    output = jnp.einsum('whqk,wkhd->wqhd', low(soft), values.reshape(head_shape), precision=HIGHEST, preferred_element_type=jnp.float32)
    return output.reshape(WINDOWS, WIN, D)

def block(field, weights, table, offset_index, extra, shifted):
    gain_one, shift_one, in_matrix, in_offset, out_matrix, out_offset, gain_two, shift_two, up_matrix, up_offset, down_matrix, down_offset = weights
    scale = HD ** (-0.5)
    normed = low(norm_rows(field, gain_one, shift_one))
    mixed = product(normed, in_matrix)
    query = low(low_back((mixed[..., :D] + in_offset[:D]) * scale))
    keys = low(low_back(mixed[..., D:2 * D]))
    values = low(low_back(mixed[..., 2 * D:] + in_offset[D:]))
    if shifted:
        query = jnp.roll(query, (-SHIFT_T, -SHIFT_S, -SHIFT_S), axis=(0, 1, 2))
        keys = jnp.roll(keys, (-SHIFT_T, -SHIFT_S, -SHIFT_S), axis=(0, 1, 2))
        values = jnp.roll(values, (-SHIFT_T, -SHIFT_S, -SHIFT_S), axis=(0, 1, 2))
    bias_heads = jnp.take(table, offset_index, axis=0).transpose(2, 0, 1)
    attended = merge_windows(attention(split_windows(query), split_windows(keys), split_windows(values), bias_heads, extra))
    if shifted:
        attended = jnp.roll(attended, (SHIFT_T, SHIFT_S, SHIFT_S), axis=(0, 1, 2))
    attended = low(low_back(attended))
    middle = field + low_back(product(attended, out_matrix)) + out_offset
    normed_two = low(norm_rows(middle, gain_two, shift_two))
    hidden = low_back(product(normed_two, up_matrix)) + up_offset
    active = low(jax.nn.gelu(hidden, approximate=False))
    return middle + low_back(product(active, down_matrix)) + down_offset

def reference(clips_in, cotangent, offset_index, first_gain, first_shift, inner_weight, inner_bias, outer_weight, outer_bias, second_gain, second_shift, up_weight, up_bias, down_weight, down_bias, bias_table):
    params = (first_gain.astype(jnp.float32), first_shift.astype(jnp.float32), inner_weight.astype(jnp.float32), inner_bias.astype(jnp.float32), outer_weight.astype(jnp.float32), outer_bias.astype(jnp.float32), second_gain.astype(jnp.float32), second_shift.astype(jnp.float32), up_weight.astype(jnp.float32), up_bias.astype(jnp.float32), down_weight.astype(jnp.float32), down_bias.astype(jnp.float32), bias_table.astype(jnp.float32))
    window_ids = split_windows(region_grid()[..., None])[..., 0]
    region_mask = jnp.where(window_ids[:, :, None] == window_ids[:, None, :], 0.0, MASKED).astype(jnp.float32)
    extras = (jnp.zeros_like(region_mask), region_mask)

    def forward(field, weights_all):
        for layer in range(LAYERS):
            weights = tuple((member[layer] for member in weights_all[:12]))
            field = block(field, weights, weights_all[12][layer], offset_index, extras[layer % 2], layer % 2 == 1)
        return field

    def per_clip(totals, pair):
        field, upstream = pair
        result, pullback = jax.vjp(forward, field.astype(jnp.float32), params)
        field_grad, param_grads = pullback(upstream.astype(jnp.float32))
        totals = jax.tree.map(jnp.add, totals, param_grads)
        return (totals, (result.astype(jnp.bfloat16), field_grad.astype(jnp.bfloat16)))
    start = jax.tree.map(jnp.zeros_like, params)
    totals, (clips_out, clips_grad) = lax.scan(per_clip, start, (clips_in, cotangent))
    return (clips_out, clips_grad, totals[0], totals[1], totals[2], totals[3], totals[4], totals[5], totals[6], totals[7], totals[8], totals[9], totals[10], totals[11], totals[12])
```

```python
import functools

import jax
import jax.numpy as jnp
import numpy as np
from jax import lax
from jax.experimental import pallas as pl
from jax.experimental.pallas import tpu as pltpu
from jax.sharding import PartitionSpec as P

D = 512
HEADS = 16
HD = 32
FF = 2048
WT = 8
WH = 7
WW = 7
FRAMES = 16
HGT = 14
WID = 14
LAYERS = 2
SHIFT_T = 4
SHIFT_S = 3
WIN = 392
BIAS_ROWS = 2535
ROWS = 16
PACKS = D // ROWS
CELLS = (2 * WH - 1) * (2 * WW - 1)

EPSILON = 1e-05
MASKED = -100.0
LOG2E = 1.4426950408889634
LN2 = 0.6931471805599453
SCALE = HD**-0.5

BF16 = jnp.bfloat16
F32 = jnp.float32
AXES = ("batch", "seq")

NT = (((1,), (1,)), ((), ()))
TN = (((0,), (0,)), ((), ()))


def params():
    return pltpu.CompilerParams(
        vmem_limit_bytes=61 * 1024 * 1024, dimension_semantics=("arbitrary",)
    )


def dot(left, right, dims=(((1,), (0,)), ((), ()))):
    return lax.dot_general(left, right, dims, preferred_element_type=F32)


def normalize(values):
    average = jnp.mean(values, axis=-1, keepdims=True)
    centred = values - average
    rate = lax.rsqrt(jnp.mean(centred * centred, axis=-1, keepdims=True) + EPSILON)
    return centred * rate, rate


def row_sum(values):
    return jnp.sum(values, axis=0, keepdims=True)


def split_three(values):
    high = values.astype(BF16)
    rest = values - high.astype(F32)
    middle = rest.astype(BF16)
    low = (rest - middle.astype(F32)).astype(BF16)
    return high, middle, low


def square(ref, first):
    return ref[:, first : first + ROWS, :].reshape(D, D)


def grid_spec(shape):
    row_blocks, col_blocks = shape[1] // WH, shape[2] // WW
    per_clip = row_blocks * col_blocks
    return pl.BlockSpec(
        (1, WH, WW, WT, D),
        lambda i: (i // per_clip, (i % per_clip) // col_blocks, i % col_blocks, 0, 0),
    )


def window_spec(*tail):
    return pl.BlockSpec((1,) + tail, lambda i: (i,) + (0,) * len(tail))


def whole_spec(*shape):
    return pl.BlockSpec(shape, lambda i: (0,) * len(shape), pipeline_mode=pl.Buffered(1))


def pack_spec(rows, index):
    return pl.BlockSpec(
        (PACKS, rows, D), lambda i: (0, index, 0), pipeline_mode=pl.Buffered(1)
    )


def head_lanes(which):
    lane = lax.broadcasted_iota(jnp.int32, (1, 128), 1)
    return (lane // HD) == which


def lane_slice(group, base=0):
    return pl.ds(pl.multiple_of(base + group * 128, 128), 128)


def attention_forward(masked, *refs):
    if masked:
        x_ref, w_ref, vec_ref, bias_ref, augq_ref, augk_ref = refs[:6]
        qkv_ref, soft_ref, rate_ref, att_ref, mid_ref, vt_s, ot_s = refs[6:]
    else:
        x_ref, w_ref, vec_ref, bias_ref = refs[:4]
        qkv_ref, soft_ref, rate_ref, att_ref, mid_ref, vt_s, ot_s = refs[4:]
    x = x_ref[0].astype(F32).reshape(WIN, D)
    normed = (normalize(x)[0] * vec_ref[0:1] + vec_ref[1:2]).astype(BF16)
    query = (dot(normed, square(w_ref, 0)) + vec_ref[2:3]) * (SCALE * LOG2E)
    qkv_ref[0, :, 0:D] = query.astype(BF16)
    qkv_ref[0, :, D : 2 * D] = dot(normed, square(w_ref, ROWS)).astype(BF16)
    values = dot(normed, square(w_ref, 2 * ROWS)) + vec_ref[3:4]
    qkv_ref[0, :, 2 * D :] = values.astype(BF16)
    vt_s[...] = jnp.transpose(values).astype(BF16)

    def group(g, carry):
        query4 = qkv_ref[0, :, lane_slice(g)]
        keys4 = qkv_ref[0, :, lane_slice(g, D)]
        if masked:
            query4 = jnp.concatenate([query4, augq_ref[0]], axis=1)
        for which in range(4):
            head = g * 4 + which
            keys = jnp.where(head_lanes(which), keys4, jnp.zeros_like(keys4))
            if masked:
                keys = jnp.concatenate([keys, augk_ref[0]], axis=1)
            total = dot(keys, query4, NT) + bias_ref[head]
            peak = jnp.max(total, axis=0, keepdims=True)
            soft = jnp.exp2(total - peak).astype(BF16)
            soft_ref[0, head] = soft
            rows = pl.ds(pl.multiple_of(head * HD, HD), HD)
            left = jnp.concatenate([vt_s[rows, :], jnp.ones((16, WIN), BF16)], axis=0)
            joined = dot(left, soft)
            rate = 1.0 / joined[HD : HD + 1]
            rate_ref[0, pl.ds(head, 1), :] = rate
            ot_s[rows, :] = joined[:HD] * rate
        return carry

    lax.fori_loop(0, 4, group, 0)
    attended = jnp.transpose(ot_s[...]).astype(BF16)
    att_ref[0] = attended
    mid_ref[0] = x + dot(attended, square(w_ref, 3 * ROWS)) + vec_ref[4:5]


def run_attention_forward(x, pack, vec, bias, aug):
    windows = x.shape[0] * (x.shape[1] // WH) * (x.shape[2] // WW)
    masked = aug is not None
    extra = list(aug) if masked else []
    return pl.pallas_call(
        functools.partial(attention_forward, masked),
        grid=(windows,),
        in_specs=[
            grid_spec(x.shape),
            pack_spec(64, 0),
            whole_spec(12, D),
            whole_spec(HEADS, WIN, WIN),
        ]
        + [window_spec(WIN, 128)] * len(extra),
        out_specs=[
            window_spec(WIN, 3 * D),
            window_spec(HEADS, WIN, WIN),
            window_spec(HEADS, WIN),
            window_spec(WIN, D),
            window_spec(WIN, D),
        ],
        out_shape=[
            jax.ShapeDtypeStruct((windows, WIN, 3 * D), BF16),
            jax.ShapeDtypeStruct((windows, HEADS, WIN, WIN), BF16),
            jax.ShapeDtypeStruct((windows, HEADS, WIN), F32),
            jax.ShapeDtypeStruct((windows, WIN, D), BF16),
            jax.ShapeDtypeStruct((windows, WIN, D), F32),
        ],
        scratch_shapes=[pltpu.VMEM((D, WIN), BF16), pltpu.VMEM((D, WIN), F32)],
        compiler_params=params(),
    )(x, pack, vec, bias, *extra)


def gelu_parts(hidden):
    cumulative = 0.5 + 0.5 * lax.erf(hidden * (0.5**0.5))
    density = jnp.exp(-0.5 * hidden * hidden) * 0.3989422804014327
    return hidden * cumulative, cumulative + hidden * density


def feed_forward(mid_ref, up_ref, down_ref, vec_ref, act_ref, slope_ref, out_ref):
    middle = mid_ref[0]
    normed = (normalize(middle)[0] * vec_ref[5:6] + vec_ref[6:7]).astype(BF16)
    total = middle + vec_ref[7:8]
    for part in range(4):
        lanes = slice(part * D, (part + 1) * D)
        hidden = dot(normed, square(up_ref, part * ROWS)) + vec_ref[8 + part : 9 + part]
        active, slope = gelu_parts(hidden)
        active = active.astype(BF16)
        act_ref[0, :, lanes] = active
        slope_ref[0, :, lanes] = slope.astype(BF16)
        down = down_ref[part * 8 : part * 8 + 8].reshape(D, D)
        total = total + dot(active, down)
    out_ref[0] = total.reshape(WH, WW, WT, D).astype(out_ref.dtype)


def run_feed_forward(middle, pack, vec, grid_shape, dtype):
    windows = middle.shape[0]
    return pl.pallas_call(
        feed_forward,
        grid=(windows,),
        in_specs=[
            window_spec(WIN, D),
            pack_spec(64, 1),
            pack_spec(64, 2),
            whole_spec(12, D),
        ],
        out_specs=[window_spec(WIN, FF), window_spec(WIN, FF), grid_spec(grid_shape)],
        out_shape=[
            jax.ShapeDtypeStruct((windows, WIN, FF), BF16),
            jax.ShapeDtypeStruct((windows, WIN, FF), BF16),
            jax.ShapeDtypeStruct(grid_shape, dtype),
        ],
        compiler_params=params(),
    )(middle, pack, pack, vec)


def norm_back(normal, rate, gained):
    first = jnp.mean(gained, axis=-1, keepdims=True)
    second = jnp.mean(gained * normal, axis=-1, keepdims=True)
    return (gained - first - normal * second) * rate


def feed_backward(
    grad_ref, act_ref, slope_ref, mid_ref, att_ref, in_ref, up_ref, down_ref, vec_ref,
    gmid_ref, gatt_ref, pack_ref, gvec_ref,
):
    @pl.when(pl.program_id(0) == 0)
    def _():
        pack_ref[...] = jnp.zeros_like(pack_ref)
        gvec_ref[...] = jnp.zeros_like(gvec_ref)

    grad = grad_ref[0].astype(F32).reshape(WIN, D)
    gvec_ref[3:4] += row_sum(grad)
    grad_low = grad.astype(BF16)
    normal, rate = normalize(mid_ref[0])
    normed = (normal * vec_ref[5:6] + vec_ref[6:7]).astype(BF16)
    gnormed = jnp.zeros((WIN, D), F32)
    for part in range(4):
        lanes = slice(part * D, (part + 1) * D)
        active = act_ref[0, :, lanes]
        pack_ref[part * 8 : part * 8 + 8, 80:144, :] += dot(active, grad_low, TN).reshape(8, 64, D)
        down = down_ref[part * 8 : part * 8 + 8].reshape(D, D)
        ghidden = dot(grad_low, down, NT) * slope_ref[0, :, lanes].astype(F32)
        gvec_ref[4 + part : 5 + part] += row_sum(ghidden)
        ghidden = ghidden.astype(BF16)
        first = ROWS * (1 + part)
        pack_ref[:, first : first + ROWS, :] += dot(normed, ghidden, TN).reshape(PACKS, ROWS, D)
        gnormed = gnormed + dot(ghidden, square(up_ref, part * ROWS), NT)
    gvec_ref[1:2] += row_sum(gnormed * normal)
    gvec_ref[2:3] += row_sum(gnormed)
    gmid = grad + norm_back(normal, rate, gnormed * vec_ref[5:6])
    gmid_ref[0] = gmid
    gvec_ref[0:1] += row_sum(gmid)
    gmid_low = gmid.astype(BF16)
    pack_ref[:, 0:ROWS, :] += dot(att_ref[0], gmid_low, TN).reshape(PACKS, ROWS, D)
    gatt_ref[0] = dot(gmid_low, square(in_ref, 3 * ROWS), NT).astype(BF16)


def run_feed_backward(grad, active, slope, middle, attended, pack, vec):
    windows = middle.shape[0]
    return pl.pallas_call(
        feed_backward,
        grid=(windows,),
        in_specs=[
            grid_spec(grad.shape),
            window_spec(WIN, FF),
            window_spec(WIN, FF),
            window_spec(WIN, D),
            window_spec(WIN, D),
            pack_spec(64, 0),
            pack_spec(64, 1),
            pack_spec(64, 2),
            whole_spec(12, D),
        ],
        out_specs=[
            window_spec(WIN, D),
            window_spec(WIN, D),
            pl.BlockSpec((PACKS, 144, D), lambda i: (0, 0, 0)),
            pl.BlockSpec((8, D), lambda i: (0, 0)),
        ],
        out_shape=[
            jax.ShapeDtypeStruct((windows, WIN, D), F32),
            jax.ShapeDtypeStruct((windows, WIN, D), BF16),
            jax.ShapeDtypeStruct((PACKS, 144, D), F32),
            jax.ShapeDtypeStruct((8, D), F32),
        ],
        compiler_params=params(),
    )(grad, active, slope, middle, attended, pack, pack, pack, vec)


def attention_backward(
    x_ref, gatt_ref, att_ref, rate_ref, soft_ref, qkv_ref, gmid_ref, in_ref, vec_ref,
    out_ref, pack_ref, gvec_ref, table_ref,
    sum_s, kt_s, qt_s, do_s, gk_s, gv_s, wide_s,
):
    step = pl.program_id(0)

    @pl.when(step == 0)
    def _():
        sum_s[...] = jnp.zeros_like(sum_s)
        pack_ref[...] = jnp.zeros_like(pack_ref)
        gvec_ref[...] = jnp.zeros_like(gvec_ref)

    lane = lax.broadcasted_iota(jnp.int32, (1, 128), 1)
    head_row = lax.broadcasted_iota(jnp.int32, (3 * HEADS, D), 0) % HEADS
    head_col = lax.broadcasted_iota(jnp.int32, (3 * HEADS, D), 1) // HD
    spread = jnp.where(head_row == head_col, 1.0, 0.0).astype(BF16)
    rates = jnp.concatenate(split_three(rate_ref[0]), axis=0)
    scaled = (gatt_ref[0].astype(F32) * dot(rates, spread, TN)).astype(BF16)
    do_s[...] = scaled
    product = scaled.astype(F32) * att_ref[0].astype(F32)
    gather_row = lax.broadcasted_iota(jnp.int32, (D, 128), 0) // HD
    gather_col = lax.broadcasted_iota(jnp.int32, (D, 128), 1)
    gather = jnp.where(
        (gather_row == gather_col % HEADS) & (gather_col < 3 * HEADS), 1.0, 0.0
    ).astype(BF16)
    high = product.astype(BF16)
    low = (product - high.astype(F32)).astype(BF16)
    inner = dot(high, gather) + dot(low, gather)
    first, second, third = split_three(inner)
    inner = jnp.where(lane < HEADS, first, jnp.where(lane < 2 * HEADS, second, third))
    kt_s[...] = jnp.transpose(qkv_ref[0, :, D : 2 * D].astype(F32)).astype(BF16)

    def group(g, carry):
        query4 = qkv_ref[0, :, lane_slice(g)]
        values4 = qkv_ref[0, :, lane_slice(g, 2 * D)]
        grad4 = do_s[:, lane_slice(g)]
        right = jnp.concatenate([grad4, inner], axis=1)
        zero = jnp.zeros_like(grad4)
        gvalues = jnp.zeros((WIN, 128), F32)
        gkeys = jnp.zeros((WIN, 128), F32)
        for which in range(4):
            head = g * 4 + which
            mine = head_lanes(which)
            minus = jnp.where((lane % HEADS == head) & (lane < 3 * HEADS), -1.0, 0.0)
            minus = jnp.broadcast_to(minus, (WIN, 128)).astype(BF16)
            left = jnp.concatenate([jnp.where(mine, values4, zero), minus], axis=1)
            soft = soft_ref[0, head]
            gtotal = soft.astype(F32) * dot(left, right, NT)
            sum_s[head] += gtotal
            gtotal = gtotal.astype(BF16)
            gvalues = gvalues + dot(soft, jnp.where(mine, grad4, zero))
            gkeys = gkeys + dot(gtotal, jnp.where(mine, query4, zero))
            rows = pl.ds(pl.multiple_of(head * HD, HD), HD)
            qt_s[rows, :] = dot(kt_s[rows, :], gtotal)
        gv_s[:, lane_slice(g)] = gvalues.astype(BF16)
        gk_s[:, lane_slice(g)] = (gkeys * LN2).astype(BF16)
        return carry

    lax.fori_loop(0, 4, group, 0)
    gquery = jnp.transpose(qt_s[...]).astype(BF16)
    gkeys = gk_s[...]
    gvalues = gv_s[...]
    normal, rate = normalize(x_ref[0].astype(F32).reshape(WIN, D))
    normed = (normal * vec_ref[0:1] + vec_ref[1:2]).astype(BF16)
    pack_ref[:, 0:ROWS, :] += (dot(normed, gquery, TN) * SCALE).reshape(PACKS, ROWS, D)
    pack_ref[:, ROWS : 2 * ROWS, :] += dot(normed, gkeys, TN).reshape(PACKS, ROWS, D)
    pack_ref[:, 2 * ROWS :, :] += dot(normed, gvalues, TN).reshape(PACKS, ROWS, D)
    gvec_ref[2:3] += row_sum(gquery.astype(F32)) * SCALE
    gvec_ref[3:4] += row_sum(gvalues.astype(F32))
    gnormed = (
        dot(gquery, square(in_ref, 0), NT) * SCALE
        + dot(gkeys, square(in_ref, ROWS), NT)
        + dot(gvalues, square(in_ref, 2 * ROWS), NT)
    )
    gvec_ref[0:1] += row_sum(gnormed * normal)
    gvec_ref[1:2] += row_sum(gnormed)
    grad = gmid_ref[0] + norm_back(normal, rate, gnormed * vec_ref[0:1])
    out_ref[0] = grad.reshape(WH, WW, WT, D).astype(out_ref.dtype)

    @pl.when(step == pl.num_programs(0) - 1)
    def _():
        table_ref[...] = jnp.zeros_like(table_ref)
        for col in range(WW):
            wide_s[...] = jnp.zeros_like(wide_s)
            for row in range(WH):
                place = (row * WW + col) * WT
                low_lane = (WH - 1 - row) * WW * WT
                wide_s[:, low_lane : low_lane + WIN] += sum_s[:, place : place + WT, :].reshape(
                    HEADS * WT, WIN
                )
            for shift in range(2 * WH - 1):
                low_lane = (shift * (2 * WW - 1) + WW - 1 - col) * WT
                table_ref[:, low_lane : low_lane + WW * WT] += wide_s[
                    :, shift * WW * WT : (shift + 1) * WW * WT
                ]


def run_attention_backward(x, gattended, attended, rates, soft, qkv, gmiddle, pack, vec, dtype):
    windows = gmiddle.shape[0]
    return pl.pallas_call(
        attention_backward,
        grid=(windows,),
        in_specs=[
            grid_spec(x.shape),
            window_spec(WIN, D),
            window_spec(WIN, D),
            window_spec(HEADS, WIN),
            window_spec(HEADS, WIN, WIN),
            window_spec(WIN, 3 * D),
            window_spec(WIN, D),
            pack_spec(64, 0),
            whole_spec(12, D),
        ],
        out_specs=[
            grid_spec(x.shape),
            pl.BlockSpec((PACKS, 48, D), lambda i: (0, 0, 0)),
            pl.BlockSpec((4, D), lambda i: (0, 0)),
            pl.BlockSpec((HEADS * WT, CELLS * WT), lambda i: (0, 0)),
        ],
        out_shape=[
            jax.ShapeDtypeStruct(x.shape, dtype),
            jax.ShapeDtypeStruct((PACKS, 48, D), F32),
            jax.ShapeDtypeStruct((4, D), F32),
            jax.ShapeDtypeStruct((HEADS * WT, CELLS * WT), F32),
        ],
        scratch_shapes=[
            pltpu.VMEM((HEADS, WIN, WIN), F32),
            pltpu.VMEM((D, WIN), BF16),
            pltpu.VMEM((D, WIN), F32),
            pltpu.VMEM((WIN, D), BF16),
            pltpu.VMEM((WIN, D), BF16),
            pltpu.VMEM((WIN, D), BF16),
            pltpu.VMEM((HEADS * WT, (2 * WH - 1) * WW * WT), F32),
        ],
        compiler_params=params(),
    )(x, gattended, attended, rates, soft, qkv, gmiddle, pack, vec)


def expand_bias(cells_ref, out_ref, wide_s):
    for col in range(WW):
        for shift in range(2 * WH - 1):
            low_lane = (shift * (2 * WW - 1) + WW - 1 - col) * WT
            wide_s[:, shift * WW * WT : (shift + 1) * WW * WT] = cells_ref[
                0, :, low_lane : low_lane + WW * WT
            ]
        for row in range(WH):
            place = (row * WW + col) * WT
            low_lane = (WH - 1 - row) * WW * WT
            out_ref[0, :, place : place + WT, :] = wide_s[:, low_lane : low_lane + WIN].reshape(
                HEADS, WT, WIN
            )


def run_expand_bias(cells):
    return pl.pallas_call(
        expand_bias,
        grid=(LAYERS,),
        in_specs=[pl.BlockSpec((1, HEADS * WT, CELLS * WT), lambda i: (i, 0, 0))],
        out_specs=pl.BlockSpec((1, HEADS, WIN, WIN), lambda i: (i, 0, 0, 0)),
        out_shape=jax.ShapeDtypeStruct((LAYERS, HEADS, WIN, WIN), F32),
        scratch_shapes=[pltpu.VMEM((HEADS * WT, (2 * WH - 1) * WW * WT), F32)],
        compiler_params=params(),
    )(cells)


def offset_places():
    frame, row, col = np.meshgrid(
        np.arange(1 - WT, WT), np.arange(1 - WH, WH), np.arange(1 - WW, WW), indexing="ij"
    )

    def place(f, r, c):
        return (np.maximum(f, 0) * WH + np.maximum(r, 0)) * WW + np.maximum(c, 0)

    return (place(frame, row, col) * WIN + place(-frame, -row, -col)).reshape(-1)


def select_rows(tables, chosen, dims):
    flat = tables.transpose(1, 0, 2).reshape(BIAS_ROWS, LAYERS * HEADS)
    pieces = dot(chosen, jnp.concatenate(split_three(flat), axis=1), dims)
    width = LAYERS * HEADS
    total = pieces[:, :width] + pieces[:, width : 2 * width] + pieces[:, 2 * width :]
    return total.reshape(BIAS_ROWS, LAYERS, HEADS).transpose(1, 0, 2)


def bias_cells(tables, chosen):
    taken = select_rows(tables, chosen, (((1,), (0,)), ((), ())))
    taken = taken.transpose(1, 0, 2).reshape(BIAS_ROWS, LAYERS * HEADS)
    taken = (taken * LOG2E).reshape(2 * WT - 1, CELLS, LAYERS * HEADS).transpose(2, 1, 0)
    placed = jnp.stack([taken[:, :, WT - 1 - t : 2 * WT - 1 - t] for t in range(WT)], axis=1)
    return placed.reshape(LAYERS, HEADS * WT, CELLS * WT)


def cells_to_rows(cells):
    shaped = cells.reshape(LAYERS, HEADS, WT, CELLS, WT)
    parts = [
        jnp.pad(shaped[:, :, t], ((0, 0), (0, 0), (0, 0), (WT - 1 - t, t))) for t in range(WT)
    ]
    total = functools.reduce(jnp.add, parts)
    return total.transpose(0, 3, 2, 1).reshape(LAYERS, BIAS_ROWS, HEADS)


def spatial_blocks(field):
    clip_count, frames_here, width = (field.shape[0], field.shape[1], field.shape[-1])
    shaped = field.reshape(clip_count, frames_here, HGT // WH, WH, WID // WW, WW, width)
    shaped = shaped.transpose(0, 2, 4, 1, 3, 5, 6)
    return shaped.reshape(clip_count * (HGT // WH) * (WID // WW), frames_here, WH * WW, width)


def roll_space(field, amount, first):
    return jnp.roll(field, (amount, amount), axis=(first, first + 1))


def swap_halves(part):
    return lax.ppermute(part, "seq", [(0, 1), (1, 0)])


class Placement:
    def __init__(self, clip_count, frames_here):
        self.clips = clip_count
        self.frames = frames_here
        self.parts = lax.axis_size("seq")
        self.near = self.parts == 2 and frames_here == WT

    def grid_shape(self):
        if self.near:
            return (self.clips, HGT, WID, WT, D)
        columns = self.clips * 4 // self.parts
        return (columns * 2, WH, WW, WT, D)

    def enter(self, field, shifted):
        if self.near:
            if shifted:
                arrived = swap_halves(field[:, :SHIFT_T])
                field = jnp.concatenate([field[:, SHIFT_T:], arrived], axis=1)
                field = roll_space(field, -SHIFT_S, 2)
            return field.transpose(0, 2, 3, 1, 4)
        if shifted:
            field = roll_space(field, -SHIFT_S, 2)
        columns = lax.all_to_all(
            spatial_blocks(field), "seq", split_axis=0, concat_axis=1, tiled=True
        )
        if shifted:
            columns = jnp.roll(columns, -SHIFT_T, axis=1)
        windows = columns.reshape(-1, WT, WH, WW, D)
        return windows.transpose(0, 2, 3, 1, 4)

    def leave(self, grid, shifted):
        if self.near:
            field = grid.transpose(0, 3, 1, 2, 4)
            if shifted:
                field = roll_space(field, SHIFT_S, 2)
                arrived = swap_halves(field[:, SHIFT_T:])
                field = jnp.concatenate([arrived, field[:, :SHIFT_T]], axis=1)
            return field
        columns = grid.transpose(0, 3, 1, 2, 4).reshape(-1, FRAMES, WH * WW, D)
        if shifted:
            columns = jnp.roll(columns, SHIFT_T, axis=1)
        columns = lax.all_to_all(columns, "seq", split_axis=1, concat_axis=0, tiled=True)
        shaped = columns.reshape(self.clips, HGT // WH, WID // WW, self.frames, WH, WW, D)
        shaped = shaped.transpose(0, 3, 1, 4, 2, 5, 6)
        field = shaped.reshape(self.clips, self.frames, HGT, WID, D)
        return roll_space(field, SHIFT_S, 2) if shifted else field

    def forth(self, grid):
        if self.near:
            arrived = swap_halves(grid[..., :SHIFT_T, :])
            grid = jnp.concatenate([grid[..., SHIFT_T:, :], arrived], axis=3)
            return roll_space(grid, -SHIFT_S, 1)
        return self.enter(self.leave(grid, False), True)

    def back(self, grid):
        if self.near:
            grid = roll_space(grid, SHIFT_S, 1)
            arrived = swap_halves(grid[..., SHIFT_T:, :])
            return jnp.concatenate([arrived, grid[..., :SHIFT_T, :]], axis=3)
        return self.enter(self.leave(grid, True), False)

    def mask_lanes(self):
        if self.near:
            index = jnp.arange(self.clips * 4, dtype=jnp.int32)
            late = jnp.full(index.shape, lax.axis_index("seq"), jnp.int32)
            block = index % 4
        else:
            columns = self.clips * 4 // self.parts
            index = jnp.arange(columns * 2, dtype=jnp.int32)
            late = index % 2
            block = (lax.axis_index("seq") * columns + index // 2) % 4
        place = np.arange(WIN)
        frame_late = jnp.asarray(place % WT >= WT - SHIFT_T).astype(jnp.int32)
        row_late = jnp.asarray(place // (WT * WW) >= WH - SHIFT_S).astype(jnp.int32)
        col_late = jnp.asarray(place // WT % WW >= WW - SHIFT_S).astype(jnp.int32)
        region = (
            late[:, None] * frame_late * 4
            + (block // 2)[:, None] * row_late * 2
            + (block % 2)[:, None] * col_late
        )
        lane = np.arange(128)
        same = (region[:, :, None] == lane % 8) & (lane < 24)
        pieces = []
        rest = np.float32(MASKED * LOG2E)
        for _ in range(3):
            piece = np.float32(np.asarray(rest).astype(BF16))
            pieces.append(piece)
            rest = np.float32(rest - piece)
        piece_of = np.zeros((128,), np.float32)
        for number, piece in enumerate(pieces):
            piece_of[8 * number : 8 * number + 8] = -piece
            piece_of[24 + number] = piece
        always = (lane >= 24) & (lane < 27)
        on_keys = jnp.where(same | always, 1.0, 0.0)
        return (on_keys * piece_of).astype(BF16), on_keys.astype(BF16)


def pack_layer(inner, outer, up, down):
    parts = [inner[:, i * D : (i + 1) * D] for i in range(3)] + [outer]
    parts = parts + [up[:, i * D : (i + 1) * D] for i in range(4)] + [down]
    return jnp.concatenate(parts, axis=0)


def per_device(
    clips_in,
    cotangent,
    offset_index,
    first_gain,
    first_shift,
    inner_weight,
    inner_bias,
    outer_weight,
    outer_bias,
    second_gain,
    second_shift,
    up_weight,
    up_bias,
    down_weight,
    down_bias,
    bias_table,
):
    place = Placement(clips_in.shape[0], clips_in.shape[1])
    rows = inner_weight.shape[1]
    devices = D // rows
    vectors = [
        first_gain, first_shift, inner_bias, outer_bias, second_gain, second_shift,
        down_bias, up_bias,
    ]
    vec_pack = jnp.concatenate(vectors, axis=1)
    width = vec_pack.shape[1]
    vec_rows = jnp.pad(vec_pack, ((0, 0), (0, D - width)))[:, None]
    vec_rows = jnp.pad(vec_rows, ((0, 0), (0, 7), (0, 0)))

    def gathered(layer):
        local = pack_layer(
            inner_weight[layer], outer_weight[layer], up_weight[layer], down_weight[layer]
        )
        local = jnp.concatenate([local, vec_rows[layer]], axis=0)
        full = lax.all_gather(local, AXES, axis=0)
        held = full[:, 12 * rows, :width].astype(F32)
        pieces = []
        start = 0
        for vector in vectors:
            size = vector.shape[1]
            pieces.append(held[:, start : start + size].reshape(-1, D))
            start += size
        vec = jnp.concatenate(pieces, axis=0)
        if rows != ROWS:
            parts = [
                full[:, i * rows : (i + 1) * rows].reshape(PACKS, ROWS, D) for i in range(8)
            ]
            parts.append(full[:, 8 * rows : 12 * rows].reshape(PACKS, 4 * ROWS, D))
            full = jnp.concatenate(parts, axis=1)
        return full, vec

    weights = [gathered(layer) for layer in range(LAYERS)]
    taken_rows = jnp.take(offset_index.reshape(-1), offset_places())
    order = jnp.arange(BIAS_ROWS, dtype=jnp.int32)
    chosen = (taken_rows[:, None] == order[None, :]).astype(BF16)
    bias = run_expand_bias(bias_cells(bias_table, chosen))
    shape = place.grid_shape()
    aug = place.mask_lanes()

    x_zero = place.enter(clips_in, False)
    upstream = place.enter(cotangent, True)
    saved = []
    x = x_zero
    for layer in range(LAYERS):
        pack, vec = weights[layer]
        qkv, soft, rates, attended, middle = run_attention_forward(
            x, pack, vec, bias[layer], aug if layer == 1 else None
        )
        active, slope, result = run_feed_forward(
            middle, pack, vec, shape, F32 if layer == 0 else BF16
        )
        saved.append((x, qkv, soft, rates, attended, middle, active, slope))
        x = place.forth(result) if layer == 0 else result
    clips_out = place.leave(x, True)

    scattered = [None] * LAYERS
    vec_parts = [None] * LAYERS
    cell_parts = [None] * LAYERS

    def scatter(value, blocks):
        if rows != ROWS:
            per = ROWS // rows
            parts = []
            start = 0
            for size in blocks:
                part = value[:, start : start + size].reshape(PACKS * per, size // per, D)
                parts.append(part)
                start += size
            value = jnp.concatenate(parts, axis=1)
        return lax.psum_scatter(value, AXES, scatter_dimension=0, tiled=False)

    for layer in reversed(range(LAYERS)):
        pack, vec = weights[layer]
        x, qkv, soft, rates, attended, middle, active, slope = saved[layer]
        gmiddle, gattended, big, gvec_two = run_feed_backward(
            upstream, active, slope, middle, attended, pack, vec
        )
        upstream, small, gvec_one, cells = run_attention_backward(
            x, gattended, attended, rates, soft, qkv, gmiddle, pack, vec,
            F32 if layer == 1 else BF16,
        )
        scattered[layer] = (
            scatter(big, [ROWS] * 5 + [4 * ROWS]),
            scatter(small, [ROWS] * 3),
        )
        vec_parts[layer] = jnp.concatenate([gvec_one, gvec_two], axis=0)
        cell_parts[layer] = cells
        if layer == 1:
            upstream = place.back(upstream)
    clips_grad = place.leave(upstream, False)

    table_rows = cells_to_rows(jnp.stack(cell_parts))
    vec_total, table_total = lax.psum((jnp.stack(vec_parts), table_rows), AXES)
    table_total = select_rows(table_total, chosen, TN)

    device = lax.axis_index(AXES)

    def own(first, count):
        whole = vec_total[:, first : first + count].reshape(LAYERS, count * D)
        size = count * D // devices
        return lax.dynamic_slice_in_dim(whole, device * size, size, axis=1)

    def both(which, first, count):
        parts = []
        for layer in range(LAYERS):
            value = scattered[layer][which]
            columns = [
                value[first + i * rows : first + (i + 1) * rows] for i in range(count)
            ]
            parts.append(jnp.concatenate(columns, axis=1))
        return jnp.stack(parts)

    down = jnp.stack([scattered[layer][0][5 * rows : 9 * rows] for layer in range(LAYERS)])
    return (
        clips_out,
        clips_grad,
        own(0, 1),
        own(1, 1),
        both(1, 0, 3),
        own(2, 2),
        both(0, 0, 1),
        own(4, 1),
        own(5, 1),
        own(6, 1),
        both(0, rows, 4),
        own(8, 4),
        down,
        own(7, 1),
        table_total,
    )


def solution(mesh):
    clips = P("batch", "seq", None, None, None)
    vector = P(None, AXES)
    matrix = P(None, AXES, None)
    return jax.shard_map(
        per_device,
        mesh=mesh,
        in_specs=(
            clips, clips, P(), vector, vector, matrix, vector, matrix, vector, vector, vector,
            matrix, vector, matrix, vector, P(),
        ),
        out_specs=(
            clips, clips, vector, vector, matrix, vector, matrix, vector, vector, vector,
            matrix, vector, matrix, vector, P(),
        ),
        check_vma=False,
    )
```

```python
import functools

import jax
import jax.numpy as jnp
import numpy as np
from jax import lax
from jax.experimental import pallas as pl
from jax.experimental.pallas import tpu as pltpu
from jax.sharding import PartitionSpec as P

D = 512
HEADS = 16
HD = 32
FF = 2048
WT = 8
WH = 7
WW = 7
FRAMES = 16
HGT = 14
WID = 14
LAYERS = 2
SHIFT_T = 4
SHIFT_S = 3
WIN = 392
BIAS_ROWS = 2535
ROWS = 16
PACKS = D // ROWS
CELLS = (2 * WH - 1) * (2 * WW - 1)

EPSILON = 1e-05
MASKED = -100.0
LOG2E = 1.4426950408889634
LN2 = 0.6931471805599453
SCALE = HD**-0.5

BF16 = jnp.bfloat16
F32 = jnp.float32
AXES = ("batch", "seq")

NT = (((1,), (1,)), ((), ()))
TN = (((0,), (0,)), ((), ()))


def params():
    return pltpu.CompilerParams(
        vmem_limit_bytes=61 * 1024 * 1024, dimension_semantics=("arbitrary",)
    )


def cost(windows, microseconds):
    return pl.CostEstimate(
        flops=int(windows * microseconds * 1e9), bytes_accessed=0, transcendentals=0
    )


def dot(left, right, dims=(((1,), (0,)), ((), ()))):
    return lax.dot_general(left, right, dims, preferred_element_type=F32)


def normalize(values):
    average = jnp.mean(values, axis=-1, keepdims=True)
    centred = values - average
    rate = lax.rsqrt(jnp.mean(centred * centred, axis=-1, keepdims=True) + EPSILON)
    return centred * rate, rate


def row_sum(values):
    return jnp.sum(values, axis=0, keepdims=True)


def split_three(values):
    high = values.astype(BF16)
    rest = values - high.astype(F32)
    middle = rest.astype(BF16)
    low = (rest - middle.astype(F32)).astype(BF16)
    return high, middle, low


def square(ref, first):
    return ref[:, first : first + ROWS, :].reshape(D, D)


def grid_spec(shape):
    row_blocks, col_blocks = shape[1] // WH, shape[2] // WW
    per_clip = row_blocks * col_blocks
    return pl.BlockSpec(
        (1, WH, WW, WT, D),
        lambda i: (i // per_clip, (i % per_clip) // col_blocks, i % col_blocks, 0, 0),
    )


def window_spec(*tail):
    return pl.BlockSpec((1,) + tail, lambda i: (i,) + (0,) * len(tail))


def whole_spec(*shape):
    return pl.BlockSpec(shape, lambda i: (0,) * len(shape), pipeline_mode=pl.Buffered(1))


def pack_spec(rows, index):
    return pl.BlockSpec(
        (PACKS, rows, D), lambda i: (0, index, 0), pipeline_mode=pl.Buffered(1)
    )


def head_lanes(which):
    lane = lax.broadcasted_iota(jnp.int32, (1, 128), 1)
    return (lane // HD) == which


def lane_slice(group, base=0):
    return pl.ds(pl.multiple_of(base + group * 128, 128), 128)


def attention_forward(masked, *refs):
    if masked:
        x_ref, w_ref, vec_ref, bias_ref, augq_ref, augk_ref = refs[:6]
        qkv_ref, soft_ref, rate_ref, att_ref, mid_ref, vt_s, ot_s = refs[6:]
    else:
        x_ref, w_ref, vec_ref, bias_ref = refs[:4]
        qkv_ref, soft_ref, rate_ref, att_ref, mid_ref, vt_s, ot_s = refs[4:]
    x = x_ref[0].astype(F32).reshape(WIN, D)
    normed = (normalize(x)[0] * vec_ref[0:1] + vec_ref[1:2]).astype(BF16)
    query = (dot(normed, square(w_ref, 0)) + vec_ref[2:3]) * (SCALE * LOG2E)
    qkv_ref[0, :, 0:D] = query.astype(BF16)
    qkv_ref[0, :, D : 2 * D] = dot(normed, square(w_ref, ROWS)).astype(BF16)
    values = dot(normed, square(w_ref, 2 * ROWS)) + vec_ref[3:4]
    qkv_ref[0, :, 2 * D :] = values.astype(BF16)
    vt_s[...] = jnp.transpose(values).astype(BF16)

    def group(g, carry):
        query4 = qkv_ref[0, :, lane_slice(g)]
        keys4 = qkv_ref[0, :, lane_slice(g, D)]
        if masked:
            query4 = jnp.concatenate([query4, augq_ref[0]], axis=1)
        for which in range(4):
            head = g * 4 + which
            keys = jnp.where(head_lanes(which), keys4, jnp.zeros_like(keys4))
            if masked:
                keys = jnp.concatenate([keys, augk_ref[0]], axis=1)
            total = dot(keys, query4, NT) + bias_ref[head]
            peak = jnp.max(total, axis=0, keepdims=True)
            soft = jnp.exp2(total - peak).astype(BF16)
            soft_ref[0, head] = soft
            rows = pl.ds(pl.multiple_of(head * HD, HD), HD)
            left = jnp.concatenate([vt_s[rows, :], jnp.ones((16, WIN), BF16)], axis=0)
            joined = dot(left, soft)
            rate = 1.0 / joined[HD : HD + 1]
            rate_ref[0, pl.ds(head, 1), :] = rate
            ot_s[rows, :] = joined[:HD] * rate
        return carry

    lax.fori_loop(0, 4, group, 0)
    attended = jnp.transpose(ot_s[...]).astype(BF16)
    att_ref[0] = attended
    mid_ref[0] = x + dot(attended, square(w_ref, 3 * ROWS)) + vec_ref[4:5]


def run_attention_forward(x, pack, vec, bias, aug):
    windows = x.shape[0] * (x.shape[1] // WH) * (x.shape[2] // WW)
    masked = aug is not None
    extra = list(aug) if masked else []
    return pl.pallas_call(
        functools.partial(attention_forward, masked),
        grid=(windows,),
        in_specs=[
            grid_spec(x.shape),
            pack_spec(64, 0),
            whole_spec(12, D),
            whole_spec(HEADS, WIN, WIN),
        ]
        + [window_spec(WIN, 128)] * len(extra),
        out_specs=[
            window_spec(WIN, 3 * D),
            window_spec(HEADS, WIN, WIN),
            window_spec(HEADS, WIN),
            window_spec(WIN, D),
            window_spec(WIN, D),
        ],
        out_shape=[
            jax.ShapeDtypeStruct((windows, WIN, 3 * D), BF16),
            jax.ShapeDtypeStruct((windows, HEADS, WIN, WIN), BF16),
            jax.ShapeDtypeStruct((windows, HEADS, WIN), F32),
            jax.ShapeDtypeStruct((windows, WIN, D), BF16),
            jax.ShapeDtypeStruct((windows, WIN, D), F32),
        ],
        scratch_shapes=[pltpu.VMEM((D, WIN), BF16), pltpu.VMEM((D, WIN), F32)],
        cost_estimate=cost(windows, 10),
        compiler_params=params(),
    )(x, pack, vec, bias, *extra)


def gelu_parts(hidden):
    cumulative = 0.5 + 0.5 * lax.erf(hidden * (0.5**0.5))
    density = jnp.exp(-0.5 * hidden * hidden) * 0.3989422804014327
    return hidden * cumulative, cumulative + hidden * density


def feed_forward(mid_ref, up_ref, down_ref, vec_ref, act_ref, slope_ref, out_ref):
    middle = mid_ref[0]
    normed = (normalize(middle)[0] * vec_ref[5:6] + vec_ref[6:7]).astype(BF16)
    total = middle + vec_ref[7:8]
    for part in range(4):
        lanes = slice(part * D, (part + 1) * D)
        hidden = dot(normed, square(up_ref, part * ROWS)) + vec_ref[8 + part : 9 + part]
        active, slope = gelu_parts(hidden)
        active = active.astype(BF16)
        act_ref[0, :, lanes] = active
        slope_ref[0, :, lanes] = slope.astype(BF16)
        down = down_ref[part * 8 : part * 8 + 8].reshape(D, D)
        total = total + dot(active, down)
    out_ref[0] = total.reshape(WH, WW, WT, D).astype(out_ref.dtype)


def run_feed_forward(middle, pack, vec, grid_shape, dtype):
    windows = middle.shape[0]
    return pl.pallas_call(
        feed_forward,
        grid=(windows,),
        in_specs=[
            window_spec(WIN, D),
            pack_spec(64, 1),
            pack_spec(64, 2),
            whole_spec(12, D),
        ],
        out_specs=[window_spec(WIN, FF), window_spec(WIN, FF), grid_spec(grid_shape)],
        out_shape=[
            jax.ShapeDtypeStruct((windows, WIN, FF), BF16),
            jax.ShapeDtypeStruct((windows, WIN, FF), BF16),
            jax.ShapeDtypeStruct(grid_shape, dtype),
        ],
        cost_estimate=cost(windows, 4),
        compiler_params=params(),
    )(middle, pack, pack, vec)


def norm_back(normal, rate, gained):
    first = jnp.mean(gained, axis=-1, keepdims=True)
    second = jnp.mean(gained * normal, axis=-1, keepdims=True)
    return (gained - first - normal * second) * rate


def feed_backward(
    grad_ref, act_ref, slope_ref, mid_ref, att_ref, in_ref, up_ref, down_ref, vec_ref,
    gmid_ref, gatt_ref, result_ref, gvec_ref, pack_ref,
):
    @pl.when(pl.program_id(0) == 0)
    def _():
        pack_ref[...] = jnp.zeros_like(pack_ref)
        gvec_ref[...] = jnp.zeros_like(gvec_ref)

    grad = grad_ref[0].astype(F32).reshape(WIN, D)
    gvec_ref[3:4] += row_sum(grad)
    grad_low = grad.astype(BF16)
    normal, rate = normalize(mid_ref[0])
    normed = (normal * vec_ref[5:6] + vec_ref[6:7]).astype(BF16)
    gnormed = jnp.zeros((WIN, D), F32)
    for part in range(4):
        lanes = slice(part * D, (part + 1) * D)
        active = act_ref[0, :, lanes]
        pack_ref[part * 8 : part * 8 + 8, 80:144, :] += dot(active, grad_low, TN).reshape(8, 64, D)
        down = down_ref[part * 8 : part * 8 + 8].reshape(D, D)
        ghidden = dot(grad_low, down, NT) * slope_ref[0, :, lanes].astype(F32)
        gvec_ref[4 + part : 5 + part] += row_sum(ghidden)
        ghidden = ghidden.astype(BF16)
        first = ROWS * (1 + part)
        pack_ref[:, first : first + ROWS, :] += dot(normed, ghidden, TN).reshape(PACKS, ROWS, D)
        gnormed = gnormed + dot(ghidden, square(up_ref, part * ROWS), NT)
    gvec_ref[1:2] += row_sum(gnormed * normal)
    gvec_ref[2:3] += row_sum(gnormed)
    gmid = grad + norm_back(normal, rate, gnormed * vec_ref[5:6])
    gmid_ref[0] = gmid
    gvec_ref[0:1] += row_sum(gmid)
    gmid_low = gmid.astype(BF16)
    pack_ref[:, 0:ROWS, :] += dot(att_ref[0], gmid_low, TN).reshape(PACKS, ROWS, D)
    gatt_ref[0] = dot(gmid_low, square(in_ref, 3 * ROWS), NT).astype(BF16)

    @pl.when(pl.program_id(0) == pl.num_programs(0) - 1)
    def _():
        result_ref[...] = pack_ref[...].astype(result_ref.dtype)


def run_feed_backward(grad, active, slope, middle, attended, pack, vec, dtype):
    windows = middle.shape[0]
    return pl.pallas_call(
        feed_backward,
        grid=(windows,),
        in_specs=[
            grid_spec(grad.shape),
            window_spec(WIN, FF),
            window_spec(WIN, FF),
            window_spec(WIN, D),
            window_spec(WIN, D),
            pack_spec(64, 0),
            pack_spec(64, 1),
            pack_spec(64, 2),
            whole_spec(12, D),
        ],
        out_specs=[
            window_spec(WIN, D),
            window_spec(WIN, D),
            whole_spec(PACKS, 144, D),
            pl.BlockSpec((8, D), lambda i: (0, 0)),
        ],
        out_shape=[
            jax.ShapeDtypeStruct((windows, WIN, D), F32),
            jax.ShapeDtypeStruct((windows, WIN, D), BF16),
            jax.ShapeDtypeStruct((PACKS, 144, D), dtype),
            jax.ShapeDtypeStruct((8, D), F32),
        ],
        scratch_shapes=[pltpu.VMEM((PACKS, 144, D), F32)],
        cost_estimate=cost(windows, 7),
        compiler_params=params(),
    )(grad, active, slope, middle, attended, pack, pack, pack, vec)


def attention_backward(
    x_ref, gatt_ref, att_ref, rate_ref, soft_ref, qkv_ref, gmid_ref, in_ref, vec_ref,
    out_ref, result_ref, gvec_ref, table_ref,
    pack_ref, sum_s, kt_s, qt_s, do_s, gk_s, gv_s, wide_s,
):
    step = pl.program_id(0)

    @pl.when(step == 0)
    def _():
        sum_s[...] = jnp.zeros_like(sum_s)
        pack_ref[...] = jnp.zeros_like(pack_ref)
        gvec_ref[...] = jnp.zeros_like(gvec_ref)

    lane = lax.broadcasted_iota(jnp.int32, (1, 128), 1)
    head_row = lax.broadcasted_iota(jnp.int32, (3 * HEADS, D), 0) % HEADS
    head_col = lax.broadcasted_iota(jnp.int32, (3 * HEADS, D), 1) // HD
    spread = jnp.where(head_row == head_col, 1.0, 0.0).astype(BF16)
    rates = jnp.concatenate(split_three(rate_ref[0]), axis=0)
    scaled = (gatt_ref[0].astype(F32) * dot(rates, spread, TN)).astype(BF16)
    do_s[...] = scaled
    product = scaled.astype(F32) * att_ref[0].astype(F32)
    gather_row = lax.broadcasted_iota(jnp.int32, (D, 128), 0) // HD
    gather_col = lax.broadcasted_iota(jnp.int32, (D, 128), 1)
    gather = jnp.where(
        (gather_row == gather_col % HEADS) & (gather_col < 3 * HEADS), 1.0, 0.0
    ).astype(BF16)
    high = product.astype(BF16)
    low = (product - high.astype(F32)).astype(BF16)
    inner = dot(high, gather) + dot(low, gather)
    first, second, third = split_three(inner)
    inner = jnp.where(lane < HEADS, first, jnp.where(lane < 2 * HEADS, second, third))
    kt_s[...] = jnp.transpose(qkv_ref[0, :, D : 2 * D].astype(F32)).astype(BF16)

    def group(g, carry):
        query4 = qkv_ref[0, :, lane_slice(g)]
        values4 = qkv_ref[0, :, lane_slice(g, 2 * D)]
        grad4 = do_s[:, lane_slice(g)]
        right = jnp.concatenate([grad4, inner], axis=1)
        zero = jnp.zeros_like(grad4)
        gvalues = jnp.zeros((WIN, 128), F32)
        gkeys = jnp.zeros((WIN, 128), F32)
        for which in range(4):
            head = g * 4 + which
            mine = head_lanes(which)
            minus = jnp.where((lane % HEADS == head) & (lane < 3 * HEADS), -1.0, 0.0)
            minus = jnp.broadcast_to(minus, (WIN, 128)).astype(BF16)
            left = jnp.concatenate([jnp.where(mine, values4, zero), minus], axis=1)
            soft = soft_ref[0, head]
            gtotal = soft.astype(F32) * dot(left, right, NT)
            sum_s[head] += gtotal
            gtotal = gtotal.astype(BF16)
            gvalues = gvalues + dot(soft, jnp.where(mine, grad4, zero))
            gkeys = gkeys + dot(gtotal, jnp.where(mine, query4, zero))
            rows = pl.ds(pl.multiple_of(head * HD, HD), HD)
            qt_s[rows, :] = dot(kt_s[rows, :], gtotal)
        gv_s[:, lane_slice(g)] = gvalues.astype(BF16)
        gk_s[:, lane_slice(g)] = (gkeys * LN2).astype(BF16)
        return carry

    lax.fori_loop(0, 4, group, 0)
    gquery = jnp.transpose(qt_s[...]).astype(BF16)
    gkeys = gk_s[...]
    gvalues = gv_s[...]
    normal, rate = normalize(x_ref[0].astype(F32).reshape(WIN, D))
    normed = (normal * vec_ref[0:1] + vec_ref[1:2]).astype(BF16)
    pack_ref[:, 0:ROWS, :] += (dot(normed, gquery, TN) * SCALE).reshape(PACKS, ROWS, D)
    pack_ref[:, ROWS : 2 * ROWS, :] += dot(normed, gkeys, TN).reshape(PACKS, ROWS, D)
    pack_ref[:, 2 * ROWS :, :] += dot(normed, gvalues, TN).reshape(PACKS, ROWS, D)
    gvec_ref[2:3] += row_sum(gquery.astype(F32)) * SCALE
    gvec_ref[3:4] += row_sum(gvalues.astype(F32))
    gnormed = (
        dot(gquery, square(in_ref, 0), NT) * SCALE
        + dot(gkeys, square(in_ref, ROWS), NT)
        + dot(gvalues, square(in_ref, 2 * ROWS), NT)
    )
    gvec_ref[0:1] += row_sum(gnormed * normal)
    gvec_ref[1:2] += row_sum(gnormed)
    grad = gmid_ref[0] + norm_back(normal, rate, gnormed * vec_ref[0:1])
    out_ref[0] = grad.reshape(WH, WW, WT, D).astype(out_ref.dtype)

    @pl.when(step == pl.num_programs(0) - 1)
    def _():
        result_ref[...] = pack_ref[...].astype(result_ref.dtype)
        table_ref[...] = jnp.zeros_like(table_ref)
        for col in range(WW):
            wide_s[...] = jnp.zeros_like(wide_s)
            for row in range(WH):
                place = (row * WW + col) * WT
                low_lane = (WH - 1 - row) * WW * WT
                wide_s[:, low_lane : low_lane + WIN] += sum_s[:, place : place + WT, :].reshape(
                    HEADS * WT, WIN
                )
            for shift in range(2 * WH - 1):
                low_lane = (shift * (2 * WW - 1) + WW - 1 - col) * WT
                table_ref[:, low_lane : low_lane + WW * WT] += wide_s[
                    :, shift * WW * WT : (shift + 1) * WW * WT
                ]


def run_attention_backward(
    x, gattended, attended, rates, soft, qkv, gmiddle, pack, vec, dtype, pack_dtype
):
    windows = gmiddle.shape[0]
    return pl.pallas_call(
        attention_backward,
        grid=(windows,),
        in_specs=[
            grid_spec(x.shape),
            window_spec(WIN, D),
            window_spec(WIN, D),
            window_spec(HEADS, WIN),
            window_spec(HEADS, WIN, WIN),
            window_spec(WIN, 3 * D),
            window_spec(WIN, D),
            pack_spec(64, 0),
            whole_spec(12, D),
        ],
        out_specs=[
            grid_spec(x.shape),
            whole_spec(PACKS, 48, D),
            pl.BlockSpec((4, D), lambda i: (0, 0)),
            pl.BlockSpec((HEADS * WT, CELLS * WT), lambda i: (0, 0)),
        ],
        out_shape=[
            jax.ShapeDtypeStruct(x.shape, dtype),
            jax.ShapeDtypeStruct((PACKS, 48, D), pack_dtype),
            jax.ShapeDtypeStruct((4, D), F32),
            jax.ShapeDtypeStruct((HEADS * WT, CELLS * WT), F32),
        ],
        scratch_shapes=[
            pltpu.VMEM((PACKS, 48, D), F32),
            pltpu.VMEM((HEADS, WIN, WIN), F32),
            pltpu.VMEM((D, WIN), BF16),
            pltpu.VMEM((D, WIN), F32),
            pltpu.VMEM((WIN, D), BF16),
            pltpu.VMEM((WIN, D), BF16),
            pltpu.VMEM((WIN, D), BF16),
            pltpu.VMEM((HEADS * WT, (2 * WH - 1) * WW * WT), F32),
        ],
        cost_estimate=cost(windows, 12),
        compiler_params=params(),
    )(x, gattended, attended, rates, soft, qkv, gmiddle, pack, vec)


def expand_bias(cells_ref, out_ref, wide_s):
    for col in range(WW):
        for shift in range(2 * WH - 1):
            low_lane = (shift * (2 * WW - 1) + WW - 1 - col) * WT
            wide_s[:, shift * WW * WT : (shift + 1) * WW * WT] = cells_ref[
                :, low_lane : low_lane + WW * WT
            ]
        for row in range(WH):
            place = (row * WW + col) * WT
            low_lane = (WH - 1 - row) * WW * WT
            out_ref[:, place : place + WT, :] = wide_s[:, low_lane : low_lane + WIN].reshape(
                HEADS, WT, WIN
            )


def run_expand_bias(cells):
    return pl.pallas_call(
        expand_bias,
        out_shape=jax.ShapeDtypeStruct((HEADS, WIN, WIN), F32),
        scratch_shapes=[pltpu.VMEM((HEADS * WT, (2 * WH - 1) * WW * WT), F32)],
        compiler_params=pltpu.CompilerParams(vmem_limit_bytes=61 * 1024 * 1024),
    )(cells)


AUX_ROWS = 8
SHARES = ((0, 0, 96, 0), (0, 96, 48, 1), (1, 0, 48, 1), (2, 0, AUX_ROWS, 0))


def fold_gradients(*refs):
    operands = refs[:3]
    big_out, small_out, aux_out = refs[3:6]
    buffers = refs[6:18]
    send_sem, recv_sem, wide_send, wide_recv = refs[18:]
    batch = lax.axis_index("batch")
    y = lax.axis_index("seq")
    z, x, core = batch // 4, (batch // 2) % 2, batch % 2
    count = len(SHARES)

    def device(z_to, x_to, core_to, y_to):
        return ((z_to * 2 + x_to) * 2 + core_to, y_to)

    barrier = pltpu.get_barrier_semaphore()

    def greet(k, carry):
        other = lax.rem(batch * 2 + y + k, 32)
        pl.semaphore_signal(
            barrier, inc=1, device_id=(other // 2, other % 2), device_id_type=pl.DeviceIdType.MESH
        )
        return carry

    lax.fori_loop(1, 32, greet, 0)
    pl.semaphore_wait(barrier, 31)

    def send(number, source, target, to):
        copy = pltpu.make_async_remote_copy(
            src_ref=source,
            dst_ref=target,
            send_sem=send_sem.at[number],
            recv_sem=recv_sem.at[number],
            device_id=to,
            device_id_type=pl.DeviceIdType.MESH,
        )
        copy.start()
        return copy

    copies = []
    for k, (which, first, size, order) in enumerate(SHARES):
        source = operands[which].at[:, :, 1 - core, :, pl.ds(first, size), :]
        copies.append(send(k, source, buffers[3 * k], device(z, x, 1 - core, y)))
    for k, (which, first, size, order) in enumerate(SHARES):
        copies[k].wait()
        held = buffers[3 * k]

        def add_core(i, carry, which=which, first=first, size=size, held=held):
            a, b = i // 2, i % 2
            mine = operands[which][a, b, core, :, first : first + size, :].astype(F32)
            held[a, b] = (held[a, b].astype(F32) + mine).astype(held.dtype)
            return carry

        lax.fori_loop(0, 8, add_core, 0)
        if order == 0:
            copies.append(send(count + k, held.at[:, 1 - x], buffers[3 * k + 1], device(z, 1 - x, core, y)))
        else:
            copies.append(send(count + k, held.at[:, :, 1 - y], buffers[3 * k + 1], device(z, x, core, 1 - y)))
    for k, (which, first, size, order) in enumerate(SHARES):
        copies[count + k].wait()
        before, held = buffers[3 * k], buffers[3 * k + 1]

        def add_next(i, carry, order=order, before=before, held=held):
            a, b = i // 2, i % 2
            mine = before[a, x, b] if order == 0 else before[a, b, y]
            held[a, b] = (held[a, b].astype(F32) + mine.astype(F32)).astype(held.dtype)
            return carry

        lax.fori_loop(0, 8, add_next, 0)
        if order == 0:
            copies.append(send(2 * count + k, held.at[:, 1 - y], buffers[3 * k + 2].at[pl.ds(0, 4)], device(z, x, core, 1 - y)))
        else:
            copies.append(send(2 * count + k, held.at[:, 1 - x], buffers[3 * k + 2].at[pl.ds(0, 4)], device(z, 1 - x, core, y)))
    far = []
    for k, (which, first, size, order) in enumerate(SHARES):
        copies[2 * count + k].wait()
        before, held = buffers[3 * k + 1], buffers[3 * k + 2]

        def add_last(a, carry, order=order, before=before, held=held):
            mine = before[a, y] if order == 0 else before[a, x]
            held[a] = (held[a].astype(F32) + mine.astype(F32)).astype(held.dtype)
            return carry

        lax.fori_loop(0, 4, add_last, 0)
        for step in range(1, 4):
            other = lax.rem(z + step, 4)
            far.append(
                send(
                    3 * count + 3 * k + step - 1,
                    held.at[other],
                    held.at[3 + step],
                    device(other, x, core, y),
                )
            )
    for k, (which, first, size, order) in enumerate(SHARES):
        for step in range(1, 4):
            far[3 * k + step - 1].wait()
        held = buffers[3 * k + 2]
        total = held[z].astype(F32) + held[4].astype(F32)
        total = total + held[5].astype(F32) + held[6].astype(F32)
        if which == 0:
            big_out[first : first + size, :] = total
        elif which == 1:
            small_out[...] = total
        else:
            aux_out[batch * 2 + y] = total

    def spread(k, carry):
        other = lax.rem(batch * 2 + y + k, 32)
        pltpu.make_async_remote_copy(
            src_ref=aux_out.at[batch * 2 + y],
            dst_ref=aux_out.at[batch * 2 + y],
            send_sem=wide_send,
            recv_sem=wide_recv,
            device_id=(other // 2, other % 2),
            device_id_type=pl.DeviceIdType.MESH,
        ).start()
        return carry

    lax.fori_loop(1, 32, spread, 0)
    others = aux_out.at[pl.ds(0, 31)]
    pltpu.make_async_copy(others, others, wide_send).wait()
    pltpu.make_async_copy(others, others, wide_recv).wait()


def run_fold_gradients(big, small, aux):
    operands = [value.reshape((4, 2, 2, 2) + value.shape[1:]) for value in (big, small, aux)]
    scratch = []
    for which, first, size, order in SHARES:
        dtype = operands[which].dtype
        scratch.append(pltpu.VMEM((4, 2, 2, size, D), dtype))
        scratch.append(pltpu.VMEM((4, 2, size, D), dtype))
        scratch.append(pltpu.VMEM((7, size, D), dtype))
    semaphores = 6 * len(SHARES)
    return pl.pallas_call(
        fold_gradients,
        in_specs=[pl.BlockSpec(memory_space=pltpu.VMEM)] * 3,
        out_specs=[pl.BlockSpec(memory_space=pltpu.VMEM)] * 3,
        out_shape=[
            jax.ShapeDtypeStruct((144, D), F32),
            jax.ShapeDtypeStruct((48, D), F32),
            jax.ShapeDtypeStruct((32, AUX_ROWS, D), F32),
        ],
        scratch_shapes=scratch
        + [
            pltpu.SemaphoreType.DMA((semaphores,)),
            pltpu.SemaphoreType.DMA((semaphores,)),
            pltpu.SemaphoreType.DMA,
            pltpu.SemaphoreType.DMA,
        ],
        compiler_params=pltpu.CompilerParams(
            vmem_limit_bytes=61 * 1024 * 1024, collective_id=1, has_side_effects=True
        ),
    )(*operands)


def offset_places():
    frame, row, col = np.meshgrid(
        np.arange(1 - WT, WT), np.arange(1 - WH, WH), np.arange(1 - WW, WW), indexing="ij"
    )

    def place(f, r, c):
        return (np.maximum(f, 0) * WH + np.maximum(r, 0)) * WW + np.maximum(c, 0)

    return (place(frame, row, col) * WIN + place(-frame, -row, -col)).reshape(-1)


def interleave():
    cell = np.arange(CELLS * WT)
    source = jnp.asarray((cell % WT) * CELLS + cell // WT, jnp.int32)
    order = jnp.arange(CELLS * WT, dtype=jnp.int32)
    return (order[:, None] == source[None, :]).astype(BF16)


def join_three(values, axis):
    first, second, third = jnp.split(values, 3, axis=axis)
    return first + second + third


def bias_cells(tables, chosen, order):
    flat = jnp.concatenate([tables[layer] for layer in range(LAYERS)], axis=1) * LOG2E
    pieces = jnp.concatenate(split_three(flat), axis=1)
    taken = dot(pieces, chosen, (((0,), (1,)), ((), ()))).astype(BF16)
    placed = jnp.stack(
        [taken[:, (WT - 1 - t) * CELLS : (2 * WT - 1 - t) * CELLS] for t in range(WT)], axis=1
    )
    cells = dot(placed.reshape(-1, WT * CELLS), order)
    return join_three(cells, 0).reshape(LAYERS, HEADS * WT, CELLS * WT)


def cells_to_rows(cells, order):
    pieces = jnp.concatenate(split_three(cells.reshape(-1, CELLS * WT)), axis=0)
    placed = join_three(dot(pieces, order, NT), 0).reshape(LAYERS * HEADS, WT, CELLS * WT)
    parts = [
        jnp.pad(placed[:, t], ((0, 0), ((WT - 1 - t) * CELLS, t * CELLS))) for t in range(WT)
    ]
    return functools.reduce(jnp.add, parts)


def rows_to_table(rows, chosen):
    pieces = jnp.concatenate(split_three(rows), axis=0)
    total = join_three(dot(chosen, pieces, (((0,), (1,)), ((), ()))), 1)
    return jnp.stack([total[:, i * HEADS : (i + 1) * HEADS] for i in range(LAYERS)])


def spatial_blocks(field):
    clip_count, frames_here, width = (field.shape[0], field.shape[1], field.shape[-1])
    shaped = field.reshape(clip_count, frames_here, HGT // WH, WH, WID // WW, WW, width)
    shaped = shaped.transpose(0, 2, 4, 1, 3, 5, 6)
    return shaped.reshape(clip_count * (HGT // WH) * (WID // WW), frames_here, WH * WW, width)


def roll_space(field, amount, first):
    return jnp.roll(field, (amount, amount), axis=(first, first + 1))


def swap_halves(part):
    return lax.ppermute(part, "seq", [(0, 1), (1, 0)])


class Placement:
    def __init__(self, clip_count, frames_here):
        self.clips = clip_count
        self.frames = frames_here
        self.parts = lax.axis_size("seq")
        self.near = self.parts == 2 and frames_here == WT

    def grid_shape(self):
        if self.near:
            return (self.clips, HGT, WID, WT, D)
        columns = self.clips * 4 // self.parts
        return (columns * 2, WH, WW, WT, D)

    def enter(self, field, shifted):
        if self.near:
            if shifted:
                arrived = swap_halves(field[:, :SHIFT_T])
                field = jnp.concatenate([field[:, SHIFT_T:], arrived], axis=1)
                field = roll_space(field, -SHIFT_S, 2)
            return field.transpose(0, 2, 3, 1, 4)
        if shifted:
            field = roll_space(field, -SHIFT_S, 2)
        columns = lax.all_to_all(
            spatial_blocks(field), "seq", split_axis=0, concat_axis=1, tiled=True
        )
        if shifted:
            columns = jnp.roll(columns, -SHIFT_T, axis=1)
        windows = columns.reshape(-1, WT, WH, WW, D)
        return windows.transpose(0, 2, 3, 1, 4)

    def leave(self, grid, shifted):
        if self.near:
            field = grid.transpose(0, 3, 1, 2, 4)
            if shifted:
                field = roll_space(field, SHIFT_S, 2)
                arrived = swap_halves(field[:, SHIFT_T:])
                field = jnp.concatenate([arrived, field[:, :SHIFT_T]], axis=1)
            return field
        columns = grid.transpose(0, 3, 1, 2, 4).reshape(-1, FRAMES, WH * WW, D)
        if shifted:
            columns = jnp.roll(columns, SHIFT_T, axis=1)
        columns = lax.all_to_all(columns, "seq", split_axis=1, concat_axis=0, tiled=True)
        shaped = columns.reshape(self.clips, HGT // WH, WID // WW, self.frames, WH, WW, D)
        shaped = shaped.transpose(0, 3, 1, 4, 2, 5, 6)
        field = shaped.reshape(self.clips, self.frames, HGT, WID, D)
        return roll_space(field, SHIFT_S, 2) if shifted else field

    def forth(self, grid):
        if self.near:
            arrived = swap_halves(grid[..., :SHIFT_T, :])
            grid = jnp.concatenate([grid[..., SHIFT_T:, :], arrived], axis=3)
            return roll_space(grid, -SHIFT_S, 1)
        return self.enter(self.leave(grid, False), True)

    def back(self, grid):
        if self.near:
            grid = roll_space(grid, SHIFT_S, 1)
            arrived = swap_halves(grid[..., SHIFT_T:, :])
            return jnp.concatenate([arrived, grid[..., :SHIFT_T, :]], axis=3)
        return self.enter(self.leave(grid, True), False)

    def mask_lanes(self):
        if self.near:
            index = jnp.arange(self.clips * 4, dtype=jnp.int32)
            late = jnp.full(index.shape, lax.axis_index("seq"), jnp.int32)
            block = index % 4
        else:
            columns = self.clips * 4 // self.parts
            index = jnp.arange(columns * 2, dtype=jnp.int32)
            late = index % 2
            block = (lax.axis_index("seq") * columns + index // 2) % 4
        place = np.arange(WIN)
        frame_late = jnp.asarray(place % WT >= WT - SHIFT_T).astype(jnp.int32)
        row_late = jnp.asarray(place // (WT * WW) >= WH - SHIFT_S).astype(jnp.int32)
        col_late = jnp.asarray(place // WT % WW >= WW - SHIFT_S).astype(jnp.int32)
        region = (
            late[:, None] * frame_late * 4
            + (block // 2)[:, None] * row_late * 2
            + (block % 2)[:, None] * col_late
        )
        lane = np.arange(128)
        same = (region[:, :, None] == lane % 8) & (lane < 24)
        pieces = []
        rest = np.float32(MASKED * LOG2E)
        for _ in range(3):
            piece = np.float32(np.asarray(rest).astype(BF16))
            pieces.append(piece)
            rest = np.float32(rest - piece)
        piece_of = np.zeros((128,), np.float32)
        for number, piece in enumerate(pieces):
            piece_of[8 * number : 8 * number + 8] = -piece
            piece_of[24 + number] = piece
        always = (lane >= 24) & (lane < 27)
        on_keys = jnp.where(same | always, 1.0, 0.0)
        return (on_keys * piece_of).astype(BF16), on_keys.astype(BF16)


def pack_layer(inner, outer, up, down):
    parts = [inner[:, i * D : (i + 1) * D] for i in range(3)] + [outer]
    parts = parts + [up[:, i * D : (i + 1) * D] for i in range(4)] + [down]
    return jnp.concatenate(parts, axis=0)


def per_device(
    clips_in,
    cotangent,
    offset_index,
    first_gain,
    first_shift,
    inner_weight,
    inner_bias,
    outer_weight,
    outer_bias,
    second_gain,
    second_shift,
    up_weight,
    up_bias,
    down_weight,
    down_bias,
    bias_table,
):
    place = Placement(clips_in.shape[0], clips_in.shape[1])
    rows = inner_weight.shape[1]
    devices = D // rows
    vectors = [
        first_gain, first_shift, inner_bias, outer_bias, second_gain, second_shift,
        down_bias, up_bias,
    ]
    vec_pack = jnp.concatenate(vectors, axis=1)
    width = vec_pack.shape[1]
    vec_rows = jnp.pad(vec_pack, ((0, 0), (0, D - width)))[:, None]
    vec_rows = jnp.pad(vec_rows, ((0, 0), (0, 7), (0, 0)))

    def gathered(layer):
        local = pack_layer(
            inner_weight[layer], outer_weight[layer], up_weight[layer], down_weight[layer]
        )
        local = jnp.concatenate([local, vec_rows[layer]], axis=0)
        full = lax.all_gather(local, AXES, axis=0)
        held = full[:, 12 * rows, :width].astype(F32)
        pieces = []
        start = 0
        for vector in vectors:
            size = vector.shape[1]
            pieces.append(held[:, start : start + size].reshape(-1, D))
            start += size
        vec = jnp.concatenate(pieces, axis=0)
        if rows != ROWS:
            parts = [
                full[:, i * rows : (i + 1) * rows].reshape(PACKS, ROWS, D) for i in range(8)
            ]
            parts.append(full[:, 8 * rows : 12 * rows].reshape(PACKS, 4 * ROWS, D))
            full = jnp.concatenate(parts, axis=1)
        return full, vec

    weights = [gathered(layer) for layer in range(LAYERS)]
    taken_rows = jnp.take(offset_index.reshape(-1), offset_places())
    order = jnp.arange(BIAS_ROWS, dtype=jnp.int32)
    chosen = (taken_rows[:, None] == order[None, :]).astype(BF16)
    interleaved = interleave()
    cells_in = bias_cells(bias_table, chosen, interleaved)
    bias = [run_expand_bias(cells_in[layer]) for layer in range(LAYERS)]
    shape = place.grid_shape()
    aug = place.mask_lanes()

    x_zero = place.enter(clips_in, False)
    upstream = place.enter(cotangent, True)
    saved = []
    x = x_zero
    for layer in range(LAYERS):
        pack, vec = weights[layer]
        qkv, soft, rates, attended, middle = run_attention_forward(
            x, pack, vec, bias[layer], aug if layer == 1 else None
        )
        active, slope, result = run_feed_forward(
            middle, pack, vec, shape, F32 if layer == 0 else BF16
        )
        saved.append((x, qkv, soft, rates, attended, middle, active, slope))
        x = place.forth(result) if layer == 0 else result
    clips_out = place.leave(x, True)

    scattered = [None] * LAYERS
    vec_parts = [None] * LAYERS
    cell_parts = [None] * LAYERS

    def scatter(value, blocks):
        if rows != ROWS:
            per = ROWS // rows
            parts = []
            start = 0
            for size in blocks:
                part = value[:, start : start + size].reshape(PACKS * per, size // per, D)
                parts.append(part)
                start += size
            value = jnp.concatenate(parts, axis=1)
        return lax.psum_scatter(value, AXES, scatter_dimension=0, tiled=False)

    folded = lax.axis_size("batch") == 16 and lax.axis_size("seq") == 2
    for layer in reversed(range(LAYERS)):
        pack, vec = weights[layer]
        x, qkv, soft, rates, attended, middle, active, slope = saved[layer]
        gmiddle, gattended, big, gvec_two = run_feed_backward(
            upstream, active, slope, middle, attended, pack, vec, F32 if layer == 1 or not folded else BF16
        )
        upstream, small, gvec_one, cells = run_attention_backward(
            x, gattended, attended, rates, soft, qkv, gmiddle, pack, vec,
            F32 if layer == 1 else BF16, F32 if layer == 1 or not folded else BF16,
        )
        if layer == 1 or not folded:
            scattered[layer] = (
                scatter(big, [ROWS] * 5 + [4 * ROWS]),
                scatter(small, [ROWS] * 3),
            )
        vec_parts[layer] = jnp.concatenate([gvec_one, gvec_two], axis=0)
        cell_parts[layer] = cells
        if layer == 1:
            upstream = place.back(upstream)
    clips_grad = place.leave(upstream, False)

    table_rows = cells_to_rows(jnp.stack(cell_parts), interleaved)
    vec_stack = jnp.stack(vec_parts)
    if folded:
        aux = jnp.concatenate([table_rows.reshape(-1), vec_stack.reshape(-1)])
        used = aux.shape[0]
        aux = jnp.pad(aux, (0, PACKS * AUX_ROWS * D - used)).reshape(PACKS, AUX_ROWS, D)
        big_own, small_own, aux = run_fold_gradients(big, small, aux)
        scattered[0] = (big_own, small_own)
        aux = aux.reshape(-1)[:used]
        table_total = aux[: table_rows.size].reshape(table_rows.shape)
        vec_total = aux[table_rows.size :].reshape(vec_stack.shape)
    else:
        vec_total, table_total = lax.psum((vec_stack, table_rows), AXES)
    table_total = rows_to_table(table_total, chosen)

    device = lax.axis_index(AXES)

    def own(first, count):
        whole = vec_total[:, first : first + count].reshape(LAYERS, count * D)
        size = count * D // devices
        return lax.dynamic_slice_in_dim(whole, device * size, size, axis=1)

    def both(which, first, count):
        parts = []
        for layer in range(LAYERS):
            value = scattered[layer][which]
            columns = [
                value[first + i * rows : first + (i + 1) * rows] for i in range(count)
            ]
            parts.append(jnp.concatenate(columns, axis=1))
        return jnp.stack(parts)

    down = jnp.stack([scattered[layer][0][5 * rows : 9 * rows] for layer in range(LAYERS)])
    return (
        clips_out,
        clips_grad,
        own(0, 1),
        own(1, 1),
        both(1, 0, 3),
        own(2, 2),
        both(0, 0, 1),
        own(4, 1),
        own(5, 1),
        own(6, 1),
        both(0, rows, 4),
        own(8, 4),
        down,
        own(7, 1),
        table_total,
    )


def solution(mesh):
    clips = P("batch", "seq", None, None, None)
    vector = P(None, AXES)
    matrix = P(None, AXES, None)
    return jax.shard_map(
        per_device,
        mesh=mesh,
        in_specs=(
            clips, clips, P(), vector, vector, matrix, vector, matrix, vector, vector, vector,
            matrix, vector, matrix, vector, P(),
        ),
        out_specs=(
            clips, clips, vector, vector, matrix, vector, matrix, vector, vector, vector,
            matrix, vector, matrix, vector, P(),
        ),
        check_vma=False,
    )
```

```python
import functools

import jax
import jax.numpy as jnp
import numpy as np
from jax import lax
from jax.experimental import pallas as pl
from jax.experimental.pallas import tpu as pltpu
from jax.sharding import PartitionSpec as P

D = 512
HEADS = 16
HD = 32
FF = 2048
WT = 8
WH = 7
WW = 7
FRAMES = 16
HGT = 14
WID = 14
LAYERS = 2
SHIFT_T = 4
SHIFT_S = 3
WIN = 392
BIAS_ROWS = 2535
ROWS = 16
PACKS = D // ROWS
CELLS = (2 * WH - 1) * (2 * WW - 1)

EPSILON = 1e-05
MASKED = -100.0
LOG2E = 1.4426950408889634
LN2 = 0.6931471805599453
SCALE = HD**-0.5

BF16 = jnp.bfloat16
F32 = jnp.float32
AXES = ("batch", "seq")

NT = (((1,), (1,)), ((), ()))
TN = (((0,), (0,)), ((), ()))


def params(collective=None):
    return pltpu.CompilerParams(
        vmem_limit_bytes=61 * 1024 * 1024,
        dimension_semantics=("arbitrary",),
        collective_id=collective,
        has_side_effects=collective is not None,
    )


def cost(windows, microseconds):
    return pl.CostEstimate(
        flops=int(windows * microseconds * 1e9), bytes_accessed=0, transcendentals=0
    )


def dot(left, right, dims=(((1,), (0,)), ((), ()))):
    return lax.dot_general(left, right, dims, preferred_element_type=F32)


def normalize(values):
    average = jnp.mean(values, axis=-1, keepdims=True)
    centred = values - average
    rate = lax.rsqrt(jnp.mean(centred * centred, axis=-1, keepdims=True) + EPSILON)
    return centred * rate, rate


def row_sum(values):
    return jnp.sum(values, axis=0, keepdims=True)


def split_three(values):
    high = values.astype(BF16)
    rest = values - high.astype(F32)
    middle = rest.astype(BF16)
    low = (rest - middle.astype(F32)).astype(BF16)
    return high, middle, low


def square(ref, first):
    return ref[:, first : first + ROWS, :].reshape(D, D)


def grid_spec(shape):
    row_blocks, col_blocks = shape[1] // WH, shape[2] // WW
    per_clip = row_blocks * col_blocks
    return pl.BlockSpec(
        (1, WH, WW, WT, D),
        lambda i: (i // per_clip, (i % per_clip) // col_blocks, i % col_blocks, 0, 0),
    )


def window_spec(*tail):
    return pl.BlockSpec((1,) + tail, lambda i: (i,) + (0,) * len(tail))


def whole_spec(*shape):
    return pl.BlockSpec(shape, lambda i: (0,) * len(shape), pipeline_mode=pl.Buffered(1))


def pack_spec(rows, index):
    return pl.BlockSpec(
        (PACKS, rows, D), lambda i: (0, index, 0), pipeline_mode=pl.Buffered(1)
    )


def head_lanes(which):
    lane = lax.broadcasted_iota(jnp.int32, (1, 128), 1)
    return (lane // HD) == which


def lane_slice(group, base=0):
    return pl.ds(pl.multiple_of(base + group * 128, 128), 128)


def neighbour():
    return (lax.axis_index("batch"), 1 - lax.axis_index("seq"))


def piece_places(forth, block):
    if forth:
        return ((0, 3, lax.rem(7 * block + 11, 14)), (3, 4, 7 * block))
    return ((0, 4, 7 * block + 3), (4, 3, lax.rem(7 * block + 7, 14)))


def window_copies(forth, step, slot, stage, out_ref, own_sem, send_sem, recv_sem):
    clip, row_block, col_block = step // 4, (step // 2) % 2, step % 2
    kept, kept_to, sent, sent_to = (4, 0, 0, 4) if forth else (0, 4, 4, 0)
    copies = []
    number = 0
    for row, rows, row_to in piece_places(forth, row_block):
        for col, cols, col_to in piece_places(forth, col_block):

            def place(frame, row_to=row_to, rows=rows, col_to=col_to, cols=cols):
                return out_ref.at[
                    clip, pl.ds(row_to, rows), pl.ds(col_to, cols), pl.ds(frame, 4), :
                ]

            def held(frame, row=row, rows=rows, col=col, cols=cols):
                return stage.at[
                    slot, pl.ds(row, rows), pl.ds(col, cols), pl.ds(frame, 4), :
                ]

            copies.append(
                pltpu.make_async_copy(held(kept), place(kept_to), own_sem.at[slot, number])
            )
            copies.append(
                pltpu.make_async_remote_copy(
                    src_ref=held(sent),
                    dst_ref=place(sent_to),
                    send_sem=send_sem.at[slot, number],
                    recv_sem=recv_sem,
                    device_id=neighbour(),
                    device_id_type=pl.DeviceIdType.MESH,
                )
            )
            number += 1
    return copies


def wait_left(copies):
    for number, copy in enumerate(copies):
        if number % 2 == 0:
            copy.wait()
        else:
            copy.wait_send()


def push_begin():
    @pl.when(pl.program_id(0) == 0)
    def _():
        barrier = pltpu.get_barrier_semaphore()
        pl.semaphore_signal(
            barrier, inc=1, device_id=neighbour(), device_id_type=pl.DeviceIdType.MESH
        )
        pl.semaphore_wait(barrier, 1)


def push_window(forth, value, out_ref, stage, own_sem, send_sem, recv_sem):
    step = pl.program_id(0)
    slot = lax.rem(step, 2)
    rest = (stage, out_ref, own_sem, send_sem, recv_sem)

    @pl.when(step >= 2)
    def _():
        wait_left(window_copies(forth, step - 2, slot, *rest))

    stage[slot] = value.reshape(WH, WW, WT, D)
    for copy in window_copies(forth, step, slot, *rest):
        copy.start()

    @pl.when(step == pl.num_programs(0) - 1)
    def _():
        wait_left(window_copies(forth, step - 1, 1 - slot, *rest))
        wait_left(window_copies(forth, step, slot, *rest))
        half = out_ref.at[:, :, :, pl.ds(4 if forth else 0, 4), :]
        pltpu.make_async_copy(half, half, recv_sem).wait()


def push_scratch():
    return [
        pltpu.VMEM((2, WH, WW, WT, D), F32),
        pltpu.SemaphoreType.DMA((2, 4)),
        pltpu.SemaphoreType.DMA((2, 4)),
        pltpu.SemaphoreType.DMA,
    ]


def gelu_parts(hidden):
    cumulative = 0.5 + 0.5 * lax.erf(hidden * (0.5**0.5))
    density = jnp.exp(-0.5 * hidden * hidden) * 0.3989422804014327
    return hidden * cumulative, cumulative + hidden * density


def block_forward(masked, pushed, forth, *refs):
    x_ref, w_ref, up_ref, down_ref, vec_ref, bias_ref = refs[:6]
    refs = refs[6:]
    if masked:
        augq_ref, augk_ref = refs[:2]
        refs = refs[2:]
    qkv_ref, soft_ref, rate_ref, att_ref, mid_ref, act_ref, slope_ref, out_ref = refs[:8]
    vt_s, ot_s = refs[8:10]
    push = refs[10:]
    if pushed:
        push_begin()
    x = x_ref[0].astype(F32).reshape(WIN, D)
    normed = (normalize(x)[0] * vec_ref[0:1] + vec_ref[1:2]).astype(BF16)
    query = (dot(normed, square(w_ref, 0)) + vec_ref[2:3]) * (SCALE * LOG2E)
    qkv_ref[0, :, 0:D] = query.astype(BF16)
    qkv_ref[0, :, D : 2 * D] = dot(normed, square(w_ref, ROWS)).astype(BF16)
    values = dot(normed, square(w_ref, 2 * ROWS)) + vec_ref[3:4]
    qkv_ref[0, :, 2 * D :] = values.astype(BF16)
    vt_s[...] = jnp.transpose(values).astype(BF16)

    def group(g, carry):
        query4 = qkv_ref[0, :, lane_slice(g)]
        keys4 = qkv_ref[0, :, lane_slice(g, D)]
        if masked:
            query4 = jnp.concatenate([query4, augq_ref[0]], axis=1)
        for which in range(4):
            head = g * 4 + which
            keys = jnp.where(head_lanes(which), keys4, jnp.zeros_like(keys4))
            if masked:
                keys = jnp.concatenate([keys, augk_ref[0]], axis=1)
            total = dot(keys, query4, NT) + bias_ref[head]
            peak = jnp.max(total, axis=0, keepdims=True)
            soft = jnp.exp2(total - peak).astype(BF16)
            soft_ref[0, head] = soft
            rows = pl.ds(pl.multiple_of(head * HD, HD), HD)
            left = jnp.concatenate([vt_s[rows, :], jnp.ones((16, WIN), BF16)], axis=0)
            joined = dot(left, soft)
            rate = 1.0 / joined[HD : HD + 1]
            rate_ref[0, pl.ds(head, 1), :] = rate
            ot_s[rows, :] = joined[:HD] * rate
        return carry

    lax.fori_loop(0, 4, group, 0)
    attended = jnp.transpose(ot_s[...]).astype(BF16)
    att_ref[0] = attended
    middle = x_ref[0].astype(F32).reshape(WIN, D)
    middle = middle + dot(attended, square(w_ref, 3 * ROWS)) + vec_ref[4:5]
    mid_ref[0] = middle
    normed = (normalize(middle)[0] * vec_ref[5:6] + vec_ref[6:7]).astype(BF16)
    total = middle + vec_ref[7:8]
    for part in range(4):
        lanes = slice(part * D, (part + 1) * D)
        hidden = dot(normed, square(up_ref, part * ROWS)) + vec_ref[8 + part : 9 + part]
        active, slope = gelu_parts(hidden)
        active = active.astype(BF16)
        act_ref[0, :, lanes] = active
        slope_ref[0, :, lanes] = slope.astype(BF16)
        down = down_ref[part * 8 : part * 8 + 8].reshape(D, D)
        total = total + dot(active, down)
    if pushed:
        push_window(forth, total, out_ref, *push)
    else:
        out_ref[0] = total.reshape(WH, WW, WT, D).astype(out_ref.dtype)


def run_block_forward(layer, x, pack, vec, bias, aug, dtype, pushed):
    windows = x.shape[0] * (x.shape[1] // WH) * (x.shape[2] // WW)
    masked = aug is not None
    extra = list(aug) if masked else []
    return pl.pallas_call(
        functools.partial(block_forward, masked, pushed, layer == 0),
        grid=(windows,),
        in_specs=[
            grid_spec(x.shape),
            pack_spec(64, 3 * layer),
            pack_spec(64, 3 * layer + 1),
            pack_spec(64, 3 * layer + 2),
            whole_spec(12, D),
            whole_spec(HEADS, WIN, WIN),
        ]
        + [window_spec(WIN, 128)] * len(extra),
        out_specs=[
            window_spec(WIN, 3 * D),
            window_spec(HEADS, WIN, WIN),
            window_spec(HEADS, WIN),
            window_spec(WIN, D),
            window_spec(WIN, D),
            window_spec(WIN, FF),
            window_spec(WIN, FF),
            pl.BlockSpec(memory_space=pl.ANY) if pushed else grid_spec(x.shape),
        ],
        out_shape=[
            jax.ShapeDtypeStruct((windows, WIN, 3 * D), BF16),
            jax.ShapeDtypeStruct((windows, HEADS, WIN, WIN), BF16),
            jax.ShapeDtypeStruct((windows, HEADS, WIN), F32),
            jax.ShapeDtypeStruct((windows, WIN, D), BF16),
            jax.ShapeDtypeStruct((windows, WIN, D), F32),
            jax.ShapeDtypeStruct((windows, WIN, FF), BF16),
            jax.ShapeDtypeStruct((windows, WIN, FF), BF16),
            jax.ShapeDtypeStruct(x.shape, dtype),
        ],
        scratch_shapes=[pltpu.VMEM((D, WIN), BF16), pltpu.VMEM((D, WIN), F32)]
        + (push_scratch() if pushed else []),
        cost_estimate=cost(windows, 13),
        compiler_params=params(2 + layer if pushed else None),
    )(x, pack, pack, pack, vec, bias, *extra)


def norm_back(normal, rate, gained):
    first = jnp.mean(gained, axis=-1, keepdims=True)
    second = jnp.mean(gained * normal, axis=-1, keepdims=True)
    return (gained - first - normal * second) * rate


def feed_backward(
    grad_ref, act_ref, slope_ref, mid_ref, att_ref, in_ref, up_ref, down_ref, vec_ref,
    gmid_ref, gatt_ref, result_ref, gvec_ref, pack_ref,
):
    @pl.when(pl.program_id(0) == 0)
    def _():
        pack_ref[...] = jnp.zeros_like(pack_ref)
        gvec_ref[...] = jnp.zeros_like(gvec_ref)

    grad = grad_ref[0].astype(F32).reshape(WIN, D)
    gvec_ref[3:4] += row_sum(grad)
    grad_low = grad.astype(BF16)
    normal, rate = normalize(mid_ref[0])
    normed = (normal * vec_ref[5:6] + vec_ref[6:7]).astype(BF16)
    gnormed = jnp.zeros((WIN, D), F32)
    for part in range(4):
        lanes = slice(part * D, (part + 1) * D)
        active = act_ref[0, :, lanes]
        pack_ref[part * 8 : part * 8 + 8, 80:144, :] += dot(active, grad_low, TN).reshape(8, 64, D)
        down = down_ref[part * 8 : part * 8 + 8].reshape(D, D)
        ghidden = dot(grad_low, down, NT) * slope_ref[0, :, lanes].astype(F32)
        gvec_ref[4 + part : 5 + part] += row_sum(ghidden)
        ghidden = ghidden.astype(BF16)
        first = ROWS * (1 + part)
        pack_ref[:, first : first + ROWS, :] += dot(normed, ghidden, TN).reshape(PACKS, ROWS, D)
        gnormed = gnormed + dot(ghidden, square(up_ref, part * ROWS), NT)
    gvec_ref[1:2] += row_sum(gnormed * normal)
    gvec_ref[2:3] += row_sum(gnormed)
    gmid = grad + norm_back(normal, rate, gnormed * vec_ref[5:6])
    gmid_ref[0] = gmid
    gvec_ref[0:1] += row_sum(gmid)
    gmid_low = gmid.astype(BF16)
    pack_ref[:, 0:ROWS, :] += dot(att_ref[0], gmid_low, TN).reshape(PACKS, ROWS, D)
    gatt_ref[0] = dot(gmid_low, square(in_ref, 3 * ROWS), NT).astype(BF16)

    @pl.when(pl.program_id(0) == pl.num_programs(0) - 1)
    def _():
        result_ref[...] = pack_ref[...].astype(result_ref.dtype)


def run_feed_backward(layer, grad, active, slope, middle, attended, pack, vec, dtype):
    windows = middle.shape[0]
    return pl.pallas_call(
        feed_backward,
        grid=(windows,),
        in_specs=[
            grid_spec(grad.shape),
            window_spec(WIN, FF),
            window_spec(WIN, FF),
            window_spec(WIN, D),
            window_spec(WIN, D),
            pack_spec(64, 3 * layer),
            pack_spec(64, 3 * layer + 1),
            pack_spec(64, 3 * layer + 2),
            whole_spec(12, D),
        ],
        out_specs=[
            window_spec(WIN, D),
            window_spec(WIN, D),
            whole_spec(PACKS, 144, D),
            pl.BlockSpec((8, D), lambda i: (0, 0)),
        ],
        out_shape=[
            jax.ShapeDtypeStruct((windows, WIN, D), F32),
            jax.ShapeDtypeStruct((windows, WIN, D), BF16),
            jax.ShapeDtypeStruct((PACKS, 192, D), dtype),
            jax.ShapeDtypeStruct((8, D), F32),
        ],
        scratch_shapes=[pltpu.VMEM((PACKS, 144, D), F32)],
        cost_estimate=cost(windows, 7),
        compiler_params=params(),
    )(grad, active, slope, middle, attended, pack, pack, pack, vec)


def attention_backward(
    pushed,
    whole_ref, x_ref, gatt_ref, att_ref, rate_ref, soft_ref, qkv_ref, gmid_ref, in_ref, vec_ref,
    out_ref, result_ref, gvec_ref, table_ref,
    pack_ref, sum_s, kt_s, qt_s, do_s, gk_s, gv_s, wide_s, *push,
):
    step = pl.program_id(0)
    if pushed:
        push_begin()

    @pl.when(step == 0)
    def _():
        sum_s[...] = jnp.zeros_like(sum_s)
        pack_ref[...] = jnp.zeros_like(pack_ref)
        gvec_ref[...] = jnp.zeros_like(gvec_ref)

    lane = lax.broadcasted_iota(jnp.int32, (1, 128), 1)
    head_row = lax.broadcasted_iota(jnp.int32, (3 * HEADS, D), 0) % HEADS
    head_col = lax.broadcasted_iota(jnp.int32, (3 * HEADS, D), 1) // HD
    spread = jnp.where(head_row == head_col, 1.0, 0.0).astype(BF16)
    rates = jnp.concatenate(split_three(rate_ref[0]), axis=0)
    scaled = (gatt_ref[0].astype(F32) * dot(rates, spread, TN)).astype(BF16)
    do_s[...] = scaled
    product = scaled.astype(F32) * att_ref[0].astype(F32)
    gather_row = lax.broadcasted_iota(jnp.int32, (D, 128), 0) // HD
    gather_col = lax.broadcasted_iota(jnp.int32, (D, 128), 1)
    gather = jnp.where(
        (gather_row == gather_col % HEADS) & (gather_col < 3 * HEADS), 1.0, 0.0
    ).astype(BF16)
    high = product.astype(BF16)
    low = (product - high.astype(F32)).astype(BF16)
    inner = dot(high, gather) + dot(low, gather)
    first, second, third = split_three(inner)
    inner = jnp.where(lane < HEADS, first, jnp.where(lane < 2 * HEADS, second, third))
    kt_s[...] = jnp.transpose(qkv_ref[0, :, D : 2 * D].astype(F32)).astype(BF16)

    def group(g, carry):
        query4 = qkv_ref[0, :, lane_slice(g)]
        values4 = qkv_ref[0, :, lane_slice(g, 2 * D)]
        grad4 = do_s[:, lane_slice(g)]
        right = jnp.concatenate([grad4, inner], axis=1)
        zero = jnp.zeros_like(grad4)
        gvalues = jnp.zeros((WIN, 128), F32)
        gkeys = jnp.zeros((WIN, 128), F32)
        for which in range(4):
            head = g * 4 + which
            mine = head_lanes(which)
            minus = jnp.where((lane % HEADS == head) & (lane < 3 * HEADS), -1.0, 0.0)
            minus = jnp.broadcast_to(minus, (WIN, 128)).astype(BF16)
            left = jnp.concatenate([jnp.where(mine, values4, zero), minus], axis=1)
            soft = soft_ref[0, head]
            gtotal = soft.astype(F32) * dot(left, right, NT)
            sum_s[head] += gtotal
            gtotal = gtotal.astype(BF16)
            gvalues = gvalues + dot(soft, jnp.where(mine, grad4, zero))
            gkeys = gkeys + dot(gtotal, jnp.where(mine, query4, zero))
            rows = pl.ds(pl.multiple_of(head * HD, HD), HD)
            qt_s[rows, :] = dot(kt_s[rows, :], gtotal)
        gv_s[:, lane_slice(g)] = gvalues.astype(BF16)
        gk_s[:, lane_slice(g)] = (gkeys * LN2).astype(BF16)
        return carry

    lax.fori_loop(0, 4, group, 0)
    gquery = jnp.transpose(qt_s[...]).astype(BF16)
    gkeys = gk_s[...]
    gvalues = gv_s[...]
    normal, rate = normalize(x_ref[0].astype(F32).reshape(WIN, D))
    normed = (normal * vec_ref[0:1] + vec_ref[1:2]).astype(BF16)
    pack_ref[:, 0:ROWS, :] += (dot(normed, gquery, TN) * SCALE).reshape(PACKS, ROWS, D)
    pack_ref[:, ROWS : 2 * ROWS, :] += dot(normed, gkeys, TN).reshape(PACKS, ROWS, D)
    pack_ref[:, 2 * ROWS :, :] += dot(normed, gvalues, TN).reshape(PACKS, ROWS, D)
    gvec_ref[2:3] += row_sum(gquery.astype(F32)) * SCALE
    gvec_ref[3:4] += row_sum(gvalues.astype(F32))
    gnormed = (
        dot(gquery, square(in_ref, 0), NT) * SCALE
        + dot(gkeys, square(in_ref, ROWS), NT)
        + dot(gvalues, square(in_ref, 2 * ROWS), NT)
    )
    gvec_ref[0:1] += row_sum(gnormed * normal)
    gvec_ref[1:2] += row_sum(gnormed)
    grad = gmid_ref[0] + norm_back(normal, rate, gnormed * vec_ref[0:1])
    if pushed:
        push_window(False, grad, out_ref, *push)
    else:
        out_ref[0] = grad.reshape(WH, WW, WT, D).astype(out_ref.dtype)

    @pl.when(step == pl.num_programs(0) - 1)
    def _():
        result_ref[...] = pack_ref[...].astype(result_ref.dtype)
        table_ref[...] = jnp.zeros_like(table_ref)
        for col in range(WW):
            wide_s[...] = jnp.zeros_like(wide_s)
            for row in range(WH):
                place = (row * WW + col) * WT
                low_lane = (WH - 1 - row) * WW * WT
                wide_s[:, low_lane : low_lane + WIN] += sum_s[:, place : place + WT, :].reshape(
                    HEADS * WT, WIN
                )
            for shift in range(2 * WH - 1):
                low_lane = (shift * (2 * WW - 1) + WW - 1 - col) * WT
                table_ref[:, low_lane : low_lane + WW * WT] += wide_s[
                    :, shift * WW * WT : (shift + 1) * WW * WT
                ]


def run_attention_backward(
    layer, whole, x, gattended, attended, rates, soft, qkv, gmiddle, pack, vec, dtype, pack_dtype, pushed
):
    windows = gmiddle.shape[0]
    return pl.pallas_call(
        functools.partial(attention_backward, pushed),
        grid=(windows,),
        in_specs=[
            pl.BlockSpec(memory_space=pl.ANY),
            grid_spec(x.shape),
            window_spec(WIN, D),
            window_spec(WIN, D),
            window_spec(HEADS, WIN),
            window_spec(HEADS, WIN, WIN),
            window_spec(WIN, 3 * D),
            window_spec(WIN, D),
            pack_spec(64, 3 * layer),
            whole_spec(12, D),
        ],
        out_specs=[
            pl.BlockSpec(memory_space=pl.ANY) if pushed else grid_spec(x.shape),
            pack_spec(48, 3),
            pl.BlockSpec((4, D), lambda i: (0, 0)),
            pl.BlockSpec((HEADS * WT, CELLS * WT), lambda i: (0, 0)),
        ],
        out_shape=[
            jax.ShapeDtypeStruct(x.shape, dtype),
            jax.ShapeDtypeStruct((PACKS, 192, D), pack_dtype),
            jax.ShapeDtypeStruct((4, D), F32),
            jax.ShapeDtypeStruct((HEADS * WT, CELLS * WT), F32),
        ],
        scratch_shapes=[
            pltpu.VMEM((PACKS, 48, D), F32),
            pltpu.VMEM((HEADS, WIN, WIN), F32),
            pltpu.VMEM((D, WIN), BF16),
            pltpu.VMEM((D, WIN), F32),
            pltpu.VMEM((WIN, D), BF16),
            pltpu.VMEM((WIN, D), BF16),
            pltpu.VMEM((WIN, D), BF16),
            pltpu.VMEM((HEADS * WT, (2 * WH - 1) * WW * WT), F32),
        ]
        + (push_scratch() if pushed else []),
        cost_estimate=cost(windows, 12),
        compiler_params=params(4 if pushed else None),
        input_output_aliases={0: 1},
    )(whole, x, gattended, attended, rates, soft, qkv, gmiddle, pack, vec)


def expand_bias(cells_ref, out_ref, wide_s):
    for col in range(WW):
        for shift in range(2 * WH - 1):
            low_lane = (shift * (2 * WW - 1) + WW - 1 - col) * WT
            wide_s[:, shift * WW * WT : (shift + 1) * WW * WT] = cells_ref[
                :, low_lane : low_lane + WW * WT
            ]
        for row in range(WH):
            place = (row * WW + col) * WT
            low_lane = (WH - 1 - row) * WW * WT
            out_ref[:, place : place + WT, :] = wide_s[:, low_lane : low_lane + WIN].reshape(
                HEADS, WT, WIN
            )


def run_expand_bias(cells):
    return pl.pallas_call(
        expand_bias,
        out_shape=jax.ShapeDtypeStruct((HEADS, WIN, WIN), F32),
        scratch_shapes=[pltpu.VMEM((HEADS * WT, (2 * WH - 1) * WW * WT), F32)],
        compiler_params=pltpu.CompilerParams(vmem_limit_bytes=61 * 1024 * 1024),
    )(cells)


AUX_ROWS = 8
SHARES = ((0, 0, 96, 0), (0, 96, 96, 1), (1, 0, AUX_ROWS, 0))


def fold_gradients(*refs):
    operands = refs[:2]
    pack_out, aux_out = refs[2:4]
    buffers = refs[4:13]
    send_sem, recv_sem, wide_send, wide_recv = refs[13:]
    batch = lax.axis_index("batch")
    y = lax.axis_index("seq")
    z, x, core = batch // 4, (batch // 2) % 2, batch % 2
    count = len(SHARES)

    def device(z_to, x_to, core_to, y_to):
        return ((z_to * 2 + x_to) * 2 + core_to, y_to)

    barrier = pltpu.get_barrier_semaphore()

    def greet(k, carry):
        other = lax.rem(batch * 2 + y + k, 32)
        pl.semaphore_signal(
            barrier, inc=1, device_id=(other // 2, other % 2), device_id_type=pl.DeviceIdType.MESH
        )
        return carry

    lax.fori_loop(1, 32, greet, 0)
    pl.semaphore_wait(barrier, 31)

    def send(number, source, target, to):
        copy = pltpu.make_async_remote_copy(
            src_ref=source,
            dst_ref=target,
            send_sem=send_sem.at[number],
            recv_sem=recv_sem.at[number],
            device_id=to,
            device_id_type=pl.DeviceIdType.MESH,
        )
        copy.start()
        return copy

    copies = []
    for k, (which, first, size, order) in enumerate(SHARES):
        source = operands[which].at[:, :, 1 - core, :, pl.ds(first, size), :]
        copies.append(send(k, source, buffers[3 * k], device(z, x, 1 - core, y)))
    for k, (which, first, size, order) in enumerate(SHARES):
        copies[k].wait()
        held = buffers[3 * k]

        def add_core(i, carry, which=which, first=first, size=size, held=held):
            a, b = i // 2, i % 2
            mine = operands[which][a, b, core, :, first : first + size, :].astype(F32)
            held[a, b] = (held[a, b].astype(F32) + mine).astype(held.dtype)
            return carry

        lax.fori_loop(0, 8, add_core, 0)
        if order == 0:
            copies.append(send(count + k, held.at[:, 1 - x], buffers[3 * k + 1], device(z, 1 - x, core, y)))
        else:
            copies.append(send(count + k, held.at[:, :, 1 - y], buffers[3 * k + 1], device(z, x, core, 1 - y)))
    for k, (which, first, size, order) in enumerate(SHARES):
        copies[count + k].wait()
        before, held = buffers[3 * k], buffers[3 * k + 1]

        def add_next(i, carry, order=order, before=before, held=held):
            a, b = i // 2, i % 2
            mine = before[a, x, b] if order == 0 else before[a, b, y]
            held[a, b] = (held[a, b].astype(F32) + mine.astype(F32)).astype(held.dtype)
            return carry

        lax.fori_loop(0, 8, add_next, 0)
        if order == 0:
            copies.append(send(2 * count + k, held.at[:, 1 - y], buffers[3 * k + 2].at[pl.ds(0, 4)], device(z, x, core, 1 - y)))
        else:
            copies.append(send(2 * count + k, held.at[:, 1 - x], buffers[3 * k + 2].at[pl.ds(0, 4)], device(z, 1 - x, core, y)))
    far = []
    for k, (which, first, size, order) in enumerate(SHARES):
        copies[2 * count + k].wait()
        before, held = buffers[3 * k + 1], buffers[3 * k + 2]

        def add_last(a, carry, order=order, before=before, held=held):
            mine = before[a, y] if order == 0 else before[a, x]
            held[a] = (held[a].astype(F32) + mine.astype(F32)).astype(held.dtype)
            return carry

        lax.fori_loop(0, 4, add_last, 0)
        for step in range(1, 4):
            other = lax.rem(z + step, 4)
            far.append(
                send(
                    3 * count + 3 * k + step - 1,
                    held.at[other],
                    held.at[3 + step],
                    device(other, x, core, y),
                )
            )
    for k, (which, first, size, order) in enumerate(SHARES):
        for step in range(1, 4):
            far[3 * k + step - 1].wait()
        held = buffers[3 * k + 2]
        total = held[z].astype(F32) + held[4].astype(F32)
        total = total + held[5].astype(F32) + held[6].astype(F32)
        if which == 0:
            pack_out[first : first + size, :] = total
        else:
            aux_out[batch * 2 + y] = total

    def spread(k, carry):
        other = lax.rem(batch * 2 + y + k, 32)
        pltpu.make_async_remote_copy(
            src_ref=aux_out.at[batch * 2 + y],
            dst_ref=aux_out.at[batch * 2 + y],
            send_sem=wide_send,
            recv_sem=wide_recv,
            device_id=(other // 2, other % 2),
            device_id_type=pl.DeviceIdType.MESH,
        ).start()
        return carry

    lax.fori_loop(1, 32, spread, 0)
    others = aux_out.at[pl.ds(0, 31)]
    pltpu.make_async_copy(others, others, wide_send).wait()
    pltpu.make_async_copy(others, others, wide_recv).wait()


def run_fold_gradients(big, aux):
    operands = [value.reshape((4, 2, 2, 2) + value.shape[1:]) for value in (big, aux)]
    scratch = []
    for which, first, size, order in SHARES:
        dtype = operands[which].dtype
        scratch.append(pltpu.VMEM((4, 2, 2, size, D), dtype))
        scratch.append(pltpu.VMEM((4, 2, size, D), dtype))
        scratch.append(pltpu.VMEM((7, size, D), dtype))
    semaphores = 6 * len(SHARES)
    return pl.pallas_call(
        fold_gradients,
        in_specs=[pl.BlockSpec(memory_space=pltpu.VMEM)] * 2,
        out_specs=[pl.BlockSpec(memory_space=pltpu.VMEM)] * 2,
        out_shape=[
            jax.ShapeDtypeStruct((192, D), F32),
            jax.ShapeDtypeStruct((32, AUX_ROWS, D), F32),
        ],
        scratch_shapes=scratch
        + [
            pltpu.SemaphoreType.DMA((semaphores,)),
            pltpu.SemaphoreType.DMA((semaphores,)),
            pltpu.SemaphoreType.DMA,
            pltpu.SemaphoreType.DMA,
        ],
        compiler_params=pltpu.CompilerParams(
            vmem_limit_bytes=61 * 1024 * 1024, collective_id=1, has_side_effects=True
        ),
    )(*operands)


def offset_places():
    frame, row, col = np.meshgrid(
        np.arange(1 - WT, WT), np.arange(1 - WH, WH), np.arange(1 - WW, WW), indexing="ij"
    )

    def place(f, r, c):
        return (np.maximum(f, 0) * WH + np.maximum(r, 0)) * WW + np.maximum(c, 0)

    return (place(frame, row, col) * WIN + place(-frame, -row, -col)).reshape(-1)


def interleave():
    cell = np.arange(CELLS * WT)
    source = jnp.asarray((cell % WT) * CELLS + cell // WT, jnp.int32)
    order = jnp.arange(CELLS * WT, dtype=jnp.int32)
    return (order[:, None] == source[None, :]).astype(BF16)


def join_three(values, axis):
    first, second, third = jnp.split(values, 3, axis=axis)
    return first + second + third


def bias_cells(tables, chosen, order):
    flat = jnp.concatenate([tables[layer] for layer in range(LAYERS)], axis=1) * LOG2E
    pieces = jnp.concatenate(split_three(flat), axis=1)
    taken = dot(pieces, chosen, (((0,), (1,)), ((), ()))).astype(BF16)
    placed = jnp.stack(
        [taken[:, (WT - 1 - t) * CELLS : (2 * WT - 1 - t) * CELLS] for t in range(WT)], axis=1
    )
    cells = dot(placed.reshape(-1, WT * CELLS), order)
    return join_three(cells, 0).reshape(LAYERS, HEADS * WT, CELLS * WT)


def cells_to_rows(cells, order):
    pieces = jnp.concatenate(split_three(cells.reshape(-1, CELLS * WT)), axis=0)
    placed = join_three(dot(pieces, order, NT), 0).reshape(LAYERS * HEADS, WT, CELLS * WT)
    parts = [
        jnp.pad(placed[:, t], ((0, 0), ((WT - 1 - t) * CELLS, t * CELLS))) for t in range(WT)
    ]
    return functools.reduce(jnp.add, parts)


def rows_to_table(rows, chosen):
    pieces = jnp.concatenate(split_three(rows), axis=0)
    total = join_three(dot(chosen, pieces, (((0,), (1,)), ((), ()))), 1)
    return jnp.stack([total[:, i * HEADS : (i + 1) * HEADS] for i in range(LAYERS)])


def spatial_blocks(field):
    clip_count, frames_here, width = (field.shape[0], field.shape[1], field.shape[-1])
    shaped = field.reshape(clip_count, frames_here, HGT // WH, WH, WID // WW, WW, width)
    shaped = shaped.transpose(0, 2, 4, 1, 3, 5, 6)
    return shaped.reshape(clip_count * (HGT // WH) * (WID // WW), frames_here, WH * WW, width)


def roll_space(field, amount, first):
    return jnp.roll(field, (amount, amount), axis=(first, first + 1))


def swap_halves(part):
    return lax.ppermute(part, "seq", [(0, 1), (1, 0)])


class Placement:
    def __init__(self, clip_count, frames_here):
        self.clips = clip_count
        self.frames = frames_here
        self.parts = lax.axis_size("seq")
        self.near = self.parts == 2 and frames_here == WT

    def grid_shape(self):
        if self.near:
            return (self.clips, HGT, WID, WT, D)
        columns = self.clips * 4 // self.parts
        return (columns * 2, WH, WW, WT, D)

    def enter(self, field, shifted):
        if self.near:
            if shifted:
                arrived = swap_halves(field[:, :SHIFT_T])
                field = jnp.concatenate([field[:, SHIFT_T:], arrived], axis=1)
                field = roll_space(field, -SHIFT_S, 2)
            return field.transpose(0, 2, 3, 1, 4)
        if shifted:
            field = roll_space(field, -SHIFT_S, 2)
        columns = lax.all_to_all(
            spatial_blocks(field), "seq", split_axis=0, concat_axis=1, tiled=True
        )
        if shifted:
            columns = jnp.roll(columns, -SHIFT_T, axis=1)
        windows = columns.reshape(-1, WT, WH, WW, D)
        return windows.transpose(0, 2, 3, 1, 4)

    def leave(self, grid, shifted):
        if self.near:
            field = grid.transpose(0, 3, 1, 2, 4)
            if shifted:
                field = roll_space(field, SHIFT_S, 2)
                arrived = swap_halves(field[:, SHIFT_T:])
                field = jnp.concatenate([arrived, field[:, :SHIFT_T]], axis=1)
            return field
        columns = grid.transpose(0, 3, 1, 2, 4).reshape(-1, FRAMES, WH * WW, D)
        if shifted:
            columns = jnp.roll(columns, SHIFT_T, axis=1)
        columns = lax.all_to_all(columns, "seq", split_axis=1, concat_axis=0, tiled=True)
        shaped = columns.reshape(self.clips, HGT // WH, WID // WW, self.frames, WH, WW, D)
        shaped = shaped.transpose(0, 3, 1, 4, 2, 5, 6)
        field = shaped.reshape(self.clips, self.frames, HGT, WID, D)
        return roll_space(field, SHIFT_S, 2) if shifted else field

    def forth(self, grid):
        return self.enter(self.leave(grid, False), True)

    def back(self, grid):
        return self.enter(self.leave(grid, True), False)

    def mask_lanes(self):
        if self.near:
            index = jnp.arange(self.clips * 4, dtype=jnp.int32)
            late = jnp.full(index.shape, lax.axis_index("seq"), jnp.int32)
            block = index % 4
        else:
            columns = self.clips * 4 // self.parts
            index = jnp.arange(columns * 2, dtype=jnp.int32)
            late = index % 2
            block = (lax.axis_index("seq") * columns + index // 2) % 4
        place = np.arange(WIN)
        frame_late = jnp.asarray(place % WT >= WT - SHIFT_T).astype(jnp.int32)
        row_late = jnp.asarray(place // (WT * WW) >= WH - SHIFT_S).astype(jnp.int32)
        col_late = jnp.asarray(place // WT % WW >= WW - SHIFT_S).astype(jnp.int32)
        region = (
            late[:, None] * frame_late * 4
            + (block // 2)[:, None] * row_late * 2
            + (block % 2)[:, None] * col_late
        )
        lane = np.arange(128)
        same = (region[:, :, None] == lane % 8) & (lane < 24)
        pieces = []
        rest = np.float32(MASKED * LOG2E)
        for _ in range(3):
            piece = np.float32(np.asarray(rest).astype(BF16))
            pieces.append(piece)
            rest = np.float32(rest - piece)
        piece_of = np.zeros((128,), np.float32)
        for number, piece in enumerate(pieces):
            piece_of[8 * number : 8 * number + 8] = -piece
            piece_of[24 + number] = piece
        always = (lane >= 24) & (lane < 27)
        on_keys = jnp.where(same | always, 1.0, 0.0)
        return (on_keys * piece_of).astype(BF16), on_keys.astype(BF16)


def pack_layer(inner, outer, up, down):
    parts = [inner[:, i * D : (i + 1) * D] for i in range(3)] + [outer]
    parts = parts + [up[:, i * D : (i + 1) * D] for i in range(4)] + [down]
    return jnp.concatenate(parts, axis=0)


def per_device(
    clips_in,
    cotangent,
    offset_index,
    first_gain,
    first_shift,
    inner_weight,
    inner_bias,
    outer_weight,
    outer_bias,
    second_gain,
    second_shift,
    up_weight,
    up_bias,
    down_weight,
    down_bias,
    bias_table,
):
    place = Placement(clips_in.shape[0], clips_in.shape[1])
    rows = inner_weight.shape[1]
    devices = D // rows
    vectors = [
        first_gain, first_shift, inner_bias, outer_bias, second_gain, second_shift,
        down_bias, up_bias,
    ]
    vec_pack = jnp.concatenate(vectors, axis=1)
    width = vec_pack.shape[1]
    vec_rows = jnp.pad(vec_pack, ((0, 14), (0, D - width)))
    local = [
        pack_layer(inner_weight[layer], outer_weight[layer], up_weight[layer], down_weight[layer])
        for layer in range(LAYERS)
    ]
    full = lax.all_gather(jnp.concatenate(local + [vec_rows], axis=0), AXES, axis=0)
    vecs = []
    for layer in range(LAYERS):
        held = full[:, 24 * rows + layer, :width].astype(F32)
        pieces = []
        start = 0
        for vector in vectors:
            size = vector.shape[1]
            pieces.append(held[:, start : start + size].reshape(-1, D))
            start += size
        vecs.append(jnp.concatenate(pieces, axis=0))
    if rows != ROWS:
        parts = []
        for first in (0, 12 * rows):
            for i in range(8):
                part = full[:, first + i * rows : first + (i + 1) * rows]
                parts.append(part.reshape(PACKS, ROWS, D))
            part = full[:, first + 8 * rows : first + 12 * rows]
            parts.append(part.reshape(PACKS, 4 * ROWS, D))
        full = jnp.concatenate(parts, axis=1)
    weights = [(full, vec) for vec in vecs]
    taken_rows = jnp.take(offset_index.reshape(-1), offset_places())
    order = jnp.arange(BIAS_ROWS, dtype=jnp.int32)
    chosen = (taken_rows[:, None] == order[None, :]).astype(BF16)
    interleaved = interleave()
    cells_in = bias_cells(bias_table, chosen, interleaved)
    bias = [run_expand_bias(cells_in[layer]) for layer in range(LAYERS)]
    shape = place.grid_shape()
    aug = place.mask_lanes()

    x_zero = place.enter(clips_in, False)
    upstream = place.enter(cotangent, True)
    saved = []
    x = x_zero
    for layer in range(LAYERS):
        pack, vec = weights[layer]
        qkv, soft, rates, attended, middle, active, slope, result = run_block_forward(
            layer, x, pack, vec, bias[layer], aug if layer == 1 else None,
            F32 if layer == 0 or place.near else BF16, place.near,
        )
        saved.append((x, qkv, soft, rates, attended, middle, active, slope))
        x = place.forth(result) if layer == 0 and not place.near else result
    clips_out = place.leave(x, not place.near).astype(BF16)

    scattered = [None] * LAYERS
    vec_parts = [None] * LAYERS
    cell_parts = [None] * LAYERS

    def scatter(value, blocks):
        if rows != ROWS:
            per = ROWS // rows
            parts = []
            start = 0
            for size in blocks:
                part = value[:, start : start + size].reshape(PACKS * per, size // per, D)
                parts.append(part)
                start += size
            value = jnp.concatenate(parts, axis=1)
        return lax.psum_scatter(value, AXES, scatter_dimension=0, tiled=False)

    folded = lax.axis_size("batch") == 16 and lax.axis_size("seq") == 2
    for layer in reversed(range(LAYERS)):
        pack, vec = weights[layer]
        x, qkv, soft, rates, attended, middle, active, slope = saved[layer]
        gmiddle, gattended, big, gvec_two = run_feed_backward(
            layer, upstream, active, slope, middle, attended, pack, vec, F32 if layer == 1 or not folded else BF16
        )
        upstream, big, gvec_one, cells = run_attention_backward(
            layer, big, x, gattended, attended, rates, soft, qkv, gmiddle, pack, vec,
            F32 if layer == 1 else BF16, F32 if layer == 1 or not folded else BF16,
            place.near and layer == 1,
        )
        if layer == 1 or not folded:
            scattered[layer] = scatter(big, [ROWS] * 5 + [4 * ROWS] + [ROWS] * 3)
        vec_parts[layer] = jnp.concatenate([gvec_one, gvec_two], axis=0)
        cell_parts[layer] = cells
        if layer == 1 and not place.near:
            upstream = place.back(upstream)
    clips_grad = place.leave(upstream, False)

    table_rows = cells_to_rows(jnp.stack(cell_parts), interleaved)
    vec_stack = jnp.stack(vec_parts)
    if folded:
        aux = jnp.concatenate([table_rows.reshape(-1), vec_stack.reshape(-1)])
        used = aux.shape[0]
        aux = jnp.pad(aux, (0, PACKS * AUX_ROWS * D - used)).reshape(PACKS, AUX_ROWS, D)
        scattered[0], aux = run_fold_gradients(big, aux)
        aux = aux.reshape(-1)[:used]
        table_total = aux[: table_rows.size].reshape(table_rows.shape)
        vec_total = aux[table_rows.size :].reshape(vec_stack.shape)
    else:
        vec_total, table_total = lax.psum((vec_stack, table_rows), AXES)
    table_total = rows_to_table(table_total, chosen)

    device = lax.axis_index(AXES)

    def own(first, count):
        whole = vec_total[:, first : first + count].reshape(LAYERS, count * D)
        size = count * D // devices
        return lax.dynamic_slice_in_dim(whole, device * size, size, axis=1)

    def both(first, count):
        parts = []
        for layer in range(LAYERS):
            value = scattered[layer]
            columns = [
                value[first + i * rows : first + (i + 1) * rows] for i in range(count)
            ]
            parts.append(jnp.concatenate(columns, axis=1))
        return jnp.stack(parts)

    down = jnp.stack([scattered[layer][5 * rows : 9 * rows] for layer in range(LAYERS)])
    return (
        clips_out,
        clips_grad,
        own(0, 1),
        own(1, 1),
        both(9 * rows, 3),
        own(2, 2),
        both(0, 1),
        own(4, 1),
        own(5, 1),
        own(6, 1),
        both(rows, 4),
        own(8, 4),
        down,
        own(7, 1),
        table_total,
    )


def solution(mesh):
    clips = P("batch", "seq", None, None, None)
    vector = P(None, AXES)
    matrix = P(None, AXES, None)
    return jax.shard_map(
        per_device,
        mesh=mesh,
        in_specs=(
            clips, clips, P(), vector, vector, matrix, vector, matrix, vector, vector, vector,
            matrix, vector, matrix, vector, P(),
        ),
        out_specs=(
            clips, clips, vector, vector, matrix, vector, matrix, vector, vector, vector,
            matrix, vector, matrix, vector, P(),
        ),
        check_vma=False,
    )
```

```python
import functools

import jax
import jax.numpy as jnp
import numpy as np
from jax import lax
from jax.experimental import pallas as pl
from jax.experimental.pallas import tpu as pltpu
from jax.sharding import PartitionSpec as P

D = 512
HEADS = 16
HD = 32
FF = 2048
WT = 8
WH = 7
WW = 7
FRAMES = 16
HGT = 14
WID = 14
LAYERS = 2
SHIFT_T = 4
SHIFT_S = 3
WIN = 392
BIAS_ROWS = 2535
ROWS = 16
PACKS = D // ROWS
CELLS = (2 * WH - 1) * (2 * WW - 1)

EPSILON = 1e-05
MASKED = -100.0
LOG2E = 1.4426950408889634
LN2 = 0.6931471805599453
SCALE = HD**-0.5

BF16 = jnp.bfloat16
F32 = jnp.float32
AXES = ("batch", "seq")

NT = (((1,), (1,)), ((), ()))
TN = (((0,), (0,)), ((), ()))


def params(collective=None):
    return pltpu.CompilerParams(
        vmem_limit_bytes=61 * 1024 * 1024,
        dimension_semantics=("arbitrary",),
        collective_id=collective,
        has_side_effects=collective is not None,
    )


def cost(windows, microseconds):
    return pl.CostEstimate(
        flops=int(windows * microseconds * 1e9), bytes_accessed=0, transcendentals=0
    )


def dot(left, right, dims=(((1,), (0,)), ((), ()))):
    return lax.dot_general(left, right, dims, preferred_element_type=F32)


def normalize(values):
    average = jnp.mean(values, axis=-1, keepdims=True)
    centred = values - average
    rate = lax.rsqrt(jnp.mean(centred * centred, axis=-1, keepdims=True) + EPSILON)
    return centred * rate, rate


def row_sum(values):
    return jnp.sum(values, axis=0, keepdims=True)


def split_three(values):
    high = values.astype(BF16)
    rest = values - high.astype(F32)
    middle = rest.astype(BF16)
    low = (rest - middle.astype(F32)).astype(BF16)
    return high, middle, low


def square(ref, first):
    return ref[:, first : first + ROWS, :].reshape(D, D)


def grid_spec(shape):
    row_blocks, col_blocks = shape[1] // WH, shape[2] // WW
    per_clip = row_blocks * col_blocks
    return pl.BlockSpec(
        (1, WH, WW, WT, D),
        lambda i: (i // per_clip, (i % per_clip) // col_blocks, i % col_blocks, 0, 0),
    )


def window_spec(*tail):
    return pl.BlockSpec((1,) + tail, lambda i: (i,) + (0,) * len(tail))


def whole_spec(*shape):
    return pl.BlockSpec(shape, lambda i: (0,) * len(shape), pipeline_mode=pl.Buffered(1))


def pack_spec(rows, index):
    return pl.BlockSpec(
        (PACKS, rows, D), lambda i: (0, index, 0), pipeline_mode=pl.Buffered(1)
    )


def head_lanes(which):
    lane = lax.broadcasted_iota(jnp.int32, (1, 128), 1)
    return (lane // HD) == which


def lane_slice(group, base=0):
    return pl.ds(pl.multiple_of(base + group * 128, 128), 128)


def neighbour():
    return (lax.axis_index("batch"), 1 - lax.axis_index("seq"))


def piece_places(forth, block):
    if forth:
        return ((0, 3, lax.rem(7 * block + 11, 14)), (3, 4, 7 * block))
    return ((0, 4, 7 * block + 3), (4, 3, lax.rem(7 * block + 7, 14)))


def window_copies(forth, step, slot, stage, out_ref, own_sem, send_sem, recv_sem):
    clip, row_block, col_block = step // 4, (step // 2) % 2, step % 2
    kept, kept_to, sent, sent_to = (4, 0, 0, 4) if forth else (0, 4, 4, 0)
    copies = []
    number = 0
    for row, rows, row_to in piece_places(forth, row_block):
        for col, cols, col_to in piece_places(forth, col_block):

            def place(frame, row_to=row_to, rows=rows, col_to=col_to, cols=cols):
                return out_ref.at[
                    clip, pl.ds(row_to, rows), pl.ds(col_to, cols), pl.ds(frame, 4), :
                ]

            def held(frame, row=row, rows=rows, col=col, cols=cols):
                return stage.at[
                    slot, pl.ds(row, rows), pl.ds(col, cols), pl.ds(frame, 4), :
                ]

            copies.append(
                pltpu.make_async_copy(held(kept), place(kept_to), own_sem.at[slot, number])
            )
            copies.append(
                pltpu.make_async_remote_copy(
                    src_ref=held(sent),
                    dst_ref=place(sent_to),
                    send_sem=send_sem.at[slot, number],
                    recv_sem=recv_sem,
                    device_id=neighbour(),
                    device_id_type=pl.DeviceIdType.MESH,
                )
            )
            number += 1
    return copies


def wait_left(copies):
    for number, copy in enumerate(copies):
        if number % 2 == 0:
            copy.wait()
        else:
            copy.wait_send()


def push_begin():
    @pl.when(pl.program_id(0) == 0)
    def _():
        barrier = pltpu.get_barrier_semaphore()
        pl.semaphore_signal(
            barrier, inc=1, device_id=neighbour(), device_id_type=pl.DeviceIdType.MESH
        )
        pl.semaphore_wait(barrier, 1)


def push_window(forth, value, out_ref, stage, own_sem, send_sem, recv_sem):
    step = pl.program_id(0)
    slot = lax.rem(step, 2)
    rest = (stage, out_ref, own_sem, send_sem, recv_sem)

    @pl.when(step >= 2)
    def _():
        wait_left(window_copies(forth, step - 2, slot, *rest))

    stage[slot] = value.reshape(WH, WW, WT, D)
    for copy in window_copies(forth, step, slot, *rest):
        copy.start()

    @pl.when(step == pl.num_programs(0) - 1)
    def _():
        wait_left(window_copies(forth, step - 1, 1 - slot, *rest))
        wait_left(window_copies(forth, step, slot, *rest))
        half = out_ref.at[:, :, :, pl.ds(4 if forth else 0, 4), :]
        pltpu.make_async_copy(half, half, recv_sem).wait()


def push_scratch():
    return [
        pltpu.VMEM((2, WH, WW, WT, D), F32),
        pltpu.SemaphoreType.DMA((2, 4)),
        pltpu.SemaphoreType.DMA((2, 4)),
        pltpu.SemaphoreType.DMA,
    ]


def gelu_parts(hidden):
    cumulative = 0.5 + 0.5 * lax.erf(hidden * (0.5**0.5))
    decay = jnp.exp2(hidden * hidden * (-0.5 * LOG2E))
    return hidden * cumulative, cumulative + hidden * decay * 0.3989422804014327


def block_forward(masked, pushed, forth, *refs):
    x_ref, w_ref, up_ref, down_ref, vec_ref, bias_ref = refs[:6]
    refs = refs[6:]
    if masked:
        augq_ref, augk_ref = refs[:2]
        refs = refs[2:]
    qkv_ref, soft_ref, rate_ref, att_ref, mid_ref, act_ref, slope_ref, out_ref = refs[:8]
    push = refs[8:]
    if pushed:
        push_begin()
    x = x_ref[0].astype(F32).reshape(WIN, D)
    normed = (normalize(x)[0] * vec_ref[0:1] + vec_ref[1:2]).astype(BF16)
    query = (dot(normed, square(w_ref, 0)) + vec_ref[2:3]) * (SCALE * LOG2E)
    qkv_ref[0, :, 0:D] = query.astype(BF16)
    qkv_ref[0, :, D : 2 * D] = dot(normed, square(w_ref, ROWS)).astype(BF16)
    values = dot(normed, square(w_ref, 2 * ROWS)) + vec_ref[3:4]
    qkv_ref[0, :, 2 * D :] = values.astype(BF16)

    def score(head):
        first = head // 4 * 128
        query4 = qkv_ref[0, :, first : first + 128]
        keys4 = qkv_ref[0, :, D + first : D + first + 128]
        query4 = jnp.where(head_lanes(head % 4), query4, jnp.zeros_like(query4))
        if masked:
            query4 = jnp.concatenate([query4, augq_ref[0]], axis=1)
            keys4 = jnp.concatenate([keys4, augk_ref[0]], axis=1)
        return dot(query4, keys4, NT)

    parts = [None, None]

    def finish(head, soft):
        first = head // 4 * 128
        mine = head_lanes(head % 4)
        values4 = qkv_ref[0, :, 2 * D + first : 2 * D + first + 128]
        values4 = jnp.where(mine, values4, jnp.zeros_like(values4))
        right = jnp.concatenate([values4, jnp.ones((WIN, 128), BF16)], axis=1)
        joined = dot(soft, right)
        rate = 1.0 / joined[:, 128:]
        part = joined[:, :128] * rate
        parts[0] = part if head % 4 == 0 else parts[0] + part
        parts[1] = rate if head % 4 == 0 else jnp.where(mine, rate, parts[1])
        if head % 4 == 3:
            att_ref[0, :, first : first + 128] = parts[0].astype(BF16)
            rate_ref[0, :, first : first + 128] = parts[1]

    total = score(0)
    last = None
    for head in range(HEADS):
        following = score(head + 1) if head < HEADS - 1 else None
        total = total + bias_ref[head]
        soft = jnp.exp2(total - jnp.max(total, axis=1, keepdims=True)).astype(BF16)
        soft_ref[0, head] = soft
        if head > 0:
            finish(head - 1, last)
        last = soft
        total = following
    finish(HEADS - 1, last)
    attended = att_ref[0]
    middle = x_ref[0].astype(F32).reshape(WIN, D)
    middle = middle + dot(attended, square(w_ref, 3 * ROWS)) + vec_ref[4:5]
    mid_ref[0] = middle
    normed = (normalize(middle)[0] * vec_ref[5:6] + vec_ref[6:7]).astype(BF16)
    total = middle + vec_ref[7:8]

    def raise_part(part):
        return dot(normed, square(up_ref, part * ROWS)) + vec_ref[8 + part : 9 + part]

    def lower_part(part, active):
        return dot(active, down_ref[part * 8 : part * 8 + 8].reshape(D, D))

    hidden = raise_part(0)
    last = None
    for part in range(4):
        following = raise_part(part + 1) if part < 3 else None
        lanes = slice(part * D, (part + 1) * D)
        active, slope = gelu_parts(hidden)
        active = active.astype(BF16)
        act_ref[0, :, lanes] = active
        slope_ref[0, :, lanes] = slope.astype(BF16)
        if part > 0:
            total = total + lower_part(part - 1, last)
        last = active
        hidden = following
    total = total + lower_part(3, last)
    if pushed:
        push_window(forth, total, out_ref, *push)
    else:
        out_ref[0] = total.reshape(WH, WW, WT, D).astype(out_ref.dtype)


def run_block_forward(layer, x, pack, vec, bias, aug, dtype, pushed):
    windows = x.shape[0] * (x.shape[1] // WH) * (x.shape[2] // WW)
    masked = aug is not None
    extra = list(aug) if masked else []
    return pl.pallas_call(
        functools.partial(block_forward, masked, pushed, layer == 0),
        grid=(windows,),
        in_specs=[
            grid_spec(x.shape),
            pack_spec(64, 3 * layer),
            pack_spec(64, 3 * layer + 1),
            pack_spec(64, 3 * layer + 2),
            whole_spec(12, D),
            whole_spec(HEADS, WIN, WIN),
        ]
        + [window_spec(WIN, 128)] * len(extra),
        out_specs=[
            window_spec(WIN, 3 * D),
            window_spec(HEADS, WIN, WIN),
            window_spec(WIN, D),
            window_spec(WIN, D),
            window_spec(WIN, D),
            window_spec(WIN, FF),
            window_spec(WIN, FF),
            pl.BlockSpec(memory_space=pl.ANY) if pushed else grid_spec(x.shape),
        ],
        out_shape=[
            jax.ShapeDtypeStruct((windows, WIN, 3 * D), BF16),
            jax.ShapeDtypeStruct((windows, HEADS, WIN, WIN), BF16),
            jax.ShapeDtypeStruct((windows, WIN, D), F32),
            jax.ShapeDtypeStruct((windows, WIN, D), BF16),
            jax.ShapeDtypeStruct((windows, WIN, D), F32),
            jax.ShapeDtypeStruct((windows, WIN, FF), BF16),
            jax.ShapeDtypeStruct((windows, WIN, FF), BF16),
            jax.ShapeDtypeStruct(x.shape, dtype),
        ],
        scratch_shapes=push_scratch() if pushed else [],
        cost_estimate=cost(windows, 13),
        compiler_params=params(2 + layer if pushed else None),
    )(x, pack, pack, pack, vec, bias, *extra)


def norm_back(normal, rate, gained):
    first = jnp.mean(gained, axis=-1, keepdims=True)
    second = jnp.mean(gained * normal, axis=-1, keepdims=True)
    return (gained - first - normal * second) * rate


def feed_backward(
    grad_ref, act_ref, slope_ref, mid_ref, att_ref, in_ref, up_ref, down_ref, vec_ref,
    gmid_ref, gatt_ref, result_ref, gvec_ref, pack_ref,
):
    @pl.when(pl.program_id(0) == 0)
    def _():
        pack_ref[...] = jnp.zeros_like(pack_ref)
        gvec_ref[...] = jnp.zeros_like(gvec_ref)

    count = mid_ref.shape[0]
    each = range(count)
    grads = [
        grad_ref[0, :, WW * w : WW * (w + 1)].astype(F32).reshape(WIN, D) for w in each
    ]
    gvec_ref[3:4] += sum(row_sum(grad) for grad in grads)
    lows = [grad.astype(BF16) for grad in grads]
    normals = [normalize(mid_ref[w]) for w in each]
    normed = [(normals[w][0] * vec_ref[5:6] + vec_ref[6:7]).astype(BF16) for w in each]
    gnormed = [jnp.zeros((WIN, D), F32) for w in each]

    def back_part(part):
        down = down_ref[part * 8 : part * 8 + 8].reshape(D, D)
        return [dot(lows[w], down, NT) for w in each]

    def finish(part, ghidden):
        first = ROWS * (1 + part)
        total = sum(dot(normed[w], ghidden[w], TN) for w in each)
        pack_ref[:, first : first + ROWS, :] += total.reshape(PACKS, ROWS, D)
        up = square(up_ref, part * ROWS)
        for w in each:
            gnormed[w] = gnormed[w] + dot(ghidden[w], up, NT)

    gactive = back_part(0)
    last = None
    for part in range(4):
        following = back_part(part + 1) if part < 3 else None
        lanes = slice(part * D, (part + 1) * D)
        ghidden = [gactive[w] * slope_ref[w, :, lanes].astype(F32) for w in each]
        gvec_ref[4 + part : 5 + part] += sum(row_sum(value) for value in ghidden)
        ghidden = [value.astype(BF16) for value in ghidden]
        total = sum(dot(act_ref[w, :, lanes], lows[w], TN) for w in each)
        pack_ref[part * 8 : part * 8 + 8, 80:144, :] += total.reshape(8, 64, D)
        if part > 0:
            finish(part - 1, last)
        last = ghidden
        gactive = following
    finish(3, last)
    outer = square(in_ref, 3 * ROWS)
    total = jnp.zeros((D, D), F32)
    for w in each:
        normal, rate = normals[w]
        gvec_ref[1:2] += row_sum(gnormed[w] * normal)
        gvec_ref[2:3] += row_sum(gnormed[w])
        gmid = grads[w] + norm_back(normal, rate, gnormed[w] * vec_ref[5:6])
        gmid_ref[w] = gmid
        gvec_ref[0:1] += row_sum(gmid)
        gmid_low = gmid.astype(BF16)
        total = total + dot(att_ref[w], gmid_low, TN)
        gatt_ref[w] = dot(gmid_low, outer, NT).astype(BF16)
    pack_ref[:, 0:ROWS, :] += total.reshape(PACKS, ROWS, D)

    @pl.when(pl.program_id(0) == pl.num_programs(0) - 1)
    def _():
        result_ref[...] = pack_ref[...].astype(result_ref.dtype)


def run_feed_backward(layer, grad, active, slope, middle, attended, pack, vec, dtype):
    windows = middle.shape[0]
    count = grad.shape[2] // WW
    row_blocks = grad.shape[1] // WH

    def some(width):
        return pl.BlockSpec((count, WIN, width), lambda i: (i, 0, 0))

    grid_block = pl.BlockSpec(
        (1, WH, count * WW, WT, D), lambda i: (i // row_blocks, i % row_blocks, 0, 0, 0)
    )
    return pl.pallas_call(
        feed_backward,
        grid=(windows // count,),
        in_specs=[
            grid_block,
            some(FF),
            some(FF),
            some(D),
            some(D),
            pack_spec(64, 3 * layer),
            pack_spec(64, 3 * layer + 1),
            pack_spec(64, 3 * layer + 2),
            whole_spec(12, D),
        ],
        out_specs=[
            some(D),
            some(D),
            whole_spec(PACKS, 144, D),
            pl.BlockSpec((8, D), lambda i: (0, 0)),
        ],
        out_shape=[
            jax.ShapeDtypeStruct((windows, WIN, D), F32),
            jax.ShapeDtypeStruct((windows, WIN, D), BF16),
            jax.ShapeDtypeStruct((PACKS, 192, D), dtype),
            jax.ShapeDtypeStruct((8, D), F32),
        ],
        scratch_shapes=[pltpu.VMEM((PACKS, 144, D), F32)],
        cost_estimate=cost(windows, 7),
        compiler_params=params(),
    )(grad, active, slope, middle, attended, pack, pack, pack, vec)


def attention_backward(
    pushed,
    whole_ref, x_ref, gatt_ref, att_ref, rate_ref, soft_ref, qkv_ref, gmid_ref, in_ref, vec_ref,
    out_ref, result_ref, gvec_ref, table_ref,
    pack_ref, sum_s, qt_s, dot_s, gkt_s, gvt_s, gq_s, do_s, wide_s, *push,
):
    step = pl.program_id(0)
    if pushed:
        push_begin()

    @pl.when(step == 0)
    def _():
        sum_s[...] = jnp.zeros_like(sum_s)
        pack_ref[...] = jnp.zeros_like(pack_ref)
        gvec_ref[...] = jnp.zeros_like(gvec_ref)

    lane = lax.broadcasted_iota(jnp.int32, (1, 128), 1)
    scaled = (gatt_ref[0].astype(F32) * rate_ref[0]).astype(BF16)
    do_s[...] = scaled
    product = scaled.astype(F32) * att_ref[0].astype(F32)
    gather_row = lax.broadcasted_iota(jnp.int32, (D, 128), 0) // HD
    gather_col = lax.broadcasted_iota(jnp.int32, (D, 128), 1)
    gather = jnp.where(
        (gather_row == gather_col % HEADS) & (gather_col < 3 * HEADS), 1.0, 0.0
    ).astype(BF16)
    high = product.astype(BF16)
    low = (product - high.astype(F32)).astype(BF16)
    inner = dot(high, gather) + dot(low, gather)
    first, second, third = split_three(inner)
    inner = jnp.where(lane < HEADS, first, jnp.where(lane < 2 * HEADS, second, third))
    qt_s[...] = jnp.transpose(qkv_ref[0, :, 0:D].astype(F32)).astype(BF16)
    dot_s[...] = jnp.transpose(scaled.astype(F32)).astype(BF16)
    minus = jnp.broadcast_to(jnp.where(lane < 3 * HEADS, -1.0, 0.0), (WIN, 128)).astype(BF16)
    zero = jnp.zeros((WIN, 128), BF16)

    def score(head):
        first = head // 4 * 128
        grad4 = jnp.where(head_lanes(head % 4), do_s[:, first : first + 128], zero)
        own = jnp.where((lane % HEADS == head) & (lane < 3 * HEADS), inner, zero)
        left = jnp.concatenate([grad4, own], axis=1)
        values4 = qkv_ref[0, :, 2 * D + first : 2 * D + first + 128]
        return dot(left, jnp.concatenate([values4, minus], axis=1), NT)

    parts = [None]

    def finish(head, soft, gtotal):
        first = head // 4 * 128
        rows = slice(head * HD, (head + 1) * HD)
        gvt_s[rows, :] = dot(dot_s[rows, :], soft)
        gkt_s[rows, :] = dot(qt_s[rows, :], gtotal)
        keys4 = qkv_ref[0, :, D + first : D + first + 128]
        part = dot(gtotal, jnp.where(head_lanes(head % 4), keys4, zero))
        parts[0] = part if head % 4 == 0 else parts[0] + part
        if head % 4 == 3:
            gq_s[:, first : first + 128] = parts[0].astype(BF16)

    slope = score(0)
    last = None
    for head in range(HEADS):
        following = score(head + 1) if head < HEADS - 1 else None
        soft = soft_ref[0, head]
        gtotal = soft.astype(F32) * slope
        sum_s[head] += gtotal
        gtotal = gtotal.astype(BF16)
        if head > 0:
            finish(head - 1, *last)
        last = (soft, gtotal)
        slope = following
    finish(HEADS - 1, *last)
    gquery = gq_s[...]
    gkeys = (jnp.transpose(gkt_s[...]) * LN2).astype(BF16)
    gvalues = jnp.transpose(gvt_s[...]).astype(BF16)
    normal, rate = normalize(x_ref[0].astype(F32).reshape(WIN, D))
    normed = (normal * vec_ref[0:1] + vec_ref[1:2]).astype(BF16)
    pack_ref[:, 0:ROWS, :] += (dot(normed, gquery, TN) * SCALE).reshape(PACKS, ROWS, D)
    pack_ref[:, ROWS : 2 * ROWS, :] += dot(normed, gkeys, TN).reshape(PACKS, ROWS, D)
    pack_ref[:, 2 * ROWS :, :] += dot(normed, gvalues, TN).reshape(PACKS, ROWS, D)
    gvec_ref[2:3] += row_sum(gquery.astype(F32)) * SCALE
    gvec_ref[3:4] += row_sum(gvalues.astype(F32))
    gnormed = (
        dot(gquery, square(in_ref, 0), NT) * SCALE
        + dot(gkeys, square(in_ref, ROWS), NT)
        + dot(gvalues, square(in_ref, 2 * ROWS), NT)
    )
    gvec_ref[0:1] += row_sum(gnormed * normal)
    gvec_ref[1:2] += row_sum(gnormed)
    grad = gmid_ref[0] + norm_back(normal, rate, gnormed * vec_ref[0:1])
    if pushed:
        push_window(False, grad, out_ref, *push)
    else:
        out_ref[0] = grad.reshape(WH, WW, WT, D).astype(out_ref.dtype)

    @pl.when(step == pl.num_programs(0) - 1)
    def _():
        result_ref[...] = pack_ref[...].astype(result_ref.dtype)
        table_ref[...] = jnp.zeros_like(table_ref)
        for col in range(WW):
            wide_s[...] = jnp.zeros_like(wide_s)
            for row in range(WH):
                place = (row * WW + col) * WT
                low_lane = (WH - 1 - row) * WW * WT
                wide_s[:, low_lane : low_lane + WIN] += sum_s[:, place : place + WT, :].reshape(
                    HEADS * WT, WIN
                )
            for shift in range(2 * WH - 1):
                low_lane = (shift * (2 * WW - 1) + WW - 1 - col) * WT
                table_ref[:, low_lane : low_lane + WW * WT] += wide_s[
                    :, shift * WW * WT : (shift + 1) * WW * WT
                ]


def run_attention_backward(
    layer, whole, x, gattended, attended, rates, soft, qkv, gmiddle, pack, vec, dtype, pack_dtype, pushed
):
    windows = gmiddle.shape[0]
    return pl.pallas_call(
        functools.partial(attention_backward, pushed),
        grid=(windows,),
        in_specs=[
            pl.BlockSpec(memory_space=pl.ANY),
            grid_spec(x.shape),
            window_spec(WIN, D),
            window_spec(WIN, D),
            window_spec(WIN, D),
            window_spec(HEADS, WIN, WIN),
            window_spec(WIN, 3 * D),
            window_spec(WIN, D),
            pack_spec(64, 3 * layer),
            whole_spec(12, D),
        ],
        out_specs=[
            pl.BlockSpec(memory_space=pl.ANY) if pushed else grid_spec(x.shape),
            pack_spec(48, 3),
            pl.BlockSpec((4, D), lambda i: (0, 0)),
            pl.BlockSpec((HEADS * WT, CELLS * WT), lambda i: (0, 0)),
        ],
        out_shape=[
            jax.ShapeDtypeStruct(x.shape, dtype),
            jax.ShapeDtypeStruct((PACKS, 192, D), pack_dtype),
            jax.ShapeDtypeStruct((4, D), F32),
            jax.ShapeDtypeStruct((HEADS * WT, CELLS * WT), F32),
        ],
        scratch_shapes=[
            pltpu.VMEM((PACKS, 48, D), F32),
            pltpu.VMEM((HEADS, WIN, WIN), F32),
            pltpu.VMEM((D, WIN), BF16),
            pltpu.VMEM((D, WIN), BF16),
            pltpu.VMEM((D, WIN), F32),
            pltpu.VMEM((D, WIN), F32),
            pltpu.VMEM((WIN, D), BF16),
            pltpu.VMEM((WIN, D), BF16),
            pltpu.VMEM((HEADS * WT, (2 * WH - 1) * WW * WT), F32),
        ]
        + (push_scratch() if pushed else []),
        cost_estimate=cost(windows, 12),
        compiler_params=params(4 if pushed else None),
        input_output_aliases={0: 1},
    )(whole, x, gattended, attended, rates, soft, qkv, gmiddle, pack, vec)


def expand_bias(cells_ref, out_ref, wide_s):
    for col in range(WW):
        for shift in range(2 * WH - 1):
            low_lane = (shift * (2 * WW - 1) + WW - 1 - col) * WT
            wide_s[:, shift * WW * WT : (shift + 1) * WW * WT] = cells_ref[
                :, low_lane : low_lane + WW * WT
            ]
        for row in range(WH):
            place = (row * WW + col) * WT
            low_lane = (WH - 1 - row) * WW * WT
            out_ref[:, place : place + WT, :] = wide_s[:, low_lane : low_lane + WIN].reshape(
                HEADS, WT, WIN
            )


def run_expand_bias(cells):
    return pl.pallas_call(
        expand_bias,
        out_shape=jax.ShapeDtypeStruct((HEADS, WIN, WIN), F32),
        scratch_shapes=[pltpu.VMEM((HEADS * WT, (2 * WH - 1) * WW * WT), F32)],
        compiler_params=pltpu.CompilerParams(vmem_limit_bytes=61 * 1024 * 1024),
    )(cells)


AUX_ROWS = 8
SHARES = ((1, 0, AUX_ROWS, 0), (0, 0, 48, 0), (0, 48, 48, 1), (0, 96, 48, 0), (0, 144, 48, 1))


def fold_gradients(*refs):
    operands = refs[:2]
    pack_out, aux_out = refs[2:4]
    buffers = refs[4:19]
    send_sem, recv_sem, wide_send, wide_recv = refs[19:]
    batch = lax.axis_index("batch")
    y = lax.axis_index("seq")
    z, x, core = batch // 4, (batch // 2) % 2, batch % 2
    count = len(SHARES)

    def device(z_to, x_to, core_to, y_to):
        return ((z_to * 2 + x_to) * 2 + core_to, y_to)

    barrier = pltpu.get_barrier_semaphore()

    def greet(k, carry):
        other = lax.rem(batch * 2 + y + k, 32)
        pl.semaphore_signal(
            barrier, inc=1, device_id=(other // 2, other % 2), device_id_type=pl.DeviceIdType.MESH
        )
        return carry

    lax.fori_loop(1, 32, greet, 0)
    pl.semaphore_wait(barrier, 31)

    def send(number, source, target, to):
        copy = pltpu.make_async_remote_copy(
            src_ref=source,
            dst_ref=target,
            send_sem=send_sem.at[number],
            recv_sem=recv_sem.at[number],
            device_id=to,
            device_id_type=pl.DeviceIdType.MESH,
        )
        copy.start()
        return copy

    copies = []
    for k, (which, first, size, order) in enumerate(SHARES):
        source = operands[which].at[:, :, 1 - core, :, pl.ds(first, size), :]
        copies.append(send(k, source, buffers[3 * k], device(z, x, 1 - core, y)))
    for k, (which, first, size, order) in enumerate(SHARES):
        copies[k].wait()
        held = buffers[3 * k]

        def add_core(i, carry, which=which, first=first, size=size, held=held):
            a, b = i // 2, i % 2
            mine = operands[which][a, b, core, :, first : first + size, :].astype(F32)
            held[a, b] = (held[a, b].astype(F32) + mine).astype(held.dtype)
            return carry

        lax.fori_loop(0, 8, add_core, 0)
        if order == 0:
            copies.append(send(count + k, held.at[:, 1 - x], buffers[3 * k + 1], device(z, 1 - x, core, y)))
        else:
            copies.append(send(count + k, held.at[:, :, 1 - y], buffers[3 * k + 1], device(z, x, core, 1 - y)))
    for k, (which, first, size, order) in enumerate(SHARES):
        copies[count + k].wait()
        before, held = buffers[3 * k], buffers[3 * k + 1]

        def add_next(i, carry, order=order, before=before, held=held):
            a, b = i // 2, i % 2
            mine = before[a, x, b] if order == 0 else before[a, b, y]
            held[a, b] = (held[a, b].astype(F32) + mine.astype(F32)).astype(held.dtype)
            return carry

        lax.fori_loop(0, 8, add_next, 0)
        if order == 0:
            copies.append(send(2 * count + k, held.at[:, 1 - y], buffers[3 * k + 2].at[pl.ds(0, 4)], device(z, x, core, 1 - y)))
        else:
            copies.append(send(2 * count + k, held.at[:, 1 - x], buffers[3 * k + 2].at[pl.ds(0, 4)], device(z, 1 - x, core, y)))
    far = []
    for k, (which, first, size, order) in enumerate(SHARES):
        copies[2 * count + k].wait()
        before, held = buffers[3 * k + 1], buffers[3 * k + 2]

        def add_last(a, carry, order=order, before=before, held=held):
            mine = before[a, y] if order == 0 else before[a, x]
            held[a] = (held[a].astype(F32) + mine.astype(F32)).astype(held.dtype)
            return carry

        lax.fori_loop(0, 4, add_last, 0)
        for step in range(1, 4):
            other = lax.rem(z + step, 4)
            far.append(
                send(
                    3 * count + 3 * k + step - 1,
                    held.at[other],
                    held.at[3 + step],
                    device(other, x, core, y),
                )
            )
    for k, (which, first, size, order) in enumerate(SHARES):
        for step in range(1, 4):
            far[3 * k + step - 1].wait()
        held = buffers[3 * k + 2]
        total = held[z].astype(F32) + held[4].astype(F32)
        total = total + held[5].astype(F32) + held[6].astype(F32)
        if which == 0:
            pack_out[first : first + size, :] = total
        else:
            aux_out[batch * 2 + y] = total

    def spread(k, carry):
        other = lax.rem(batch * 2 + y + k, 32)
        pltpu.make_async_remote_copy(
            src_ref=aux_out.at[batch * 2 + y],
            dst_ref=aux_out.at[batch * 2 + y],
            send_sem=wide_send,
            recv_sem=wide_recv,
            device_id=(other // 2, other % 2),
            device_id_type=pl.DeviceIdType.MESH,
        ).start()
        return carry

    lax.fori_loop(1, 32, spread, 0)
    others = aux_out.at[pl.ds(0, 31)]
    pltpu.make_async_copy(others, others, wide_send).wait()
    pltpu.make_async_copy(others, others, wide_recv).wait()


def run_fold_gradients(big, aux):
    operands = [value.reshape((4, 2, 2, 2) + value.shape[1:]) for value in (big, aux)]
    scratch = []
    for which, first, size, order in SHARES:
        dtype = operands[which].dtype
        scratch.append(pltpu.VMEM((4, 2, 2, size, D), dtype))
        scratch.append(pltpu.VMEM((4, 2, size, D), dtype))
        scratch.append(pltpu.VMEM((7, size, D), dtype))
    semaphores = 6 * len(SHARES)
    return pl.pallas_call(
        fold_gradients,
        in_specs=[pl.BlockSpec(memory_space=pltpu.VMEM)] * 2,
        out_specs=[pl.BlockSpec(memory_space=pltpu.VMEM)] * 2,
        out_shape=[
            jax.ShapeDtypeStruct((192, D), F32),
            jax.ShapeDtypeStruct((32, AUX_ROWS, D), F32),
        ],
        scratch_shapes=scratch
        + [
            pltpu.SemaphoreType.DMA((semaphores,)),
            pltpu.SemaphoreType.DMA((semaphores,)),
            pltpu.SemaphoreType.DMA,
            pltpu.SemaphoreType.DMA,
        ],
        compiler_params=pltpu.CompilerParams(
            vmem_limit_bytes=61 * 1024 * 1024, collective_id=1, has_side_effects=True
        ),
    )(*operands)


def offset_places():
    frame, row, col = np.meshgrid(
        np.arange(1 - WT, WT), np.arange(1 - WH, WH), np.arange(1 - WW, WW), indexing="ij"
    )

    def place(f, r, c):
        return (np.maximum(f, 0) * WH + np.maximum(r, 0)) * WW + np.maximum(c, 0)

    return (place(frame, row, col) * WIN + place(-frame, -row, -col)).reshape(-1)[::-1].copy()


def interleave():
    cell = np.arange(CELLS * WT)
    source = jnp.asarray((cell % WT) * CELLS + cell // WT, jnp.int32)
    order = jnp.arange(CELLS * WT, dtype=jnp.int32)
    return (order[:, None] == source[None, :]).astype(BF16)


def join_three(values, axis):
    first, second, third = jnp.split(values, 3, axis=axis)
    return first + second + third


def bias_cells(tables, chosen, order):
    flat = jnp.concatenate([tables[layer] for layer in range(LAYERS)], axis=1) * LOG2E
    pieces = jnp.concatenate(split_three(flat), axis=1)
    taken = dot(pieces, chosen, (((0,), (1,)), ((), ()))).astype(BF16)
    placed = jnp.stack(
        [taken[:, (WT - 1 - t) * CELLS : (2 * WT - 1 - t) * CELLS] for t in range(WT)], axis=1
    )
    cells = dot(placed.reshape(-1, WT * CELLS), order)
    return join_three(cells, 0).reshape(LAYERS, HEADS * WT, CELLS * WT)


def cells_to_rows(cells, order):
    pieces = jnp.concatenate(split_three(cells.reshape(-1, CELLS * WT)), axis=0)
    placed = join_three(dot(pieces, order, NT), 0).reshape(LAYERS * HEADS, WT, CELLS * WT)
    parts = [
        jnp.pad(placed[:, t], ((0, 0), ((WT - 1 - t) * CELLS, t * CELLS))) for t in range(WT)
    ]
    return functools.reduce(jnp.add, parts)


def rows_to_table(rows, chosen):
    pieces = jnp.concatenate(split_three(rows), axis=0)
    total = join_three(dot(chosen, pieces, (((0,), (1,)), ((), ()))), 1)
    return jnp.stack([total[:, i * HEADS : (i + 1) * HEADS] for i in range(LAYERS)])


def spatial_blocks(field):
    clip_count, frames_here, width = (field.shape[0], field.shape[1], field.shape[-1])
    shaped = field.reshape(clip_count, frames_here, HGT // WH, WH, WID // WW, WW, width)
    shaped = shaped.transpose(0, 2, 4, 1, 3, 5, 6)
    return shaped.reshape(clip_count * (HGT // WH) * (WID // WW), frames_here, WH * WW, width)


def roll_space(field, amount, first):
    return jnp.roll(field, (amount, amount), axis=(first, first + 1))


def swap_halves(part):
    return lax.ppermute(part, "seq", [(0, 1), (1, 0)])


class Placement:
    def __init__(self, clip_count, frames_here):
        self.clips = clip_count
        self.frames = frames_here
        self.parts = lax.axis_size("seq")
        self.near = self.parts == 2 and frames_here == WT

    def grid_shape(self):
        if self.near:
            return (self.clips, HGT, WID, WT, D)
        columns = self.clips * 4 // self.parts
        return (columns * 2, WH, WW, WT, D)

    def enter(self, field, shifted):
        if self.near:
            if shifted:
                arrived = swap_halves(field[:, :SHIFT_T])
                field = jnp.concatenate([field[:, SHIFT_T:], arrived], axis=1)
                field = roll_space(field, -SHIFT_S, 2)
            return field.transpose(0, 2, 3, 1, 4)
        if shifted:
            field = roll_space(field, -SHIFT_S, 2)
        columns = lax.all_to_all(
            spatial_blocks(field), "seq", split_axis=0, concat_axis=1, tiled=True
        )
        if shifted:
            columns = jnp.roll(columns, -SHIFT_T, axis=1)
        windows = columns.reshape(-1, WT, WH, WW, D)
        return windows.transpose(0, 2, 3, 1, 4)

    def leave(self, grid, shifted):
        if self.near:
            field = grid.transpose(0, 3, 1, 2, 4)
            if shifted:
                field = roll_space(field, SHIFT_S, 2)
                arrived = swap_halves(field[:, SHIFT_T:])
                field = jnp.concatenate([arrived, field[:, :SHIFT_T]], axis=1)
            return field
        columns = grid.transpose(0, 3, 1, 2, 4).reshape(-1, FRAMES, WH * WW, D)
        if shifted:
            columns = jnp.roll(columns, SHIFT_T, axis=1)
        columns = lax.all_to_all(columns, "seq", split_axis=1, concat_axis=0, tiled=True)
        shaped = columns.reshape(self.clips, HGT // WH, WID // WW, self.frames, WH, WW, D)
        shaped = shaped.transpose(0, 3, 1, 4, 2, 5, 6)
        field = shaped.reshape(self.clips, self.frames, HGT, WID, D)
        return roll_space(field, SHIFT_S, 2) if shifted else field

    def forth(self, grid):
        return self.enter(self.leave(grid, False), True)

    def back(self, grid):
        return self.enter(self.leave(grid, True), False)

    def mask_lanes(self):
        if self.near:
            index = jnp.arange(self.clips * 4, dtype=jnp.int32)
            late = jnp.full(index.shape, lax.axis_index("seq"), jnp.int32)
            block = index % 4
        else:
            columns = self.clips * 4 // self.parts
            index = jnp.arange(columns * 2, dtype=jnp.int32)
            late = index % 2
            block = (lax.axis_index("seq") * columns + index // 2) % 4
        place = np.arange(WIN)
        frame_late = jnp.asarray(place % WT >= WT - SHIFT_T).astype(jnp.int32)
        row_late = jnp.asarray(place // (WT * WW) >= WH - SHIFT_S).astype(jnp.int32)
        col_late = jnp.asarray(place // WT % WW >= WW - SHIFT_S).astype(jnp.int32)
        region = (
            late[:, None] * frame_late * 4
            + (block // 2)[:, None] * row_late * 2
            + (block % 2)[:, None] * col_late
        )
        lane = np.arange(128)
        same = (region[:, :, None] == lane % 8) & (lane < 24)
        pieces = []
        rest = np.float32(MASKED * LOG2E)
        for _ in range(3):
            piece = np.float32(np.asarray(rest).astype(BF16))
            pieces.append(piece)
            rest = np.float32(rest - piece)
        piece_of = np.zeros((128,), np.float32)
        for number, piece in enumerate(pieces):
            piece_of[8 * number : 8 * number + 8] = -piece
            piece_of[24 + number] = piece
        always = (lane >= 24) & (lane < 27)
        on_keys = jnp.where(same | always, 1.0, 0.0)
        return (on_keys * piece_of).astype(BF16), on_keys.astype(BF16)


def pack_layer(inner, outer, up, down):
    parts = [inner[:, i * D : (i + 1) * D] for i in range(3)] + [outer]
    parts = parts + [up[:, i * D : (i + 1) * D] for i in range(4)] + [down]
    return jnp.concatenate(parts, axis=0)


def per_device(
    clips_in,
    cotangent,
    offset_index,
    first_gain,
    first_shift,
    inner_weight,
    inner_bias,
    outer_weight,
    outer_bias,
    second_gain,
    second_shift,
    up_weight,
    up_bias,
    down_weight,
    down_bias,
    bias_table,
):
    place = Placement(clips_in.shape[0], clips_in.shape[1])
    rows = inner_weight.shape[1]
    devices = D // rows
    vectors = [
        first_gain, first_shift, inner_bias, outer_bias, second_gain, second_shift,
        down_bias, up_bias,
    ]
    vec_pack = jnp.concatenate(vectors, axis=1)
    width = vec_pack.shape[1]
    vec_rows = jnp.pad(vec_pack, ((0, 14), (0, D - width)))
    local = [
        pack_layer(inner_weight[layer], outer_weight[layer], up_weight[layer], down_weight[layer])
        for layer in range(LAYERS)
    ]
    full = lax.all_gather(jnp.concatenate(local + [vec_rows], axis=0), AXES, axis=0)
    vecs = []
    for layer in range(LAYERS):
        held = full[:, 24 * rows + layer, :width].astype(F32)
        pieces = []
        start = 0
        for vector in vectors:
            size = vector.shape[1]
            pieces.append(held[:, start : start + size].reshape(-1, D))
            start += size
        vecs.append(jnp.concatenate(pieces, axis=0))
    if rows != ROWS:
        parts = []
        for first in (0, 12 * rows):
            for i in range(8):
                part = full[:, first + i * rows : first + (i + 1) * rows]
                parts.append(part.reshape(PACKS, ROWS, D))
            part = full[:, first + 8 * rows : first + 12 * rows]
            parts.append(part.reshape(PACKS, 4 * ROWS, D))
        full = jnp.concatenate(parts, axis=1)
    weights = [(full, vec) for vec in vecs]
    taken_rows = jnp.take(offset_index.reshape(-1), offset_places())
    order = jnp.arange(BIAS_ROWS, dtype=jnp.int32)
    chosen = (taken_rows[:, None] == order[None, :]).astype(BF16)
    interleaved = interleave()
    cells_in = bias_cells(bias_table, chosen, interleaved)
    bias = [run_expand_bias(cells_in[layer]) for layer in range(LAYERS)]
    shape = place.grid_shape()
    aug = place.mask_lanes()

    x_zero = place.enter(clips_in, False)
    upstream = place.enter(cotangent, True)
    saved = []
    x = x_zero
    for layer in range(LAYERS):
        pack, vec = weights[layer]
        qkv, soft, rates, attended, middle, active, slope, result = run_block_forward(
            layer, x, pack, vec, bias[layer], aug if layer == 1 else None,
            F32 if layer == 0 or place.near else BF16, place.near,
        )
        saved.append((x, qkv, soft, rates, attended, middle, active, slope))
        x = place.forth(result) if layer == 0 and not place.near else result
    clips_out = place.leave(x, not place.near).astype(BF16)

    scattered = [None] * LAYERS
    vec_parts = [None] * LAYERS
    cell_parts = [None] * LAYERS

    def scatter(value, blocks):
        if rows != ROWS:
            per = ROWS // rows
            parts = []
            start = 0
            for size in blocks:
                part = value[:, start : start + size].reshape(PACKS * per, size // per, D)
                parts.append(part)
                start += size
            value = jnp.concatenate(parts, axis=1)
        return lax.psum_scatter(value, AXES, scatter_dimension=0, tiled=False)

    folded = lax.axis_size("batch") == 16 and lax.axis_size("seq") == 2
    for layer in reversed(range(LAYERS)):
        pack, vec = weights[layer]
        x, qkv, soft, rates, attended, middle, active, slope = saved[layer]
        gmiddle, gattended, big, gvec_two = run_feed_backward(
            layer, upstream, active, slope, middle, attended, pack, vec, F32 if layer == 1 or not folded else BF16
        )
        upstream, big, gvec_one, cells = run_attention_backward(
            layer, big, x, gattended, attended, rates, soft, qkv, gmiddle, pack, vec,
            F32 if layer == 1 else BF16, F32 if layer == 1 or not folded else BF16,
            place.near and layer == 1,
        )
        if layer == 1 or not folded:
            scattered[layer] = scatter(big, [ROWS] * 5 + [4 * ROWS] + [ROWS] * 3)
        vec_parts[layer] = jnp.concatenate([gvec_one, gvec_two], axis=0)
        cell_parts[layer] = cells
        if layer == 1 and not place.near:
            upstream = place.back(upstream)
    clips_grad = place.leave(upstream, False)

    table_rows = cells_to_rows(jnp.stack(cell_parts), interleaved)
    vec_stack = jnp.stack(vec_parts)
    if folded:
        aux = jnp.concatenate([table_rows.reshape(-1), vec_stack.reshape(-1)])
        used = aux.shape[0]
        aux = jnp.pad(aux, (0, PACKS * AUX_ROWS * D - used)).reshape(PACKS, AUX_ROWS, D)
        scattered[0], aux = run_fold_gradients(big, aux)
        aux = aux.reshape(-1)[:used]
        table_total = aux[: table_rows.size].reshape(table_rows.shape)
        vec_total = aux[table_rows.size :].reshape(vec_stack.shape)
    else:
        vec_total, table_total = lax.psum((vec_stack, table_rows), AXES)
    table_total = rows_to_table(table_total, chosen)

    device = lax.axis_index(AXES)

    def own(first, count):
        whole = vec_total[:, first : first + count].reshape(LAYERS, count * D)
        size = count * D // devices
        return lax.dynamic_slice_in_dim(whole, device * size, size, axis=1)

    def both(first, count):
        parts = []
        for layer in range(LAYERS):
            value = scattered[layer]
            columns = [
                value[first + i * rows : first + (i + 1) * rows] for i in range(count)
            ]
            parts.append(jnp.concatenate(columns, axis=1))
        return jnp.stack(parts)

    down = jnp.stack([scattered[layer][5 * rows : 9 * rows] for layer in range(LAYERS)])
    return (
        clips_out,
        clips_grad,
        own(0, 1),
        own(1, 1),
        both(9 * rows, 3),
        own(2, 2),
        both(0, 1),
        own(4, 1),
        own(5, 1),
        own(6, 1),
        both(rows, 4),
        own(8, 4),
        down,
        own(7, 1),
        table_total,
    )


def solution(mesh):
    clips = P("batch", "seq", None, None, None)
    vector = P(None, AXES)
    matrix = P(None, AXES, None)
    return jax.shard_map(
        per_device,
        mesh=mesh,
        in_specs=(
            clips, clips, P(), vector, vector, matrix, vector, matrix, vector, vector, vector,
            matrix, vector, matrix, vector, P(),
        ),
        out_specs=(
            clips, clips, vector, vector, matrix, vector, matrix, vector, vector, vector,
            matrix, vector, matrix, vector, P(),
        ),
        check_vma=False,
    )
```

```python
import functools

import jax
import jax.numpy as jnp
import numpy as np
from jax import lax
from jax.experimental import pallas as pl
from jax.experimental.pallas import tpu as pltpu
from jax.sharding import PartitionSpec as P

D = 512
HEADS = 16
HD = 32
FF = 2048
WT = 8
WH = 7
WW = 7
FRAMES = 16
HGT = 14
WID = 14
LAYERS = 2
SHIFT_T = 4
SHIFT_S = 3
WIN = 392
BIAS_ROWS = 2535
ROWS = 16
PACKS = D // ROWS
CELLS = (2 * WH - 1) * (2 * WW - 1)

EPSILON = 1e-05
MASKED = -100.0
LOG2E = 1.4426950408889634
LN2 = 0.6931471805599453
SCALE = HD**-0.5

BF16 = jnp.bfloat16
F32 = jnp.float32
AXES = ("batch", "seq")

NT = (((1,), (1,)), ((), ()))
TN = (((0,), (0,)), ((), ()))


def params(collective=None):
    return pltpu.CompilerParams(
        vmem_limit_bytes=61 * 1024 * 1024,
        dimension_semantics=("arbitrary",),
        collective_id=collective,
        has_side_effects=collective is not None,
    )


def cost(windows, microseconds):
    return pl.CostEstimate(
        flops=int(windows * microseconds * 2e8), bytes_accessed=0, transcendentals=0
    )


def dot(left, right, dims=(((1,), (0,)), ((), ()))):
    return lax.dot_general(left, right, dims, preferred_element_type=F32)


def normalize(values):
    average = jnp.mean(values, axis=-1, keepdims=True)
    centred = values - average
    rate = lax.rsqrt(jnp.mean(centred * centred, axis=-1, keepdims=True) + EPSILON)
    return centred * rate, rate


def row_sum(values):
    return jnp.sum(values, axis=0, keepdims=True)


def split_three(values):
    high = values.astype(BF16)
    rest = values - high.astype(F32)
    middle = rest.astype(BF16)
    low = (rest - middle.astype(F32)).astype(BF16)
    return high, middle, low


def square(ref, first):
    return ref[:, first : first + ROWS, :].reshape(D, D)


def grid_spec(shape):
    row_blocks, col_blocks = shape[1] // WH, shape[2] // WW
    per_clip = row_blocks * col_blocks
    return pl.BlockSpec(
        (1, WH, WW, WT, D),
        lambda i: (i // per_clip, (i % per_clip) // col_blocks, i % col_blocks, 0, 0),
    )


def window_spec(*tail):
    return pl.BlockSpec((1,) + tail, lambda i: (i,) + (0,) * len(tail))


def whole_spec(*shape):
    return pl.BlockSpec(shape, lambda i: (0,) * len(shape), pipeline_mode=pl.Buffered(1))


def pack_spec(rows, index):
    return pl.BlockSpec(
        (PACKS, rows, D), lambda i: (0, index, 0), pipeline_mode=pl.Buffered(1)
    )


def head_lanes(which):
    lane = lax.broadcasted_iota(jnp.int32, (1, 128), 1)
    return (lane // HD) == which


def lane_slice(group, base=0):
    return pl.ds(pl.multiple_of(base + group * 128, 128), 128)


def neighbour():
    return (lax.axis_index("batch"), 1 - lax.axis_index("seq"))


def piece_places(forth, block):
    if forth:
        return ((0, 3, lax.rem(7 * block + 11, 14)), (3, 4, 7 * block))
    return ((0, 4, 7 * block + 3), (4, 3, lax.rem(7 * block + 7, 14)))


def window_copies(forth, step, slot, stage, out_ref, own_sem, send_sem, recv_sem):
    clip, row_block, col_block = step // 4, (step // 2) % 2, step % 2
    kept, kept_to, sent, sent_to = (4, 0, 0, 4) if forth else (0, 4, 4, 0)
    copies = []
    number = 0
    for row, rows, row_to in piece_places(forth, row_block):
        for col, cols, col_to in piece_places(forth, col_block):

            def place(frame, row_to=row_to, rows=rows, col_to=col_to, cols=cols):
                return out_ref.at[
                    clip, pl.ds(row_to, rows), pl.ds(col_to, cols), pl.ds(frame, 4), :
                ]

            def held(frame, row=row, rows=rows, col=col, cols=cols):
                return stage.at[
                    slot, pl.ds(row, rows), pl.ds(col, cols), pl.ds(frame, 4), :
                ]

            copies.append(
                pltpu.make_async_copy(held(kept), place(kept_to), own_sem.at[slot, number])
            )
            copies.append(
                pltpu.make_async_remote_copy(
                    src_ref=held(sent),
                    dst_ref=place(sent_to),
                    send_sem=send_sem.at[slot, number],
                    recv_sem=recv_sem,
                    device_id=neighbour(),
                    device_id_type=pl.DeviceIdType.MESH,
                )
            )
            number += 1
    return copies


def wait_left(copies):
    for number, copy in enumerate(copies):
        if number % 2 == 0:
            copy.wait()
        else:
            copy.wait_send()


def own_place():
    batch = lax.axis_index("batch")
    return batch // 4, (batch // 2) % 2, batch % 2, lax.axis_index("seq")


def device_at(z, x, core, y):
    return ((z * 2 + x) * 2 + core, y)


def push_begin(carried):
    @pl.when(pl.program_id(0) == 0)
    def _():
        barrier = pltpu.get_barrier_semaphore()
        peers = [neighbour()]
        if carried:
            z, x, core, y = own_place()
            peers += [device_at(lax.rem(z + i, 4), x, core, y) for i in range(1, 4)]
            peers += [device_at(z, 1 - x, core, y), device_at(z, x, 1 - core, y)]
        for peer in peers:
            pl.semaphore_signal(
                barrier, inc=1, device_id=peer, device_id_type=pl.DeviceIdType.MESH
            )
        pl.semaphore_wait(barrier, len(peers))


def carry_gather(shard_ref, full_ref, shard_sem, send_sem, recv_sem):
    step = pl.program_id(0)
    z, x, core, y = own_place()
    mine = full_ref.at[z, x, core, y]
    keep = pltpu.make_async_copy(shard_ref, mine, shard_sem)

    def send(number, source, target, to):
        return pltpu.make_async_remote_copy(
            src_ref=source,
            dst_ref=target,
            send_sem=send_sem.at[number],
            recv_sem=recv_sem.at[number],
            device_id=to,
            device_id_type=pl.DeviceIdType.MESH,
        )

    pair = full_ref.at[z, x, core]
    plane = full_ref.at[:, x, core]
    half = full_ref.at[:, :, core]
    over_y = send(0, shard_ref, mine, device_at(z, x, core, 1 - y))
    over_z = [
        send(i, pair, pair, device_at(lax.rem(z + i, 4), x, core, y)) for i in range(1, 4)
    ]
    over_x = send(4, plane, plane, device_at(z, 1 - x, core, y))
    over_core = send(5, half, half, device_at(z, x, 1 - core, y))

    @pl.when(step == 0)
    def _():
        keep.start()
        over_y.start()

    @pl.when(step == 1)
    def _():
        keep.wait()
        over_y.wait()
        for copy in over_z:
            copy.start()

    @pl.when(step == 4)
    def _():
        for copy in over_z:
            copy.wait()
        over_x.start()

    @pl.when(step == 7)
    def _():
        over_x.wait()
        over_core.start()

    return over_core


def push_window(forth, value, out_ref, stage, own_sem, send_sem, recv_sem):
    step = pl.program_id(0)
    slot = lax.rem(step, 2)
    rest = (stage, out_ref, own_sem, send_sem, recv_sem)

    @pl.when(step >= 2)
    def _():
        wait_left(window_copies(forth, step - 2, slot, *rest))

    stage[slot] = value.reshape(WH, WW, WT, D)
    for copy in window_copies(forth, step, slot, *rest):
        copy.start()

    @pl.when(step == pl.num_programs(0) - 1)
    def _():
        wait_left(window_copies(forth, step - 1, 1 - slot, *rest))
        wait_left(window_copies(forth, step, slot, *rest))
        half = out_ref.at[:, :, :, pl.ds(4 if forth else 0, 4), :]
        pltpu.make_async_copy(half, half, recv_sem).wait()


def push_scratch():
    return [
        pltpu.VMEM((2, WH, WW, WT, D), F32),
        pltpu.SemaphoreType.DMA((2, 4)),
        pltpu.SemaphoreType.DMA((2, 4)),
        pltpu.SemaphoreType.DMA,
    ]


def gelu_parts(hidden):
    cumulative = 0.5 + 0.5 * lax.erf(hidden * (0.5**0.5))
    decay = jnp.exp2(hidden * hidden * (-0.5 * LOG2E))
    return hidden * cumulative, cumulative + hidden * decay * 0.3989422804014327


def block_forward(masked, pushed, forth, carried, *refs):
    x_ref, w_ref, up_ref, down_ref, vec_ref, bias_ref = refs[:6]
    refs = refs[6:]
    if masked:
        augq_ref, augk_ref = refs[:2]
        refs = refs[2:]
    if carried:
        shard_ref = refs[0]
        refs = refs[1:]
    qkv_ref, soft_ref, rate_ref, att_ref, mid_ref, act_ref, slope_ref, out_ref = refs[:8]
    push = refs[8:]
    if pushed:
        push_begin(carried)
    if carried:
        last_copy = carry_gather(shard_ref, push[0], *push[5:])
        push = push[1:5]
    x = x_ref[0].astype(F32).reshape(WIN, D)
    normed = (normalize(x)[0] * vec_ref[0:1] + vec_ref[1:2]).astype(BF16)
    query = (dot(normed, square(w_ref, 0)) + vec_ref[2:3]) * (SCALE * LOG2E)
    qkv_ref[0, :, 0:D] = query.astype(BF16)
    qkv_ref[0, :, D : 2 * D] = dot(normed, square(w_ref, ROWS)).astype(BF16)
    values = dot(normed, square(w_ref, 2 * ROWS)) + vec_ref[3:4]
    qkv_ref[0, :, 2 * D :] = values.astype(BF16)

    def score(head):
        first = head // 4 * 128
        query4 = qkv_ref[0, :, first : first + 128]
        keys4 = qkv_ref[0, :, D + first : D + first + 128]
        query4 = jnp.where(head_lanes(head % 4), query4, jnp.zeros_like(query4))
        if masked:
            query4 = jnp.concatenate([query4, augq_ref[0]], axis=1)
            keys4 = jnp.concatenate([keys4, augk_ref[0]], axis=1)
        return dot(query4, keys4, NT)

    parts = [None, None]

    def finish(head, soft):
        first = head // 4 * 128
        mine = head_lanes(head % 4)
        values4 = qkv_ref[0, :, 2 * D + first : 2 * D + first + 128]
        values4 = jnp.where(mine, values4, jnp.zeros_like(values4))
        right = jnp.concatenate([values4, jnp.ones((WIN, 128), BF16)], axis=1)
        joined = dot(soft, right)
        rate = 1.0 / joined[:, 128:]
        part = joined[:, :128] * rate
        parts[0] = part if head % 4 == 0 else parts[0] + part
        parts[1] = rate if head % 4 == 0 else jnp.where(mine, rate, parts[1])
        if head % 4 == 3:
            att_ref[0, :, first : first + 128] = parts[0].astype(BF16)
            rate_ref[0, :, first : first + 128] = parts[1]

    total = score(0)
    last = None
    for head in range(HEADS):
        following = score(head + 1) if head < HEADS - 1 else None
        total = total + bias_ref[head]
        soft = jnp.exp2(total - jnp.max(total, axis=1, keepdims=True)).astype(BF16)
        soft_ref[0, head] = soft
        if head > 0:
            finish(head - 1, last)
        last = soft
        total = following
    finish(HEADS - 1, last)
    attended = att_ref[0]
    middle = x_ref[0].astype(F32).reshape(WIN, D)
    middle = middle + dot(attended, square(w_ref, 3 * ROWS)) + vec_ref[4:5]
    mid_ref[0] = middle
    normed = (normalize(middle)[0] * vec_ref[5:6] + vec_ref[6:7]).astype(BF16)
    total = middle + vec_ref[7:8]

    def raise_part(part):
        return dot(normed, square(up_ref, part * ROWS)) + vec_ref[8 + part : 9 + part]

    def lower_part(part, active):
        return dot(active, down_ref[part * 8 : part * 8 + 8].reshape(D, D))

    hidden = raise_part(0)
    last = None
    for part in range(4):
        following = raise_part(part + 1) if part < 3 else None
        lanes = slice(part * D, (part + 1) * D)
        active, slope = gelu_parts(hidden)
        active = active.astype(BF16)
        act_ref[0, :, lanes] = active
        slope_ref[0, :, lanes] = slope.astype(BF16)
        if part > 0:
            total = total + lower_part(part - 1, last)
        last = active
        hidden = following
    total = total + lower_part(3, last)
    if pushed:
        push_window(forth, total, out_ref, *push)
        if carried:
            @pl.when(pl.program_id(0) == pl.num_programs(0) - 1)
            def _():
                last_copy.wait()
    else:
        out_ref[0] = total.reshape(WH, WW, WT, D).astype(out_ref.dtype)


def run_block_forward(layer, x, pack, vec, bias, aug, dtype, pushed, shard):
    windows = x.shape[0] * (x.shape[1] // WH) * (x.shape[2] // WW)
    masked = aug is not None
    extra = list(aug) if masked else []
    carried = shard is not None
    space = [pl.BlockSpec(memory_space=pl.ANY)] if carried else []
    full = [jax.ShapeDtypeStruct((4, 2, 2, 2, 192, D), BF16)] if carried else []
    semaphores = [
        pltpu.SemaphoreType.DMA,
        pltpu.SemaphoreType.DMA((6,)),
        pltpu.SemaphoreType.DMA((6,)),
    ]
    return pl.pallas_call(
        functools.partial(block_forward, masked, pushed, layer == 0, carried),
        grid=(windows,),
        in_specs=[
            grid_spec(x.shape),
            pack_spec(64, 0),
            pack_spec(64, 1),
            pack_spec(64, 2),
            whole_spec(12, D),
            whole_spec(HEADS, WIN, WIN),
        ]
        + [window_spec(WIN, 128)] * len(extra)
        + space,
        out_specs=[
            window_spec(WIN, 3 * D),
            window_spec(HEADS, WIN, WIN),
            window_spec(WIN, D),
            window_spec(WIN, D),
            window_spec(WIN, D),
            window_spec(WIN, FF),
            window_spec(WIN, FF),
            pl.BlockSpec(memory_space=pl.ANY) if pushed else grid_spec(x.shape),
        ]
        + space,
        out_shape=[
            jax.ShapeDtypeStruct((windows, WIN, 3 * D), BF16),
            jax.ShapeDtypeStruct((windows, HEADS, WIN, WIN), BF16),
            jax.ShapeDtypeStruct((windows, WIN, D), F32),
            jax.ShapeDtypeStruct((windows, WIN, D), BF16),
            jax.ShapeDtypeStruct((windows, WIN, D), F32),
            jax.ShapeDtypeStruct((windows, WIN, FF), BF16),
            jax.ShapeDtypeStruct((windows, WIN, FF), BF16),
            jax.ShapeDtypeStruct(x.shape, dtype),
        ]
        + full,
        scratch_shapes=(push_scratch() if pushed else []) + (semaphores if carried else []),
        cost_estimate=cost(windows, 13),
        compiler_params=params(2 + layer if pushed else None),
    )(x, pack, pack, pack, vec, bias, *extra, *([shard] if carried else []))


def norm_back(normal, rate, gained):
    first = jnp.mean(gained, axis=-1, keepdims=True)
    second = jnp.mean(gained * normal, axis=-1, keepdims=True)
    return (gained - first - normal * second) * rate


def feed_backward(
    grad_ref, act_ref, slope_ref, mid_ref, att_ref, in_ref, up_ref, down_ref, vec_ref,
    gmid_ref, gatt_ref, result_ref, gvec_ref, pack_ref,
):
    @pl.when(pl.program_id(0) == 0)
    def _():
        pack_ref[...] = jnp.zeros_like(pack_ref)
        gvec_ref[...] = jnp.zeros_like(gvec_ref)

    count = mid_ref.shape[0]
    each = range(count)
    grads = [
        grad_ref[0, :, WW * w : WW * (w + 1)].astype(F32).reshape(WIN, D) for w in each
    ]
    gvec_ref[3:4] += sum(row_sum(grad) for grad in grads)
    lows = [grad.astype(BF16) for grad in grads]
    normals = [normalize(mid_ref[w]) for w in each]
    gnormed = [jnp.zeros((count * WIN, D), F32)]

    low_all = jnp.concatenate(grads, axis=0).astype(BF16)
    normed_all = jnp.concatenate(
        [normals[w][0] * vec_ref[5:6] + vec_ref[6:7] for w in each], axis=0
    ).astype(BF16)

    def back_part(part):
        return dot(low_all, down_ref[part * 8 : part * 8 + 8].reshape(D, D), NT)

    def finish(part, ghidden):
        first = ROWS * (1 + part)
        total = dot(normed_all, ghidden, TN)
        pack_ref[:, first : first + ROWS, :] += total.reshape(PACKS, ROWS, D)
        gnormed[0] = gnormed[0] + dot(ghidden, square(up_ref, part * ROWS), NT)

    gactive = back_part(0)
    last = None
    for part in range(4):
        following = back_part(part + 1) if part < 3 else None
        lanes = slice(part * D, (part + 1) * D)
        slopes = [slope_ref[w, :, lanes].astype(F32) for w in each]
        ghidden = gactive * jnp.concatenate(slopes, axis=0)
        gvec_ref[4 + part : 5 + part] += row_sum(ghidden)
        ghidden = ghidden.astype(BF16)
        total = sum(dot(act_ref[w, :, lanes], lows[w], TN) for w in each)
        pack_ref[part * 8 : part * 8 + 8, 80:144, :] += total.reshape(8, 64, D)
        if part > 0:
            finish(part - 1, last)
        last = ghidden
        gactive = following
    finish(3, last)
    outer = square(in_ref, 0)
    total = jnp.zeros((D, D), F32)
    gnormed = [gnormed[0][WIN * w : WIN * (w + 1)] for w in each]
    for w in each:
        normal, rate = normals[w]
        gvec_ref[1:2] += row_sum(gnormed[w] * normal)
        gvec_ref[2:3] += row_sum(gnormed[w])
        gmid = grads[w] + norm_back(normal, rate, gnormed[w] * vec_ref[5:6])
        gmid_ref[w] = gmid
        gvec_ref[0:1] += row_sum(gmid)
        gmid_low = gmid.astype(BF16)
        total = total + dot(att_ref[w], gmid_low, TN)
        gatt_ref[w] = dot(gmid_low, outer, NT).astype(BF16)
    pack_ref[:, 0:ROWS, :] += total.reshape(PACKS, ROWS, D)

    @pl.when(pl.program_id(0) == pl.num_programs(0) - 1)
    def _():
        result_ref[...] = pack_ref[...].astype(result_ref.dtype)


def run_feed_backward(layer, grad, active, slope, middle, attended, pack, vec, dtype):
    windows = middle.shape[0]
    count = grad.shape[2] // WW
    row_blocks = grad.shape[1] // WH

    def some(width):
        return pl.BlockSpec((count, WIN, width), lambda i: (i, 0, 0))

    grid_block = pl.BlockSpec(
        (1, WH, count * WW, WT, D), lambda i: (i // row_blocks, i % row_blocks, 0, 0, 0)
    )
    return pl.pallas_call(
        feed_backward,
        grid=(windows // count,),
        in_specs=[
            grid_block,
            some(FF),
            some(FF),
            some(D),
            some(D),
            pack_spec(ROWS, 3),
            pack_spec(64, 1),
            pack_spec(64, 2),
            whole_spec(12, D),
        ],
        out_specs=[
            some(D),
            some(D),
            whole_spec(PACKS, 144, D),
            pl.BlockSpec((8, D), lambda i: (0, 0)),
        ],
        out_shape=[
            jax.ShapeDtypeStruct((windows, WIN, D), F32),
            jax.ShapeDtypeStruct((windows, WIN, D), BF16),
            jax.ShapeDtypeStruct((PACKS, 192, D), dtype),
            jax.ShapeDtypeStruct((8, D), F32),
        ],
        scratch_shapes=[pltpu.VMEM((PACKS, 144, D), F32)],
        cost_estimate=cost(windows, 7),
        compiler_params=params(),
    )(grad, active, slope, middle, attended, pack, pack, pack, vec)


def attention_backward(
    pushed,
    whole_ref, x_ref, gatt_ref, att_ref, rate_ref, soft_ref, qkv_ref, gmid_ref, in_ref, vec_ref,
    out_ref, result_ref, gvec_ref, table_ref,
    pack_ref, sum_s, qt_s, dot_s, gkt_s, gvt_s, gq_s, do_s, wide_s, *push,
):
    step = pl.program_id(0)
    if pushed:
        push_begin(False)

    @pl.when(step == 0)
    def _():
        sum_s[...] = jnp.zeros_like(sum_s)
        pack_ref[...] = jnp.zeros_like(pack_ref)
        gvec_ref[...] = jnp.zeros_like(gvec_ref)

    lane = lax.broadcasted_iota(jnp.int32, (1, 128), 1)
    scaled = (gatt_ref[0].astype(F32) * rate_ref[0]).astype(BF16)
    do_s[...] = scaled
    product = scaled.astype(F32) * att_ref[0].astype(F32)
    gather_row = lax.broadcasted_iota(jnp.int32, (D, 128), 0) // HD
    gather_col = lax.broadcasted_iota(jnp.int32, (D, 128), 1)
    gather = jnp.where(
        (gather_row == gather_col % HEADS) & (gather_col < 3 * HEADS), 1.0, 0.0
    ).astype(BF16)
    high = product.astype(BF16)
    low = (product - high.astype(F32)).astype(BF16)
    inner = dot(high, gather) + dot(low, gather)
    first, second, third = split_three(inner)
    inner = jnp.where(lane < HEADS, first, jnp.where(lane < 2 * HEADS, second, third))
    qt_s[...] = jnp.transpose(qkv_ref[0, :, 0:D].astype(F32)).astype(BF16)
    dot_s[...] = jnp.transpose(scaled.astype(F32)).astype(BF16)
    minus = jnp.broadcast_to(jnp.where(lane < 3 * HEADS, -1.0, 0.0), (WIN, 128)).astype(BF16)
    zero = jnp.zeros((WIN, 128), BF16)

    def score(head):
        first = head // 4 * 128
        grad4 = jnp.where(head_lanes(head % 4), do_s[:, first : first + 128], zero)
        own = jnp.where((lane % HEADS == head) & (lane < 3 * HEADS), inner, zero)
        left = jnp.concatenate([grad4, own], axis=1)
        values4 = qkv_ref[0, :, 2 * D + first : 2 * D + first + 128]
        return dot(left, jnp.concatenate([values4, minus], axis=1), NT)

    parts = [None]

    def finish(head, soft, gtotal):
        first = head // 4 * 128
        rows = slice(head * HD, (head + 1) * HD)
        gvt_s[rows, :] = dot(dot_s[rows, :], soft)
        gkt_s[rows, :] = dot(qt_s[rows, :], gtotal)
        keys4 = qkv_ref[0, :, D + first : D + first + 128]
        part = dot(gtotal, jnp.where(head_lanes(head % 4), keys4, zero))
        parts[0] = part if head % 4 == 0 else parts[0] + part
        if head % 4 == 3:
            gq_s[:, first : first + 128] = parts[0].astype(BF16)

    slope = score(0)
    last = None
    for head in range(HEADS):
        following = score(head + 1) if head < HEADS - 1 else None
        soft = soft_ref[0, head]
        gtotal = soft.astype(F32) * slope
        sum_s[head] += gtotal
        gtotal = gtotal.astype(BF16)
        if head > 0:
            finish(head - 1, *last)
        last = (soft, gtotal)
        slope = following
    finish(HEADS - 1, *last)
    gquery = gq_s[...]
    gkeys = (jnp.transpose(gkt_s[...]) * LN2).astype(BF16)
    gvalues = jnp.transpose(gvt_s[...]).astype(BF16)
    normal, rate = normalize(x_ref[0].astype(F32).reshape(WIN, D))
    normed = (normal * vec_ref[0:1] + vec_ref[1:2]).astype(BF16)
    pack_ref[:, 0:ROWS, :] += (dot(normed, gquery, TN) * SCALE).reshape(PACKS, ROWS, D)
    pack_ref[:, ROWS : 2 * ROWS, :] += dot(normed, gkeys, TN).reshape(PACKS, ROWS, D)
    pack_ref[:, 2 * ROWS :, :] += dot(normed, gvalues, TN).reshape(PACKS, ROWS, D)
    gvec_ref[2:3] += row_sum(gquery.astype(F32)) * SCALE
    gvec_ref[3:4] += row_sum(gvalues.astype(F32))
    gnormed = (
        dot(gquery, square(in_ref, 0), NT) * SCALE
        + dot(gkeys, square(in_ref, ROWS), NT)
        + dot(gvalues, square(in_ref, 2 * ROWS), NT)
    )
    gvec_ref[0:1] += row_sum(gnormed * normal)
    gvec_ref[1:2] += row_sum(gnormed)
    grad = gmid_ref[0] + norm_back(normal, rate, gnormed * vec_ref[0:1])
    if pushed:
        push_window(False, grad, out_ref, *push)
    else:
        out_ref[0] = grad.reshape(WH, WW, WT, D).astype(out_ref.dtype)

    @pl.when(step == pl.num_programs(0) - 1)
    def _():
        result_ref[...] = pack_ref[...].astype(result_ref.dtype)
        table_ref[...] = jnp.zeros_like(table_ref)
        for col in range(WW):
            wide_s[...] = jnp.zeros_like(wide_s)
            for row in range(WH):
                place = (row * WW + col) * WT
                low_lane = (WH - 1 - row) * WW * WT
                wide_s[:, low_lane : low_lane + WIN] += sum_s[:, place : place + WT, :].reshape(
                    HEADS * WT, WIN
                )
            for shift in range(2 * WH - 1):
                low_lane = (shift * (2 * WW - 1) + WW - 1 - col) * WT
                table_ref[:, low_lane : low_lane + WW * WT] += wide_s[
                    :, shift * WW * WT : (shift + 1) * WW * WT
                ]


def run_attention_backward(
    layer, whole, x, gattended, attended, rates, soft, qkv, gmiddle, pack, vec, dtype, pack_dtype, pushed
):
    windows = gmiddle.shape[0]
    return pl.pallas_call(
        functools.partial(attention_backward, pushed),
        grid=(windows,),
        in_specs=[
            pl.BlockSpec(memory_space=pl.ANY),
            grid_spec(x.shape),
            window_spec(WIN, D),
            window_spec(WIN, D),
            window_spec(WIN, D),
            window_spec(HEADS, WIN, WIN),
            window_spec(WIN, 3 * D),
            window_spec(WIN, D),
            pack_spec(48, 0),
            whole_spec(12, D),
        ],
        out_specs=[
            pl.BlockSpec(memory_space=pl.ANY) if pushed else grid_spec(x.shape),
            pack_spec(48, 3),
            pl.BlockSpec((4, D), lambda i: (0, 0)),
            pl.BlockSpec((HEADS * WT, CELLS * WT), lambda i: (0, 0)),
        ],
        out_shape=[
            jax.ShapeDtypeStruct(x.shape, dtype),
            jax.ShapeDtypeStruct((PACKS, 192, D), pack_dtype),
            jax.ShapeDtypeStruct((4, D), F32),
            jax.ShapeDtypeStruct((HEADS * WT, CELLS * WT), F32),
        ],
        scratch_shapes=[
            pltpu.VMEM((PACKS, 48, D), F32),
            pltpu.VMEM((HEADS, WIN, WIN), F32),
            pltpu.VMEM((D, WIN), BF16),
            pltpu.VMEM((D, WIN), BF16),
            pltpu.VMEM((D, WIN), F32),
            pltpu.VMEM((D, WIN), F32),
            pltpu.VMEM((WIN, D), BF16),
            pltpu.VMEM((WIN, D), BF16),
            pltpu.VMEM((HEADS * WT, (2 * WH - 1) * WW * WT), F32),
        ]
        + (push_scratch() if pushed else []),
        cost_estimate=cost(windows, 12),
        compiler_params=params(4 if pushed else None),
        input_output_aliases={0: 1},
    )(whole, x, gattended, attended, rates, soft, qkv, gmiddle, pack, vec)


def expand_bias(cells_ref, out_ref, wide_s):
    for col in range(WW):
        for shift in range(2 * WH - 1):
            low_lane = (shift * (2 * WW - 1) + WW - 1 - col) * WT
            wide_s[:, shift * WW * WT : (shift + 1) * WW * WT] = cells_ref[
                :, low_lane : low_lane + WW * WT
            ]
        for row in range(WH):
            place = (row * WW + col) * WT
            low_lane = (WH - 1 - row) * WW * WT
            out_ref[:, place : place + WT, :] = wide_s[:, low_lane : low_lane + WIN].reshape(
                HEADS, WT, WIN
            )


def run_expand_bias(cells):
    return pl.pallas_call(
        expand_bias,
        out_shape=jax.ShapeDtypeStruct((HEADS, WIN, WIN), F32),
        scratch_shapes=[pltpu.VMEM((HEADS * WT, (2 * WH - 1) * WW * WT), F32)],
        compiler_params=pltpu.CompilerParams(vmem_limit_bytes=61 * 1024 * 1024),
    )(cells)


AUX_ROWS = 8
SHARES = ((1, 0, AUX_ROWS, 0), (0, 0, 48, 0), (0, 48, 48, 1), (0, 96, 48, 0), (0, 144, 48, 1))


def fold_gradients(*refs):
    operands = refs[:2]
    pack_out, aux_out = refs[2:4]
    buffers = refs[4:19]
    send_sem, recv_sem, wide_send, wide_recv = refs[19:]
    batch = lax.axis_index("batch")
    y = lax.axis_index("seq")
    z, x, core = batch // 4, (batch // 2) % 2, batch % 2
    count = len(SHARES)

    def device(z_to, x_to, core_to, y_to):
        return ((z_to * 2 + x_to) * 2 + core_to, y_to)

    barrier = pltpu.get_barrier_semaphore()

    def greet(k, carry):
        other = lax.rem(batch * 2 + y + k, 32)
        pl.semaphore_signal(
            barrier, inc=1, device_id=(other // 2, other % 2), device_id_type=pl.DeviceIdType.MESH
        )
        return carry

    lax.fori_loop(1, 32, greet, 0)
    pl.semaphore_wait(barrier, 31)

    def send(number, source, target, to):
        copy = pltpu.make_async_remote_copy(
            src_ref=source,
            dst_ref=target,
            send_sem=send_sem.at[number],
            recv_sem=recv_sem.at[number],
            device_id=to,
            device_id_type=pl.DeviceIdType.MESH,
        )
        copy.start()
        return copy

    copies = []
    for k, (which, first, size, order) in enumerate(SHARES):
        source = operands[which].at[:, :, 1 - core, :, pl.ds(first, size), :]
        copies.append(send(k, source, buffers[3 * k], device(z, x, 1 - core, y)))
    for k, (which, first, size, order) in enumerate(SHARES):
        copies[k].wait()
        held = buffers[3 * k]

        def add_core(i, carry, which=which, first=first, size=size, held=held):
            a, b = i // 2, i % 2
            mine = operands[which][a, b, core, :, first : first + size, :].astype(F32)
            held[a, b] = (held[a, b].astype(F32) + mine).astype(held.dtype)
            return carry

        lax.fori_loop(0, 8, add_core, 0)
        if order == 0:
            copies.append(send(count + k, held.at[:, 1 - x], buffers[3 * k + 1], device(z, 1 - x, core, y)))
        else:
            copies.append(send(count + k, held.at[:, :, 1 - y], buffers[3 * k + 1], device(z, x, core, 1 - y)))
    for k, (which, first, size, order) in enumerate(SHARES):
        copies[count + k].wait()
        before, held = buffers[3 * k], buffers[3 * k + 1]

        def add_next(i, carry, order=order, before=before, held=held):
            a, b = i // 2, i % 2
            mine = before[a, x, b] if order == 0 else before[a, b, y]
            held[a, b] = (held[a, b].astype(F32) + mine.astype(F32)).astype(held.dtype)
            return carry

        lax.fori_loop(0, 8, add_next, 0)
        if order == 0:
            copies.append(send(2 * count + k, held.at[:, 1 - y], buffers[3 * k + 2].at[pl.ds(0, 4)], device(z, x, core, 1 - y)))
        else:
            copies.append(send(2 * count + k, held.at[:, 1 - x], buffers[3 * k + 2].at[pl.ds(0, 4)], device(z, 1 - x, core, y)))
    far = []
    for k, (which, first, size, order) in enumerate(SHARES):
        copies[2 * count + k].wait()
        before, held = buffers[3 * k + 1], buffers[3 * k + 2]

        def add_last(a, carry, order=order, before=before, held=held):
            mine = before[a, y] if order == 0 else before[a, x]
            held[a] = (held[a].astype(F32) + mine.astype(F32)).astype(held.dtype)
            return carry

        lax.fori_loop(0, 4, add_last, 0)
        for step in range(1, 4):
            other = lax.rem(z + step, 4)
            far.append(
                send(
                    3 * count + 3 * k + step - 1,
                    held.at[other],
                    held.at[3 + step],
                    device(other, x, core, y),
                )
            )
    def spread(k, carry):
        other = lax.rem(batch * 2 + y + k, 32)
        pltpu.make_async_remote_copy(
            src_ref=aux_out.at[batch * 2 + y],
            dst_ref=aux_out.at[batch * 2 + y],
            send_sem=wide_send,
            recv_sem=wide_recv,
            device_id=(other // 2, other % 2),
            device_id_type=pl.DeviceIdType.MESH,
        ).start()
        return carry

    for k, (which, first, size, order) in enumerate(SHARES):
        for step in range(1, 4):
            far[3 * k + step - 1].wait()
        held = buffers[3 * k + 2]
        total = held[z].astype(F32) + held[4].astype(F32)
        total = total + held[5].astype(F32) + held[6].astype(F32)
        if which == 0:
            pack_out[first : first + size, :] = total
        else:
            aux_out[batch * 2 + y] = total

    lax.fori_loop(1, 32, spread, 0)
    others = aux_out.at[pl.ds(0, 31)]
    pltpu.make_async_copy(others, others, wide_send).wait()
    pltpu.make_async_copy(others, others, wide_recv).wait()


def run_fold_gradients(big, aux):
    operands = [value.reshape((4, 2, 2, 2) + value.shape[1:]) for value in (big, aux)]
    scratch = []
    for which, first, size, order in SHARES:
        dtype = operands[which].dtype
        scratch.append(pltpu.VMEM((4, 2, 2, size, D), dtype))
        scratch.append(pltpu.VMEM((4, 2, size, D), dtype))
        scratch.append(pltpu.VMEM((7, size, D), dtype))
    semaphores = 6 * len(SHARES)
    return pl.pallas_call(
        fold_gradients,
        in_specs=[pl.BlockSpec(memory_space=pltpu.VMEM)] * 2,
        out_specs=[pl.BlockSpec(memory_space=pltpu.VMEM)] * 2,
        out_shape=[
            jax.ShapeDtypeStruct((192, D), F32),
            jax.ShapeDtypeStruct((32, AUX_ROWS, D), F32),
        ],
        scratch_shapes=scratch
        + [
            pltpu.SemaphoreType.DMA((semaphores,)),
            pltpu.SemaphoreType.DMA((semaphores,)),
            pltpu.SemaphoreType.DMA,
            pltpu.SemaphoreType.DMA,
        ],
        cost_estimate=cost(1, 1),
        compiler_params=pltpu.CompilerParams(
            vmem_limit_bytes=61 * 1024 * 1024, collective_id=1, has_side_effects=True
        ),
    )(*operands)


def offset_places():
    frame, row, col = np.meshgrid(
        np.arange(1 - WT, WT), np.arange(1 - WH, WH), np.arange(1 - WW, WW), indexing="ij"
    )

    def place(f, r, c):
        return (np.maximum(f, 0) * WH + np.maximum(r, 0)) * WW + np.maximum(c, 0)

    return (place(frame, row, col) * WIN + place(-frame, -row, -col)).reshape(-1)[::-1].copy()


def interleave():
    cell = np.arange(CELLS * WT)
    source = jnp.asarray((cell % WT) * CELLS + cell // WT, jnp.int32)
    order = jnp.arange(CELLS * WT, dtype=jnp.int32)
    return (order[:, None] == source[None, :]).astype(BF16)


def join_three(values, axis):
    first, second, third = jnp.split(values, 3, axis=axis)
    return first + second + third


def bias_cells(tables, chosen, order):
    flat = jnp.concatenate([tables[layer] for layer in range(LAYERS)], axis=1) * LOG2E
    pieces = jnp.concatenate(split_three(flat), axis=1)
    taken = dot(pieces, chosen, (((0,), (1,)), ((), ()))).astype(BF16)
    placed = jnp.stack(
        [taken[:, (WT - 1 - t) * CELLS : (2 * WT - 1 - t) * CELLS] for t in range(WT)], axis=1
    )
    cells = dot(placed.reshape(-1, WT * CELLS), order)
    return join_three(cells, 0).reshape(LAYERS, HEADS * WT, CELLS * WT)


def cells_to_rows(cells, order):
    pieces = jnp.concatenate(split_three(cells.reshape(-1, CELLS * WT)), axis=0)
    placed = join_three(dot(pieces, order, NT), 0).reshape(LAYERS * HEADS, WT, CELLS * WT)
    parts = [
        jnp.pad(placed[:, t], ((0, 0), ((WT - 1 - t) * CELLS, t * CELLS))) for t in range(WT)
    ]
    return functools.reduce(jnp.add, parts)


def rows_to_table(rows, chosen):
    pieces = jnp.concatenate(split_three(rows), axis=0)
    total = join_three(dot(chosen, pieces, (((0,), (1,)), ((), ()))), 1)
    return jnp.stack([total[:, i * HEADS : (i + 1) * HEADS] for i in range(LAYERS)])


def spatial_blocks(field):
    clip_count, frames_here, width = (field.shape[0], field.shape[1], field.shape[-1])
    shaped = field.reshape(clip_count, frames_here, HGT // WH, WH, WID // WW, WW, width)
    shaped = shaped.transpose(0, 2, 4, 1, 3, 5, 6)
    return shaped.reshape(clip_count * (HGT // WH) * (WID // WW), frames_here, WH * WW, width)


def roll_space(field, amount, first):
    return jnp.roll(field, (amount, amount), axis=(first, first + 1))


def swap_halves(part):
    return lax.ppermute(part, "seq", [(0, 1), (1, 0)])


class Placement:
    def __init__(self, clip_count, frames_here):
        self.clips = clip_count
        self.frames = frames_here
        self.parts = lax.axis_size("seq")
        self.near = self.parts == 2 and frames_here == WT

    def grid_shape(self):
        if self.near:
            return (self.clips, HGT, WID, WT, D)
        columns = self.clips * 4 // self.parts
        return (columns * 2, WH, WW, WT, D)

    def enter(self, field, shifted):
        if self.near:
            if shifted:
                arrived = swap_halves(field[:, :SHIFT_T])
                field = jnp.concatenate([field[:, SHIFT_T:], arrived], axis=1)
                field = roll_space(field, -SHIFT_S, 2)
            return field.transpose(0, 2, 3, 1, 4)
        if shifted:
            field = roll_space(field, -SHIFT_S, 2)
        columns = lax.all_to_all(
            spatial_blocks(field), "seq", split_axis=0, concat_axis=1, tiled=True
        )
        if shifted:
            columns = jnp.roll(columns, -SHIFT_T, axis=1)
        windows = columns.reshape(-1, WT, WH, WW, D)
        return windows.transpose(0, 2, 3, 1, 4)

    def leave(self, grid, shifted):
        if self.near:
            field = grid.transpose(0, 3, 1, 2, 4)
            if shifted:
                field = roll_space(field, SHIFT_S, 2)
                arrived = swap_halves(field[:, SHIFT_T:])
                field = jnp.concatenate([arrived, field[:, :SHIFT_T]], axis=1)
            return field
        columns = grid.transpose(0, 3, 1, 2, 4).reshape(-1, FRAMES, WH * WW, D)
        if shifted:
            columns = jnp.roll(columns, SHIFT_T, axis=1)
        columns = lax.all_to_all(columns, "seq", split_axis=1, concat_axis=0, tiled=True)
        shaped = columns.reshape(self.clips, HGT // WH, WID // WW, self.frames, WH, WW, D)
        shaped = shaped.transpose(0, 3, 1, 4, 2, 5, 6)
        field = shaped.reshape(self.clips, self.frames, HGT, WID, D)
        return roll_space(field, SHIFT_S, 2) if shifted else field

    def forth(self, grid):
        return self.enter(self.leave(grid, False), True)

    def back(self, grid):
        return self.enter(self.leave(grid, True), False)

    def mask_lanes(self):
        if self.near:
            index = jnp.arange(self.clips * 4, dtype=jnp.int32)
            late = jnp.full(index.shape, lax.axis_index("seq"), jnp.int32)
            block = index % 4
        else:
            columns = self.clips * 4 // self.parts
            index = jnp.arange(columns * 2, dtype=jnp.int32)
            late = index % 2
            block = (lax.axis_index("seq") * columns + index // 2) % 4
        place = np.arange(WIN)
        frame_late = jnp.asarray(place % WT >= WT - SHIFT_T).astype(jnp.int32)
        row_late = jnp.asarray(place // (WT * WW) >= WH - SHIFT_S).astype(jnp.int32)
        col_late = jnp.asarray(place // WT % WW >= WW - SHIFT_S).astype(jnp.int32)
        region = (
            late[:, None] * frame_late * 4
            + (block // 2)[:, None] * row_late * 2
            + (block % 2)[:, None] * col_late
        )
        lane = np.arange(128)
        same = (region[:, :, None] == lane % 8) & (lane < 24)
        pieces = []
        rest = np.float32(MASKED * LOG2E)
        for _ in range(3):
            piece = np.float32(np.asarray(rest).astype(BF16))
            pieces.append(piece)
            rest = np.float32(rest - piece)
        piece_of = np.zeros((128,), np.float32)
        for number, piece in enumerate(pieces):
            piece_of[8 * number : 8 * number + 8] = -piece
            piece_of[24 + number] = piece
        always = (lane >= 24) & (lane < 27)
        on_keys = jnp.where(same | always, 1.0, 0.0)
        return (on_keys * piece_of).astype(BF16), on_keys.astype(BF16)


def pack_layer(inner, outer, up, down):
    parts = [inner[:, i * D : (i + 1) * D] for i in range(3)] + [outer]
    parts = parts + [up[:, i * D : (i + 1) * D] for i in range(4)] + [down]
    return jnp.concatenate(parts, axis=0)


def per_device(
    clips_in,
    cotangent,
    offset_index,
    first_gain,
    first_shift,
    inner_weight,
    inner_bias,
    outer_weight,
    outer_bias,
    second_gain,
    second_shift,
    up_weight,
    up_bias,
    down_weight,
    down_bias,
    bias_table,
):
    place = Placement(clips_in.shape[0], clips_in.shape[1])
    rows = inner_weight.shape[1]
    devices = D // rows
    vectors = [
        first_gain, first_shift, inner_bias, outer_bias, second_gain, second_shift,
        down_bias, up_bias,
    ]
    vec_pack = jnp.concatenate(vectors, axis=1)
    width = vec_pack.shape[1]
    vec_rows = jnp.pad(vec_pack, ((0, 14), (0, D - width)))
    local = [
        pack_layer(inner_weight[layer], outer_weight[layer], up_weight[layer], down_weight[layer])
        for layer in range(LAYERS)
    ]
    folded = lax.axis_size("batch") == 16 and lax.axis_size("seq") == 2
    shape = place.grid_shape()
    carried = folded and place.near and shape[0] == 2
    first_part = [local[0], vec_rows] if carried else local + [vec_rows]
    full = lax.all_gather(jnp.concatenate(first_part, axis=0), AXES, axis=0)
    vecs = []
    for layer in range(LAYERS):
        held = full[:, full.shape[1] - 16 + layer, :width].astype(F32)
        pieces = []
        start = 0
        for vector in vectors:
            size = vector.shape[1]
            pieces.append(held[:, start : start + size].reshape(-1, D))
            start += size
        vecs.append(jnp.concatenate(pieces, axis=0))
    packs = [full, None]
    if not carried:
        for layer in range(LAYERS):
            parts = []
            first = 12 * rows * layer
            for i in range(8):
                part = full[:, first + i * rows : first + (i + 1) * rows]
                parts.append(part.reshape(PACKS, ROWS, D))
            part = full[:, first + 8 * rows : first + 12 * rows]
            parts.append(part.reshape(PACKS, 4 * ROWS, D))
            packs[layer] = jnp.concatenate(parts, axis=1)
    taken_rows = jnp.take(offset_index.reshape(-1), offset_places())
    order = jnp.arange(BIAS_ROWS, dtype=jnp.int32)
    chosen = (taken_rows[:, None] == order[None, :]).astype(BF16)
    interleaved = interleave()
    cells_in = bias_cells(bias_table, chosen, interleaved)
    bias = [run_expand_bias(cells_in[layer]) for layer in range(LAYERS)]
    aug = place.mask_lanes()

    x_zero = place.enter(clips_in, False)
    upstream = place.enter(cotangent, True)
    saved = []
    x = x_zero
    for layer in range(LAYERS):
        outs = run_block_forward(
            layer, x, packs[layer], vecs[layer], bias[layer], aug if layer == 1 else None,
            F32 if layer == 0 or place.near else BF16, place.near,
            local[1] if carried and layer == 0 else None,
        )
        qkv, soft, rates, attended, middle, active, slope, result = outs[:8]
        if carried and layer == 0:
            packs[1] = outs[8].reshape(PACKS, 192, D)
        saved.append((x, qkv, soft, rates, attended, middle, active, slope))
        x = place.forth(result) if layer == 0 and not place.near else result
    clips_out = place.leave(x, not place.near).astype(BF16)

    scattered = [None] * LAYERS
    vec_parts = [None] * LAYERS
    cell_parts = [None] * LAYERS

    def scatter(value, blocks):
        if rows != ROWS:
            per = ROWS // rows
            parts = []
            start = 0
            for size in blocks:
                part = value[:, start : start + size].reshape(PACKS * per, size // per, D)
                parts.append(part)
                start += size
            value = jnp.concatenate(parts, axis=1)
        return lax.psum_scatter(value, AXES, scatter_dimension=0, tiled=False)

    for layer in reversed(range(LAYERS)):
        pack, vec = packs[layer], vecs[layer]
        x, qkv, soft, rates, attended, middle, active, slope = saved[layer]
        gmiddle, gattended, big, gvec_two = run_feed_backward(
            layer, upstream, active, slope, middle, attended, pack, vec, BF16 if folded else F32
        )
        upstream, big, gvec_one, cells = run_attention_backward(
            layer, big, x, gattended, attended, rates, soft, qkv, gmiddle, pack, vec,
            F32 if layer == 1 else BF16, BF16 if folded else F32,
            place.near and layer == 1,
        )
        if layer == 1 or not folded:
            scattered[layer] = scatter(big, [ROWS] * 5 + [4 * ROWS] + [ROWS] * 3)
        vec_parts[layer] = jnp.concatenate([gvec_one, gvec_two], axis=0)
        cell_parts[layer] = cells
        if layer == 1 and not place.near:
            upstream = place.back(upstream)
    clips_grad = place.leave(upstream, False)

    table_rows = cells_to_rows(jnp.stack(cell_parts), interleaved)
    vec_stack = jnp.stack(vec_parts)
    if folded:
        aux = jnp.concatenate([table_rows.reshape(-1), vec_stack.reshape(-1)])
        used = aux.shape[0]
        aux = jnp.pad(aux, (0, PACKS * AUX_ROWS * D - used)).reshape(PACKS, AUX_ROWS, D)
        big, scattered[1] = lax.optimization_barrier((big, scattered[1]))
        scattered[0], aux = run_fold_gradients(big, aux)
        aux = aux.reshape(-1)[:used]
        table_total = aux[: table_rows.size].reshape(table_rows.shape)
        vec_total = aux[table_rows.size :].reshape(vec_stack.shape)
    else:
        vec_total, table_total = lax.psum((vec_stack, table_rows), AXES)
    table_total = rows_to_table(table_total, chosen)

    scattered = [value.astype(F32) for value in scattered]
    device = lax.axis_index(AXES)

    def own(first, count):
        whole = vec_total[:, first : first + count].reshape(LAYERS, count * D)
        size = count * D // devices
        return lax.dynamic_slice_in_dim(whole, device * size, size, axis=1)

    def both(first, count):
        parts = []
        for layer in range(LAYERS):
            value = scattered[layer]
            columns = [
                value[first + i * rows : first + (i + 1) * rows] for i in range(count)
            ]
            parts.append(jnp.concatenate(columns, axis=1))
        return jnp.stack(parts)

    down = jnp.stack([scattered[layer][5 * rows : 9 * rows] for layer in range(LAYERS)])
    return (
        clips_out,
        clips_grad,
        own(0, 1),
        own(1, 1),
        both(9 * rows, 3),
        own(2, 2),
        both(0, 1),
        own(4, 1),
        own(5, 1),
        own(6, 1),
        both(rows, 4),
        own(8, 4),
        down,
        own(7, 1),
        table_total,
    )


def solution(mesh):
    clips = P("batch", "seq", None, None, None)
    vector = P(None, AXES)
    matrix = P(None, AXES, None)
    return jax.shard_map(
        per_device,
        mesh=mesh,
        in_specs=(
            clips, clips, P(), vector, vector, matrix, vector, matrix, vector, vector, vector,
            matrix, vector, matrix, vector, P(),
        ),
        out_specs=(
            clips, clips, vector, vector, matrix, vector, matrix, vector, vector, vector,
            matrix, vector, matrix, vector, P(),
        ),
        check_vma=False,
    )
```

```python
import functools

import jax
import jax.numpy as jnp
import numpy as np
from jax import lax
from jax.experimental import pallas as pl
from jax.experimental.pallas import tpu as pltpu
from jax.sharding import PartitionSpec as P

D = 512
HEADS = 16
HD = 32
FF = 2048
WT = 8
WH = 7
WW = 7
FRAMES = 16
HGT = 14
WID = 14
LAYERS = 2
SHIFT_T = 4
SHIFT_S = 3
WIN = 392
BIAS_ROWS = 2535
ROWS = 16
PACKS = D // ROWS
CELLS = (2 * WH - 1) * (2 * WW - 1)

EPSILON = 1e-05
MASKED = -100.0
LOG2E = 1.4426950408889634
LN2 = 0.6931471805599453
SCALE = HD**-0.5

BF16 = jnp.bfloat16
F32 = jnp.float32
AXES = ("batch", "seq")

NT = (((1,), (1,)), ((), ()))
TN = (((0,), (0,)), ((), ()))


def params(collective=None):
    return pltpu.CompilerParams(
        vmem_limit_bytes=61 * 1024 * 1024,
        dimension_semantics=("arbitrary",),
        collective_id=collective,
        has_side_effects=collective is not None,
    )


def cost(windows, microseconds):
    return pl.CostEstimate(
        flops=int(windows * microseconds * 2e8), bytes_accessed=0, transcendentals=0
    )


def dot(left, right, dims=(((1,), (0,)), ((), ()))):
    return lax.dot_general(left, right, dims, preferred_element_type=F32)


def normalize(values):
    average = jnp.mean(values, axis=-1, keepdims=True)
    centred = values - average
    rate = lax.rsqrt(jnp.mean(centred * centred, axis=-1, keepdims=True) + EPSILON)
    return centred * rate, rate


def row_sum(values):
    return jnp.sum(values, axis=0, keepdims=True)


def split_three(values):
    high = values.astype(BF16)
    rest = values - high.astype(F32)
    middle = rest.astype(BF16)
    low = (rest - middle.astype(F32)).astype(BF16)
    return high, middle, low


def square(ref, first):
    return ref[:, first : first + ROWS, :].reshape(D, D)


def grid_spec(shape):
    row_blocks, col_blocks = shape[1] // WH, shape[2] // WW
    per_clip = row_blocks * col_blocks
    return pl.BlockSpec(
        (1, WH, WW, WT, D),
        lambda i: (i // per_clip, (i % per_clip) // col_blocks, i % col_blocks, 0, 0),
    )


def window_spec(*tail):
    return pl.BlockSpec((1,) + tail, lambda i: (i,) + (0,) * len(tail))


def whole_spec(*shape):
    return pl.BlockSpec(shape, lambda i: (0,) * len(shape), pipeline_mode=pl.Buffered(1))


def pack_spec(rows, index):
    return pl.BlockSpec(
        (PACKS, rows, D), lambda i: (0, index, 0), pipeline_mode=pl.Buffered(1)
    )


def head_lanes(which):
    lane = lax.broadcasted_iota(jnp.int32, (1, 128), 1)
    return (lane // HD) == which


def lane_slice(group, base=0):
    return pl.ds(pl.multiple_of(base + group * 128, 128), 128)


def neighbour():
    return (lax.axis_index("batch"), 1 - lax.axis_index("seq"))


def piece_places(forth, block):
    if forth:
        return ((0, 3, lax.rem(7 * block + 11, 14)), (3, 4, 7 * block))
    return ((0, 4, 7 * block + 3), (4, 3, lax.rem(7 * block + 7, 14)))


def window_copies(forth, step, slot, stage, out_ref, own_sem, send_sem, recv_sem):
    clip, row_block, col_block = step // 4, (step // 2) % 2, step % 2
    kept, kept_to, sent, sent_to = (4, 0, 0, 4) if forth else (0, 4, 4, 0)
    copies = []
    number = 0
    for row, rows, row_to in piece_places(forth, row_block):
        for col, cols, col_to in piece_places(forth, col_block):

            def place(frame, row_to=row_to, rows=rows, col_to=col_to, cols=cols):
                return out_ref.at[
                    clip, pl.ds(row_to, rows), pl.ds(col_to, cols), pl.ds(frame, 4), :
                ]

            def held(frame, row=row, rows=rows, col=col, cols=cols):
                return stage.at[
                    slot, pl.ds(row, rows), pl.ds(col, cols), pl.ds(frame, 4), :
                ]

            copies.append(
                pltpu.make_async_copy(held(kept), place(kept_to), own_sem.at[slot, number])
            )
            copies.append(
                pltpu.make_async_remote_copy(
                    src_ref=held(sent),
                    dst_ref=place(sent_to),
                    send_sem=send_sem.at[slot, number],
                    recv_sem=recv_sem,
                    device_id=neighbour(),
                    device_id_type=pl.DeviceIdType.MESH,
                )
            )
            number += 1
    return copies


def wait_left(copies):
    for number, copy in enumerate(copies):
        if number % 2 == 0:
            copy.wait()
        else:
            copy.wait_send()


def own_place():
    batch = lax.axis_index("batch")
    return batch // 4, (batch // 2) % 2, batch % 2, lax.axis_index("seq")


def device_at(z, x, core, y):
    return ((z * 2 + x) * 2 + core, y)


def push_begin(carried):
    @pl.when(pl.program_id(0) == 0)
    def _():
        barrier = pltpu.get_barrier_semaphore()
        peers = [neighbour()]
        if carried:
            z, x, core, y = own_place()
            peers += [device_at(lax.rem(z + i, 4), x, core, y) for i in range(1, 4)]
            peers += [device_at(z, 1 - x, core, y), device_at(z, x, 1 - core, y)]
        for peer in peers:
            pl.semaphore_signal(
                barrier, inc=1, device_id=peer, device_id_type=pl.DeviceIdType.MESH
            )
        pl.semaphore_wait(barrier, len(peers))


def carry_gather(shard_ref, full_ref, shard_sem, send_sem, recv_sem):
    step = pl.program_id(0)
    z, x, core, y = own_place()
    mine = full_ref.at[z, x, core, y]
    keep = pltpu.make_async_copy(shard_ref, mine, shard_sem)

    def send(number, source, target, to):
        return pltpu.make_async_remote_copy(
            src_ref=source,
            dst_ref=target,
            send_sem=send_sem.at[number],
            recv_sem=recv_sem.at[number],
            device_id=to,
            device_id_type=pl.DeviceIdType.MESH,
        )

    top, bottom = pl.ds(0, 96), pl.ds(96, 96)
    top_pair = full_ref.at[z, x, core, :, top, :]
    low_pair = full_ref.at[z, x, core, :, bottom, :]
    top_line = full_ref.at[:, x, core, :, top, :]
    low_both = full_ref.at[z, :, core, :, bottom, :]
    half = full_ref.at[:, :, core]
    over_y = send(0, shard_ref, mine, device_at(z, x, core, 1 - y))
    levels = [device_at(lax.rem(z + i, 4), x, core, y) for i in range(1, 4)]
    top_z = [send(1 + i, top_pair, top_pair, to) for i, to in enumerate(levels)]
    low_x = send(4, low_pair, low_pair, device_at(z, 1 - x, core, y))
    top_x = send(5, top_line, top_line, device_at(z, 1 - x, core, y))
    low_z = [send(6 + i, low_both, low_both, to) for i, to in enumerate(levels)]
    over_core = send(9, half, half, device_at(z, x, 1 - core, y))

    @pl.when(step == 0)
    def _():
        keep.start()
        over_y.start()

    @pl.when(step == 1)
    def _():
        keep.wait()
        over_y.wait()
        low_x.start()
        for copy in top_z:
            copy.start()

    @pl.when(step == 3)
    def _():
        low_x.wait()
        for copy in low_z:
            copy.start()
        for copy in top_z:
            copy.wait()
        top_x.start()

    @pl.when(step == 6)
    def _():
        for copy in low_z:
            copy.wait()
        top_x.wait()
        over_core.start()

    return over_core


def push_window(forth, value, out_ref, stage, own_sem, send_sem, recv_sem):
    step = pl.program_id(0)
    slot = lax.rem(step, 2)
    rest = (stage, out_ref, own_sem, send_sem, recv_sem)

    @pl.when(step >= 2)
    def _():
        wait_left(window_copies(forth, step - 2, slot, *rest))

    stage[slot] = value.reshape(WH, WW, WT, D)
    for copy in window_copies(forth, step, slot, *rest):
        copy.start()

    @pl.when(step == pl.num_programs(0) - 1)
    def _():
        wait_left(window_copies(forth, step - 1, 1 - slot, *rest))
        wait_left(window_copies(forth, step, slot, *rest))
        half = out_ref.at[:, :, :, pl.ds(4 if forth else 0, 4), :]
        pltpu.make_async_copy(half, half, recv_sem).wait()


def push_scratch():
    return [
        pltpu.VMEM((2, WH, WW, WT, D), F32),
        pltpu.SemaphoreType.DMA((2, 4)),
        pltpu.SemaphoreType.DMA((2, 4)),
        pltpu.SemaphoreType.DMA,
    ]


def gelu_parts(hidden):
    cumulative = 0.5 + 0.5 * lax.erf(hidden * (0.5**0.5))
    decay = jnp.exp2(hidden * hidden * (-0.5 * LOG2E))
    return hidden * cumulative, cumulative + hidden * decay * 0.3989422804014327


def block_forward(masked, pushed, forth, carried, *refs):
    x_ref, w_ref, up_ref, down_ref, vec_ref, bias_ref = refs[:6]
    refs = refs[6:]
    if masked:
        augq_ref, augk_ref = refs[:2]
        refs = refs[2:]
    if carried:
        shard_ref = refs[0]
        refs = refs[1:]
    qkv_ref, soft_ref, rate_ref, att_ref, mid_ref, act_ref, slope_ref, out_ref = refs[:8]
    push = refs[8:]
    if pushed:
        push_begin(carried)
    if carried:
        last_copy = carry_gather(shard_ref, push[0], *push[5:])
        push = push[1:5]
    x = x_ref[0].astype(F32).reshape(WIN, D)
    normed = (normalize(x)[0] * vec_ref[0:1] + vec_ref[1:2]).astype(BF16)
    query = (dot(normed, square(w_ref, 0)) + vec_ref[2:3]) * (SCALE * LOG2E)
    qkv_ref[0, :, 0:D] = query.astype(BF16)
    qkv_ref[0, :, D : 2 * D] = dot(normed, square(w_ref, ROWS)).astype(BF16)
    values = dot(normed, square(w_ref, 2 * ROWS)) + vec_ref[3:4]
    qkv_ref[0, :, 2 * D :] = values.astype(BF16)

    def score(head):
        first = head // 4 * 128
        query4 = qkv_ref[0, :, first : first + 128]
        keys4 = qkv_ref[0, :, D + first : D + first + 128]
        query4 = jnp.where(head_lanes(head % 4), query4, jnp.zeros_like(query4))
        if masked:
            query4 = jnp.concatenate([query4, augq_ref[0]], axis=1)
            keys4 = jnp.concatenate([keys4, augk_ref[0]], axis=1)
        return dot(query4, keys4, NT)

    parts = [None, None]

    def finish(head, soft):
        first = head // 4 * 128
        mine = head_lanes(head % 4)
        values4 = qkv_ref[0, :, 2 * D + first : 2 * D + first + 128]
        values4 = jnp.where(mine, values4, jnp.zeros_like(values4))
        right = jnp.concatenate([values4, jnp.ones((WIN, 128), BF16)], axis=1)
        joined = dot(soft, right)
        rate = 1.0 / joined[:, 128:]
        part = joined[:, :128] * rate
        parts[0] = part if head % 4 == 0 else parts[0] + part
        parts[1] = rate if head % 4 == 0 else jnp.where(mine, rate, parts[1])
        if head % 4 == 3:
            att_ref[0, :, first : first + 128] = parts[0].astype(BF16)
            rate_ref[0, :, first : first + 128] = parts[1]

    total = score(0)
    last = None
    for head in range(HEADS):
        following = score(head + 1) if head < HEADS - 1 else None
        total = total + bias_ref[head]
        soft = jnp.exp2(total - jnp.max(total, axis=1, keepdims=True)).astype(BF16)
        soft_ref[0, head] = soft
        if head > 0:
            finish(head - 1, last)
        last = soft
        total = following
    finish(HEADS - 1, last)
    attended = att_ref[0]
    middle = x_ref[0].astype(F32).reshape(WIN, D)
    middle = middle + dot(attended, square(w_ref, 3 * ROWS)) + vec_ref[4:5]
    mid_ref[0] = middle
    normed = (normalize(middle)[0] * vec_ref[5:6] + vec_ref[6:7]).astype(BF16)
    total = middle + vec_ref[7:8]

    def raise_part(part):
        return dot(normed, square(up_ref, part * ROWS)) + vec_ref[8 + part : 9 + part]

    def lower_part(part, active):
        return dot(active, down_ref[part * 8 : part * 8 + 8].reshape(D, D))

    hidden = raise_part(0)
    last = None
    for part in range(4):
        following = raise_part(part + 1) if part < 3 else None
        lanes = slice(part * D, (part + 1) * D)
        active, slope = gelu_parts(hidden)
        active = active.astype(BF16)
        act_ref[0, :, lanes] = active
        slope_ref[0, :, lanes] = slope.astype(BF16)
        if part > 0:
            total = total + lower_part(part - 1, last)
        last = active
        hidden = following
    total = total + lower_part(3, last)
    if pushed:
        push_window(forth, total, out_ref, *push)
        if carried:
            @pl.when(pl.program_id(0) == pl.num_programs(0) - 1)
            def _():
                last_copy.wait()
    else:
        out_ref[0] = total.reshape(WH, WW, WT, D).astype(out_ref.dtype)


def run_block_forward(layer, x, pack, vec, bias, aug, dtype, pushed, shard):
    windows = x.shape[0] * (x.shape[1] // WH) * (x.shape[2] // WW)
    masked = aug is not None
    extra = list(aug) if masked else []
    carried = shard is not None
    space = [pl.BlockSpec(memory_space=pl.ANY)] if carried else []
    full = [jax.ShapeDtypeStruct((4, 2, 2, 2, 192, D), BF16)] if carried else []
    semaphores = [
        pltpu.SemaphoreType.DMA,
        pltpu.SemaphoreType.DMA((10,)),
        pltpu.SemaphoreType.DMA((10,)),
    ]
    return pl.pallas_call(
        functools.partial(block_forward, masked, pushed, layer == 0, carried),
        grid=(windows,),
        in_specs=[
            grid_spec(x.shape),
            pack_spec(64, 0),
            pack_spec(64, 1),
            pack_spec(64, 2),
            whole_spec(12, D),
            whole_spec(HEADS, WIN, WIN),
        ]
        + [window_spec(WIN, 128)] * len(extra)
        + space,
        out_specs=[
            window_spec(WIN, 3 * D),
            window_spec(HEADS, WIN, WIN),
            window_spec(WIN, D),
            window_spec(WIN, D),
            window_spec(WIN, D),
            window_spec(WIN, FF),
            window_spec(WIN, FF),
            pl.BlockSpec(memory_space=pl.ANY) if pushed else grid_spec(x.shape),
        ]
        + space,
        out_shape=[
            jax.ShapeDtypeStruct((windows, WIN, 3 * D), BF16),
            jax.ShapeDtypeStruct((windows, HEADS, WIN, WIN), BF16),
            jax.ShapeDtypeStruct((windows, WIN, D), F32),
            jax.ShapeDtypeStruct((windows, WIN, D), BF16),
            jax.ShapeDtypeStruct((windows, WIN, D), F32),
            jax.ShapeDtypeStruct((windows, WIN, FF), BF16),
            jax.ShapeDtypeStruct((windows, WIN, FF), BF16),
            jax.ShapeDtypeStruct(x.shape, dtype),
        ]
        + full,
        scratch_shapes=(push_scratch() if pushed else []) + (semaphores if carried else []),
        cost_estimate=cost(windows, 13),
        compiler_params=params(2 + layer if pushed else None),
    )(x, pack, pack, pack, vec, bias, *extra, *([shard] if carried else []))


def norm_back(normal, rate, gained):
    first = jnp.mean(gained, axis=-1, keepdims=True)
    second = jnp.mean(gained * normal, axis=-1, keepdims=True)
    return (gained - first - normal * second) * rate


def feed_backward(
    grad_ref, act_ref, slope_ref, mid_ref, att_ref, in_ref, up_ref, down_ref, vec_ref,
    gmid_ref, gatt_ref, result_ref, gvec_ref, pack_ref,
):
    @pl.when(pl.program_id(0) == 0)
    def _():
        pack_ref[...] = jnp.zeros_like(pack_ref)
        gvec_ref[...] = jnp.zeros_like(gvec_ref)

    count = mid_ref.shape[0]
    each = range(count)
    grads = [
        grad_ref[0, :, WW * w : WW * (w + 1)].astype(F32).reshape(WIN, D) for w in each
    ]
    gvec_ref[3:4] += sum(row_sum(grad) for grad in grads)
    lows = [grad.astype(BF16) for grad in grads]
    normals = [normalize(mid_ref[w]) for w in each]
    gnormed = [jnp.zeros((count * WIN, D), F32)]

    low_all = jnp.concatenate(grads, axis=0).astype(BF16)
    normed_all = jnp.concatenate(
        [normals[w][0] * vec_ref[5:6] + vec_ref[6:7] for w in each], axis=0
    ).astype(BF16)

    def back_part(part):
        return dot(low_all, down_ref[part * 8 : part * 8 + 8].reshape(D, D), NT)

    def finish(part, ghidden):
        first = ROWS * (1 + part)
        total = dot(normed_all, ghidden, TN)
        pack_ref[:, first : first + ROWS, :] += total.reshape(PACKS, ROWS, D)
        gnormed[0] = gnormed[0] + dot(ghidden, square(up_ref, part * ROWS), NT)

    gactive = back_part(0)
    last = None
    for part in range(4):
        following = back_part(part + 1) if part < 3 else None
        lanes = slice(part * D, (part + 1) * D)
        slopes = [slope_ref[w, :, lanes].astype(F32) for w in each]
        ghidden = gactive * jnp.concatenate(slopes, axis=0)
        gvec_ref[4 + part : 5 + part] += row_sum(ghidden)
        ghidden = ghidden.astype(BF16)
        total = sum(dot(act_ref[w, :, lanes], lows[w], TN) for w in each)
        pack_ref[part * 8 : part * 8 + 8, 80:144, :] += total.reshape(8, 64, D)
        if part > 0:
            finish(part - 1, last)
        last = ghidden
        gactive = following
    finish(3, last)
    outer = square(in_ref, 0)
    total = jnp.zeros((D, D), F32)
    gnormed = [gnormed[0][WIN * w : WIN * (w + 1)] for w in each]
    for w in each:
        normal, rate = normals[w]
        gvec_ref[1:2] += row_sum(gnormed[w] * normal)
        gvec_ref[2:3] += row_sum(gnormed[w])
        gmid = grads[w] + norm_back(normal, rate, gnormed[w] * vec_ref[5:6])
        gmid_ref[w] = gmid
        gvec_ref[0:1] += row_sum(gmid)
        gmid_low = gmid.astype(BF16)
        total = total + dot(att_ref[w], gmid_low, TN)
        gatt_ref[w] = dot(gmid_low, outer, NT).astype(BF16)
    pack_ref[:, 0:ROWS, :] += total.reshape(PACKS, ROWS, D)

    @pl.when(pl.program_id(0) == pl.num_programs(0) - 1)
    def _():
        result_ref[...] = pack_ref[...].astype(result_ref.dtype)


def run_feed_backward(layer, grad, active, slope, middle, attended, pack, vec, dtype):
    windows = middle.shape[0]
    count = grad.shape[2] // WW
    row_blocks = grad.shape[1] // WH

    def some(width):
        return pl.BlockSpec((count, WIN, width), lambda i: (i, 0, 0))

    grid_block = pl.BlockSpec(
        (1, WH, count * WW, WT, D), lambda i: (i // row_blocks, i % row_blocks, 0, 0, 0)
    )
    return pl.pallas_call(
        feed_backward,
        grid=(windows // count,),
        in_specs=[
            grid_block,
            some(FF),
            some(FF),
            some(D),
            some(D),
            pack_spec(ROWS, 3),
            pack_spec(64, 1),
            pack_spec(64, 2),
            whole_spec(12, D),
        ],
        out_specs=[
            some(D),
            some(D),
            whole_spec(PACKS, 144, D),
            pl.BlockSpec((8, D), lambda i: (0, 0)),
        ],
        out_shape=[
            jax.ShapeDtypeStruct((windows, WIN, D), F32),
            jax.ShapeDtypeStruct((windows, WIN, D), BF16),
            jax.ShapeDtypeStruct((PACKS, 192, D), dtype),
            jax.ShapeDtypeStruct((8, D), F32),
        ],
        scratch_shapes=[pltpu.VMEM((PACKS, 144, D), F32)],
        cost_estimate=cost(windows, 7),
        compiler_params=params(),
    )(grad, active, slope, middle, attended, pack, pack, pack, vec)


def attention_backward(
    pushed,
    whole_ref, x_ref, gatt_ref, att_ref, rate_ref, soft_ref, qkv_ref, gmid_ref, in_ref, vec_ref,
    out_ref, result_ref, gvec_ref, table_ref,
    pack_ref, sum_s, qt_s, dot_s, gkt_s, gvt_s, gq_s, do_s, wide_s, *push,
):
    step = pl.program_id(0)
    if pushed:
        push_begin(False)

    @pl.when(step == 0)
    def _():
        sum_s[...] = jnp.zeros_like(sum_s)
        pack_ref[...] = jnp.zeros_like(pack_ref)
        gvec_ref[...] = jnp.zeros_like(gvec_ref)

    lane = lax.broadcasted_iota(jnp.int32, (1, 128), 1)
    scaled = (gatt_ref[0].astype(F32) * rate_ref[0]).astype(BF16)
    do_s[...] = scaled
    product = scaled.astype(F32) * att_ref[0].astype(F32)
    gather_row = lax.broadcasted_iota(jnp.int32, (D, 128), 0) // HD
    gather_col = lax.broadcasted_iota(jnp.int32, (D, 128), 1)
    gather = jnp.where(
        (gather_row == gather_col % HEADS) & (gather_col < 3 * HEADS), 1.0, 0.0
    ).astype(BF16)
    high = product.astype(BF16)
    low = (product - high.astype(F32)).astype(BF16)
    inner = dot(high, gather) + dot(low, gather)
    first, second, third = split_three(inner)
    inner = jnp.where(lane < HEADS, first, jnp.where(lane < 2 * HEADS, second, third))
    qt_s[...] = jnp.transpose(qkv_ref[0, :, 0:D].astype(F32)).astype(BF16)
    dot_s[...] = jnp.transpose(scaled.astype(F32)).astype(BF16)
    minus = jnp.broadcast_to(jnp.where(lane < 3 * HEADS, -1.0, 0.0), (WIN, 128)).astype(BF16)
    zero = jnp.zeros((WIN, 128), BF16)

    def score(head):
        first = head // 4 * 128
        grad4 = jnp.where(head_lanes(head % 4), do_s[:, first : first + 128], zero)
        own = jnp.where((lane % HEADS == head) & (lane < 3 * HEADS), inner, zero)
        left = jnp.concatenate([grad4, own], axis=1)
        values4 = qkv_ref[0, :, 2 * D + first : 2 * D + first + 128]
        return dot(left, jnp.concatenate([values4, minus], axis=1), NT)

    parts = [None]

    def finish(head, soft, gtotal):
        first = head // 4 * 128
        rows = slice(head * HD, (head + 1) * HD)
        gvt_s[rows, :] = dot(dot_s[rows, :], soft)
        gkt_s[rows, :] = dot(qt_s[rows, :], gtotal)
        keys4 = qkv_ref[0, :, D + first : D + first + 128]
        part = dot(gtotal, jnp.where(head_lanes(head % 4), keys4, zero))
        parts[0] = part if head % 4 == 0 else parts[0] + part
        if head % 4 == 3:
            gq_s[:, first : first + 128] = parts[0].astype(BF16)

    slope = score(0)
    last = None
    for head in range(HEADS):
        following = score(head + 1) if head < HEADS - 1 else None
        soft = soft_ref[0, head]
        gtotal = soft.astype(F32) * slope
        sum_s[head] += gtotal
        gtotal = gtotal.astype(BF16)
        if head > 0:
            finish(head - 1, *last)
        last = (soft, gtotal)
        slope = following
    finish(HEADS - 1, *last)
    gquery = gq_s[...]
    gkeys = (jnp.transpose(gkt_s[...]) * LN2).astype(BF16)
    gvalues = jnp.transpose(gvt_s[...]).astype(BF16)
    normal, rate = normalize(x_ref[0].astype(F32).reshape(WIN, D))
    normed = (normal * vec_ref[0:1] + vec_ref[1:2]).astype(BF16)
    pack_ref[:, 0:ROWS, :] += (dot(normed, gquery, TN) * SCALE).reshape(PACKS, ROWS, D)
    pack_ref[:, ROWS : 2 * ROWS, :] += dot(normed, gkeys, TN).reshape(PACKS, ROWS, D)
    pack_ref[:, 2 * ROWS :, :] += dot(normed, gvalues, TN).reshape(PACKS, ROWS, D)
    gvec_ref[2:3] += row_sum(gquery.astype(F32)) * SCALE
    gvec_ref[3:4] += row_sum(gvalues.astype(F32))
    gnormed = (
        dot(gquery, square(in_ref, 0), NT) * SCALE
        + dot(gkeys, square(in_ref, ROWS), NT)
        + dot(gvalues, square(in_ref, 2 * ROWS), NT)
    )
    gvec_ref[0:1] += row_sum(gnormed * normal)
    gvec_ref[1:2] += row_sum(gnormed)
    grad = gmid_ref[0] + norm_back(normal, rate, gnormed * vec_ref[0:1])
    if pushed:
        push_window(False, grad, out_ref, *push)
    else:
        out_ref[0] = grad.reshape(WH, WW, WT, D).astype(out_ref.dtype)

    @pl.when(step == pl.num_programs(0) - 1)
    def _():
        result_ref[...] = pack_ref[...].astype(result_ref.dtype)
        table_ref[...] = jnp.zeros_like(table_ref)
        for col in range(WW):
            wide_s[...] = jnp.zeros_like(wide_s)
            for row in range(WH):
                place = (row * WW + col) * WT
                low_lane = (WH - 1 - row) * WW * WT
                wide_s[:, low_lane : low_lane + WIN] += sum_s[:, place : place + WT, :].reshape(
                    HEADS * WT, WIN
                )
            for shift in range(2 * WH - 1):
                low_lane = (shift * (2 * WW - 1) + WW - 1 - col) * WT
                table_ref[:, low_lane : low_lane + WW * WT] += wide_s[
                    :, shift * WW * WT : (shift + 1) * WW * WT
                ]


def run_attention_backward(
    layer, whole, x, gattended, attended, rates, soft, qkv, gmiddle, pack, vec, dtype, pack_dtype, pushed
):
    windows = gmiddle.shape[0]
    return pl.pallas_call(
        functools.partial(attention_backward, pushed),
        grid=(windows,),
        in_specs=[
            pl.BlockSpec(memory_space=pl.ANY),
            grid_spec(x.shape),
            window_spec(WIN, D),
            window_spec(WIN, D),
            window_spec(WIN, D),
            window_spec(HEADS, WIN, WIN),
            window_spec(WIN, 3 * D),
            window_spec(WIN, D),
            pack_spec(48, 0),
            whole_spec(12, D),
        ],
        out_specs=[
            pl.BlockSpec(memory_space=pl.ANY) if pushed else grid_spec(x.shape),
            pack_spec(48, 3),
            pl.BlockSpec((4, D), lambda i: (0, 0)),
            pl.BlockSpec((HEADS * WT, CELLS * WT), lambda i: (0, 0)),
        ],
        out_shape=[
            jax.ShapeDtypeStruct(x.shape, dtype),
            jax.ShapeDtypeStruct((PACKS, 192, D), pack_dtype),
            jax.ShapeDtypeStruct((4, D), F32),
            jax.ShapeDtypeStruct((HEADS * WT, CELLS * WT), F32),
        ],
        scratch_shapes=[
            pltpu.VMEM((PACKS, 48, D), F32),
            pltpu.VMEM((HEADS, WIN, WIN), F32),
            pltpu.VMEM((D, WIN), BF16),
            pltpu.VMEM((D, WIN), BF16),
            pltpu.VMEM((D, WIN), F32),
            pltpu.VMEM((D, WIN), F32),
            pltpu.VMEM((WIN, D), BF16),
            pltpu.VMEM((WIN, D), BF16),
            pltpu.VMEM((HEADS * WT, (2 * WH - 1) * WW * WT), F32),
        ]
        + (push_scratch() if pushed else []),
        cost_estimate=cost(windows, 12),
        compiler_params=params(4 if pushed else None),
        input_output_aliases={0: 1},
    )(whole, x, gattended, attended, rates, soft, qkv, gmiddle, pack, vec)


def expand_bias(cells_ref, out_ref, wide_s):
    for col in range(WW):
        for shift in range(2 * WH - 1):
            low_lane = (shift * (2 * WW - 1) + WW - 1 - col) * WT
            wide_s[:, shift * WW * WT : (shift + 1) * WW * WT] = cells_ref[
                :, low_lane : low_lane + WW * WT
            ]
        for row in range(WH):
            place = (row * WW + col) * WT
            low_lane = (WH - 1 - row) * WW * WT
            out_ref[:, place : place + WT, :] = wide_s[:, low_lane : low_lane + WIN].reshape(
                HEADS, WT, WIN
            )


def run_expand_bias(cells):
    return pl.pallas_call(
        expand_bias,
        out_shape=jax.ShapeDtypeStruct((HEADS, WIN, WIN), F32),
        scratch_shapes=[pltpu.VMEM((HEADS * WT, (2 * WH - 1) * WW * WT), F32)],
        compiler_params=pltpu.CompilerParams(vmem_limit_bytes=61 * 1024 * 1024),
    )(cells)


AUX_ROWS = 8
SHARES = ((1, 0, AUX_ROWS, 0), (0, 0, 48, 0), (0, 48, 48, 1), (0, 96, 48, 0), (0, 144, 48, 1))


def fold_gradients(*refs):
    operands = refs[:2]
    pack_out, aux_out = refs[2:4]
    buffers = refs[4:19]
    send_sem, recv_sem, wide_send, wide_recv = refs[19:]
    batch = lax.axis_index("batch")
    y = lax.axis_index("seq")
    z, x, core = batch // 4, (batch // 2) % 2, batch % 2
    count = len(SHARES)

    def device(z_to, x_to, core_to, y_to):
        return ((z_to * 2 + x_to) * 2 + core_to, y_to)

    barrier = pltpu.get_barrier_semaphore()

    def greet(k, carry):
        other = lax.rem(batch * 2 + y + k, 32)
        pl.semaphore_signal(
            barrier, inc=1, device_id=(other // 2, other % 2), device_id_type=pl.DeviceIdType.MESH
        )
        return carry

    lax.fori_loop(1, 32, greet, 0)
    pl.semaphore_wait(barrier, 31)

    def send(number, source, target, to):
        copy = pltpu.make_async_remote_copy(
            src_ref=source,
            dst_ref=target,
            send_sem=send_sem.at[number],
            recv_sem=recv_sem.at[number],
            device_id=to,
            device_id_type=pl.DeviceIdType.MESH,
        )
        copy.start()
        return copy

    copies = []
    for k, (which, first, size, order) in enumerate(SHARES):
        source = operands[which].at[:, :, 1 - core, :, pl.ds(first, size), :]
        copies.append(send(k, source, buffers[3 * k], device(z, x, 1 - core, y)))
    for k, (which, first, size, order) in enumerate(SHARES):
        copies[k].wait()
        held = buffers[3 * k]

        def add_core(i, carry, which=which, first=first, size=size, held=held):
            a, b = i // 2, i % 2
            mine = operands[which][a, b, core, :, first : first + size, :].astype(F32)
            held[a, b] = (held[a, b].astype(F32) + mine).astype(held.dtype)
            return carry

        lax.fori_loop(0, 8, add_core, 0)
        if order == 0:
            copies.append(send(count + k, held.at[:, 1 - x], buffers[3 * k + 1], device(z, 1 - x, core, y)))
        else:
            copies.append(send(count + k, held.at[:, :, 1 - y], buffers[3 * k + 1], device(z, x, core, 1 - y)))
    for k, (which, first, size, order) in enumerate(SHARES):
        copies[count + k].wait()
        before, held = buffers[3 * k], buffers[3 * k + 1]

        def add_next(i, carry, order=order, before=before, held=held):
            a, b = i // 2, i % 2
            mine = before[a, x, b] if order == 0 else before[a, b, y]
            held[a, b] = (held[a, b].astype(F32) + mine.astype(F32)).astype(held.dtype)
            return carry

        lax.fori_loop(0, 8, add_next, 0)
        if order == 0:
            copies.append(send(2 * count + k, held.at[:, 1 - y], buffers[3 * k + 2].at[pl.ds(0, 4)], device(z, x, core, 1 - y)))
        else:
            copies.append(send(2 * count + k, held.at[:, 1 - x], buffers[3 * k + 2].at[pl.ds(0, 4)], device(z, 1 - x, core, y)))
    far = []
    for k, (which, first, size, order) in enumerate(SHARES):
        copies[2 * count + k].wait()
        before, held = buffers[3 * k + 1], buffers[3 * k + 2]

        def add_last(a, carry, order=order, before=before, held=held):
            mine = before[a, y] if order == 0 else before[a, x]
            held[a] = (held[a].astype(F32) + mine.astype(F32)).astype(held.dtype)
            return carry

        lax.fori_loop(0, 4, add_last, 0)
        for step in range(1, 4):
            other = lax.rem(z + step, 4)
            far.append(
                send(
                    3 * count + 3 * k + step - 1,
                    held.at[other],
                    held.at[3 + step],
                    device(other, x, core, y),
                )
            )
    def spread(k, carry):
        other = lax.rem(batch * 2 + y + k, 32)
        pltpu.make_async_remote_copy(
            src_ref=aux_out.at[batch * 2 + y],
            dst_ref=aux_out.at[batch * 2 + y],
            send_sem=wide_send,
            recv_sem=wide_recv,
            device_id=(other // 2, other % 2),
            device_id_type=pl.DeviceIdType.MESH,
        ).start()
        return carry

    for k, (which, first, size, order) in enumerate(SHARES):
        for step in range(1, 4):
            far[3 * k + step - 1].wait()
        held = buffers[3 * k + 2]
        total = held[z].astype(F32) + held[4].astype(F32)
        total = total + held[5].astype(F32) + held[6].astype(F32)
        if which == 0:
            pack_out[first : first + size, :] = total
        else:
            aux_out[batch * 2 + y] = total

    lax.fori_loop(1, 32, spread, 0)
    others = aux_out.at[pl.ds(0, 31)]
    pltpu.make_async_copy(others, others, wide_send).wait()
    pltpu.make_async_copy(others, others, wide_recv).wait()


def run_fold_gradients(big, aux):
    operands = [value.reshape((4, 2, 2, 2) + value.shape[1:]) for value in (big, aux)]
    scratch = []
    for which, first, size, order in SHARES:
        dtype = operands[which].dtype
        scratch.append(pltpu.VMEM((4, 2, 2, size, D), dtype))
        scratch.append(pltpu.VMEM((4, 2, size, D), dtype))
        scratch.append(pltpu.VMEM((7, size, D), dtype))
    semaphores = 6 * len(SHARES)
    return pl.pallas_call(
        fold_gradients,
        in_specs=[pl.BlockSpec(memory_space=pltpu.VMEM)] * 2,
        out_specs=[pl.BlockSpec(memory_space=pltpu.VMEM)] * 2,
        out_shape=[
            jax.ShapeDtypeStruct((192, D), F32),
            jax.ShapeDtypeStruct((32, AUX_ROWS, D), F32),
        ],
        scratch_shapes=scratch
        + [
            pltpu.SemaphoreType.DMA((semaphores,)),
            pltpu.SemaphoreType.DMA((semaphores,)),
            pltpu.SemaphoreType.DMA,
            pltpu.SemaphoreType.DMA,
        ],
        cost_estimate=cost(1, 1),
        compiler_params=pltpu.CompilerParams(
            vmem_limit_bytes=61 * 1024 * 1024, collective_id=1, has_side_effects=True
        ),
    )(*operands)


def offset_places():
    frame, row, col = np.meshgrid(
        np.arange(1 - WT, WT), np.arange(1 - WH, WH), np.arange(1 - WW, WW), indexing="ij"
    )

    def place(f, r, c):
        return (np.maximum(f, 0) * WH + np.maximum(r, 0)) * WW + np.maximum(c, 0)

    return (place(frame, row, col) * WIN + place(-frame, -row, -col)).reshape(-1)[::-1].copy()


def interleave():
    cell = np.arange(CELLS * WT)
    source = jnp.asarray((cell % WT) * CELLS + cell // WT, jnp.int32)
    order = jnp.arange(CELLS * WT, dtype=jnp.int32)
    return (order[:, None] == source[None, :]).astype(BF16)


def join_three(values, axis):
    first, second, third = jnp.split(values, 3, axis=axis)
    return first + second + third


def bias_cells(tables, chosen, order):
    flat = jnp.concatenate([tables[layer] for layer in range(LAYERS)], axis=1) * LOG2E
    pieces = jnp.concatenate(split_three(flat), axis=1)
    taken = dot(pieces, chosen, (((0,), (1,)), ((), ()))).astype(BF16)
    placed = jnp.stack(
        [taken[:, (WT - 1 - t) * CELLS : (2 * WT - 1 - t) * CELLS] for t in range(WT)], axis=1
    )
    cells = dot(placed.reshape(-1, WT * CELLS), order)
    return join_three(cells, 0).reshape(LAYERS, HEADS * WT, CELLS * WT)


def cells_to_rows(cells, order):
    pieces = jnp.concatenate(split_three(cells.reshape(-1, CELLS * WT)), axis=0)
    placed = join_three(dot(pieces, order, NT), 0).reshape(LAYERS * HEADS, WT, CELLS * WT)
    parts = [
        jnp.pad(placed[:, t], ((0, 0), ((WT - 1 - t) * CELLS, t * CELLS))) for t in range(WT)
    ]
    return functools.reduce(jnp.add, parts)


def rows_to_table(rows, chosen):
    pieces = jnp.concatenate(split_three(rows), axis=0)
    total = join_three(dot(chosen, pieces, (((0,), (1,)), ((), ()))), 1)
    return jnp.stack([total[:, i * HEADS : (i + 1) * HEADS] for i in range(LAYERS)])


def spatial_blocks(field):
    clip_count, frames_here, width = (field.shape[0], field.shape[1], field.shape[-1])
    shaped = field.reshape(clip_count, frames_here, HGT // WH, WH, WID // WW, WW, width)
    shaped = shaped.transpose(0, 2, 4, 1, 3, 5, 6)
    return shaped.reshape(clip_count * (HGT // WH) * (WID // WW), frames_here, WH * WW, width)


def roll_space(field, amount, first):
    return jnp.roll(field, (amount, amount), axis=(first, first + 1))


def swap_halves(part):
    return lax.ppermute(part, "seq", [(0, 1), (1, 0)])


class Placement:
    def __init__(self, clip_count, frames_here):
        self.clips = clip_count
        self.frames = frames_here
        self.parts = lax.axis_size("seq")
        self.near = self.parts == 2 and frames_here == WT

    def grid_shape(self):
        if self.near:
            return (self.clips, HGT, WID, WT, D)
        columns = self.clips * 4 // self.parts
        return (columns * 2, WH, WW, WT, D)

    def enter(self, field, shifted):
        if self.near:
            if shifted:
                arrived = swap_halves(field[:, :SHIFT_T])
                field = jnp.concatenate([field[:, SHIFT_T:], arrived], axis=1)
                field = roll_space(field, -SHIFT_S, 2)
            return field.transpose(0, 2, 3, 1, 4)
        if shifted:
            field = roll_space(field, -SHIFT_S, 2)
        columns = lax.all_to_all(
            spatial_blocks(field), "seq", split_axis=0, concat_axis=1, tiled=True
        )
        if shifted:
            columns = jnp.roll(columns, -SHIFT_T, axis=1)
        windows = columns.reshape(-1, WT, WH, WW, D)
        return windows.transpose(0, 2, 3, 1, 4)

    def leave(self, grid, shifted):
        if self.near:
            field = grid.transpose(0, 3, 1, 2, 4)
            if shifted:
                field = roll_space(field, SHIFT_S, 2)
                arrived = swap_halves(field[:, SHIFT_T:])
                field = jnp.concatenate([arrived, field[:, :SHIFT_T]], axis=1)
            return field
        columns = grid.transpose(0, 3, 1, 2, 4).reshape(-1, FRAMES, WH * WW, D)
        if shifted:
            columns = jnp.roll(columns, SHIFT_T, axis=1)
        columns = lax.all_to_all(columns, "seq", split_axis=1, concat_axis=0, tiled=True)
        shaped = columns.reshape(self.clips, HGT // WH, WID // WW, self.frames, WH, WW, D)
        shaped = shaped.transpose(0, 3, 1, 4, 2, 5, 6)
        field = shaped.reshape(self.clips, self.frames, HGT, WID, D)
        return roll_space(field, SHIFT_S, 2) if shifted else field

    def forth(self, grid):
        return self.enter(self.leave(grid, False), True)

    def back(self, grid):
        return self.enter(self.leave(grid, True), False)

    def mask_lanes(self):
        if self.near:
            index = jnp.arange(self.clips * 4, dtype=jnp.int32)
            late = jnp.full(index.shape, lax.axis_index("seq"), jnp.int32)
            block = index % 4
        else:
            columns = self.clips * 4 // self.parts
            index = jnp.arange(columns * 2, dtype=jnp.int32)
            late = index % 2
            block = (lax.axis_index("seq") * columns + index // 2) % 4
        place = np.arange(WIN)
        frame_late = jnp.asarray(place % WT >= WT - SHIFT_T).astype(jnp.int32)
        row_late = jnp.asarray(place // (WT * WW) >= WH - SHIFT_S).astype(jnp.int32)
        col_late = jnp.asarray(place // WT % WW >= WW - SHIFT_S).astype(jnp.int32)
        region = (
            late[:, None] * frame_late * 4
            + (block // 2)[:, None] * row_late * 2
            + (block % 2)[:, None] * col_late
        )
        lane = np.arange(128)
        same = (region[:, :, None] == lane % 8) & (lane < 24)
        pieces = []
        rest = np.float32(MASKED * LOG2E)
        for _ in range(3):
            piece = np.float32(np.asarray(rest).astype(BF16))
            pieces.append(piece)
            rest = np.float32(rest - piece)
        piece_of = np.zeros((128,), np.float32)
        for number, piece in enumerate(pieces):
            piece_of[8 * number : 8 * number + 8] = -piece
            piece_of[24 + number] = piece
        always = (lane >= 24) & (lane < 27)
        on_keys = jnp.where(same | always, 1.0, 0.0)
        return (on_keys * piece_of).astype(BF16), on_keys.astype(BF16)


def pack_layer(inner, outer, up, down):
    parts = [inner[:, i * D : (i + 1) * D] for i in range(3)] + [outer]
    parts = parts + [up[:, i * D : (i + 1) * D] for i in range(4)] + [down]
    return jnp.concatenate(parts, axis=0)


def per_device(
    clips_in,
    cotangent,
    offset_index,
    first_gain,
    first_shift,
    inner_weight,
    inner_bias,
    outer_weight,
    outer_bias,
    second_gain,
    second_shift,
    up_weight,
    up_bias,
    down_weight,
    down_bias,
    bias_table,
):
    place = Placement(clips_in.shape[0], clips_in.shape[1])
    rows = inner_weight.shape[1]
    devices = D // rows
    vectors = [
        first_gain, first_shift, inner_bias, outer_bias, second_gain, second_shift,
        down_bias, up_bias,
    ]
    vec_pack = jnp.concatenate(vectors, axis=1)
    width = vec_pack.shape[1]
    vec_rows = jnp.pad(vec_pack, ((0, 14), (0, D - width)))
    local = [
        pack_layer(inner_weight[layer], outer_weight[layer], up_weight[layer], down_weight[layer])
        for layer in range(LAYERS)
    ]
    folded = lax.axis_size("batch") == 16 and lax.axis_size("seq") == 2
    shape = place.grid_shape()
    carried = folded and place.near and shape[0] == 2
    first_part = [local[0], vec_rows] if carried else local + [vec_rows]
    full = lax.all_gather(jnp.concatenate(first_part, axis=0), AXES, axis=0)
    vecs = []
    for layer in range(LAYERS):
        held = full[:, full.shape[1] - 16 + layer, :width].astype(F32)
        pieces = []
        start = 0
        for vector in vectors:
            size = vector.shape[1]
            pieces.append(held[:, start : start + size].reshape(-1, D))
            start += size
        vecs.append(jnp.concatenate(pieces, axis=0))
    packs = [full, None]
    if not carried:
        for layer in range(LAYERS):
            parts = []
            first = 12 * rows * layer
            for i in range(8):
                part = full[:, first + i * rows : first + (i + 1) * rows]
                parts.append(part.reshape(PACKS, ROWS, D))
            part = full[:, first + 8 * rows : first + 12 * rows]
            parts.append(part.reshape(PACKS, 4 * ROWS, D))
            packs[layer] = jnp.concatenate(parts, axis=1)
    taken_rows = jnp.take(offset_index.reshape(-1), offset_places())
    order = jnp.arange(BIAS_ROWS, dtype=jnp.int32)
    chosen = (taken_rows[:, None] == order[None, :]).astype(BF16)
    interleaved = interleave()
    cells_in = bias_cells(bias_table, chosen, interleaved)
    bias = [run_expand_bias(cells_in[layer]) for layer in range(LAYERS)]
    aug = place.mask_lanes()

    x_zero = place.enter(clips_in, False)
    upstream = place.enter(cotangent, True)
    saved = []
    x = x_zero
    for layer in range(LAYERS):
        outs = run_block_forward(
            layer, x, packs[layer], vecs[layer], bias[layer], aug if layer == 1 else None,
            F32 if layer == 0 or place.near else BF16, place.near,
            local[1] if carried and layer == 0 else None,
        )
        qkv, soft, rates, attended, middle, active, slope, result = outs[:8]
        if carried and layer == 0:
            packs[1] = outs[8].reshape(PACKS, 192, D)
        saved.append((x, qkv, soft, rates, attended, middle, active, slope))
        x = place.forth(result) if layer == 0 and not place.near else result
    clips_out = place.leave(x, not place.near).astype(BF16)

    scattered = [None] * LAYERS
    vec_parts = [None] * LAYERS
    cell_parts = [None] * LAYERS

    def scatter(value, blocks):
        if rows != ROWS:
            per = ROWS // rows
            parts = []
            start = 0
            for size in blocks:
                part = value[:, start : start + size].reshape(PACKS * per, size // per, D)
                parts.append(part)
                start += size
            value = jnp.concatenate(parts, axis=1)
        return lax.psum_scatter(value, AXES, scatter_dimension=0, tiled=False)

    for layer in reversed(range(LAYERS)):
        pack, vec = packs[layer], vecs[layer]
        x, qkv, soft, rates, attended, middle, active, slope = saved[layer]
        gmiddle, gattended, big, gvec_two = run_feed_backward(
            layer, upstream, active, slope, middle, attended, pack, vec, BF16 if folded else F32
        )
        upstream, big, gvec_one, cells = run_attention_backward(
            layer, big, x, gattended, attended, rates, soft, qkv, gmiddle, pack, vec,
            F32 if layer == 1 else BF16, BF16 if folded else F32,
            place.near and layer == 1,
        )
        if layer == 1 or not folded:
            scattered[layer] = scatter(big, [ROWS] * 5 + [4 * ROWS] + [ROWS] * 3)
        vec_parts[layer] = jnp.concatenate([gvec_one, gvec_two], axis=0)
        cell_parts[layer] = cells
        if layer == 1 and not place.near:
            upstream = place.back(upstream)
    clips_grad = place.leave(upstream, False)

    table_rows = cells_to_rows(jnp.stack(cell_parts), interleaved)
    vec_stack = jnp.stack(vec_parts)
    if folded:
        aux = jnp.concatenate([table_rows.reshape(-1), vec_stack.reshape(-1)])
        used = aux.shape[0]
        aux = jnp.pad(aux, (0, PACKS * AUX_ROWS * D - used)).reshape(PACKS, AUX_ROWS, D)
        big, scattered[1] = lax.optimization_barrier((big, scattered[1]))
        scattered[0], aux = run_fold_gradients(big, aux)
        aux = aux.reshape(-1)[:used]
        table_total = aux[: table_rows.size].reshape(table_rows.shape)
        vec_total = aux[table_rows.size :].reshape(vec_stack.shape)
    else:
        vec_total, table_total = lax.psum((vec_stack, table_rows), AXES)
    table_total = rows_to_table(table_total, chosen)

    scattered = [value.astype(F32) for value in scattered]
    device = lax.axis_index(AXES)

    def own(first, count):
        whole = vec_total[:, first : first + count].reshape(LAYERS, count * D)
        size = count * D // devices
        return lax.dynamic_slice_in_dim(whole, device * size, size, axis=1)

    def both(first, count):
        parts = []
        for layer in range(LAYERS):
            value = scattered[layer]
            columns = [
                value[first + i * rows : first + (i + 1) * rows] for i in range(count)
            ]
            parts.append(jnp.concatenate(columns, axis=1))
        return jnp.stack(parts)

    down = jnp.stack([scattered[layer][5 * rows : 9 * rows] for layer in range(LAYERS)])
    return (
        clips_out,
        clips_grad,
        own(0, 1),
        own(1, 1),
        both(9 * rows, 3),
        own(2, 2),
        both(0, 1),
        own(4, 1),
        own(5, 1),
        own(6, 1),
        both(rows, 4),
        own(8, 4),
        down,
        own(7, 1),
        table_total,
    )


def solution(mesh):
    clips = P("batch", "seq", None, None, None)
    vector = P(None, AXES)
    matrix = P(None, AXES, None)
    return jax.shard_map(
        per_device,
        mesh=mesh,
        in_specs=(
            clips, clips, P(), vector, vector, matrix, vector, matrix, vector, vector, vector,
            matrix, vector, matrix, vector, P(),
        ),
        out_specs=(
            clips, clips, vector, vector, matrix, vector, matrix, vector, vector, vector,
            matrix, vector, matrix, vector, P(),
        ),
        check_vma=False,
    )
```
